32 devices in a mesh: blk: 2 (over x), wide: 16 (over z, y, core).
Axes of the slice: x: 2, y: 2, z: 4, core: 2. Of those that a mesh axis runs over, the one named last changes fastest.
Arguments:
- layer_input: bfloat16 [16, 256, 2048], P('wide', 'blk'), may hold values from -6 to 6
- lengths: int32 [16], P('wide'), may hold values from 129 to 256, as said below
- w_query: bfloat16 [2048, 2048], P(('blk', 'wide')), may hold values from -0.125 to 0.125
- w_key: bfloat16 [2048, 2048], P(('blk', 'wide')), may hold values from -0.125 to 0.125
- w_value: bfloat16 [2048, 2048], P(('blk', 'wide')), may hold values from -0.125 to 0.125
- w_output: bfloat16 [2048, 2048], P(('blk', 'wide')), may hold values from -0.125 to 0.125
- query_gain: bfloat16 [2048], P(('blk', 'wide')), may hold values from 0.099609375 to 1.8984375
- key_gain: bfloat16 [2048], P(('blk', 'wide')), may hold values from 0.099609375 to 1.8984375
- attn_gain: bfloat16 [2048], P(('blk', 'wide')), may hold values from 0.099609375 to 1.8984375
- mlp_gain: bfloat16 [2048], P(('blk', 'wide')), may hold values from 0.099609375 to 1.8984375
- w_gate: bfloat16 [2048, 8192], P('blk', 'wide'), may hold values from -0.125 to 0.125
- w_up: bfloat16 [2048, 8192], P('blk', 'wide'), may hold values from -0.125 to 0.125
- w_down: bfloat16 [2048, 8192], P('blk', 'wide'), may hold values from -0.0625 to 0.0625
- grad_output: bfloat16 [16, 256, 2048], P('wide', 'blk'), may hold values from -6 to 6
Outputs:
- output: bfloat16 [16, 256, 2048], P('wide', 'blk')
- input_grad: bfloat16 [16, 256, 2048], P('wide', 'blk')
- grad_w_query: float32 [2048, 2048], P(('blk', 'wide'))
- grad_w_key: float32 [2048, 2048], P(('blk', 'wide'))
- grad_w_value: float32 [2048, 2048], P(('blk', 'wide'))
- grad_w_output: float32 [2048, 2048], P(('blk', 'wide'))
- grad_query_gain: float32 [2048], P(('blk', 'wide'))
- grad_key_gain: float32 [2048], P(('blk', 'wide'))
- grad_attn_gain: float32 [2048], P(('blk', 'wide'))
- grad_mlp_gain: float32 [2048], P(('blk', 'wide'))
- grad_w_gate: float32 [2048, 8192], P('blk', 'wide')
- grad_w_up: float32 [2048, 8192], P('blk', 'wide')
- grad_w_down: float32 [2048, 8192], P('blk', 'wide')
The draws below stay inside these ranges and needn't reach their ends.
Inputs may be any that keep to these rules, and one draw needn't show every extreme that they name: `lengths`: every sequence has at least 129 valid tokens, and one has exactly 256.
All inputs are finite; a program needn't handle non-finite values.
Results may differ from the reference program's by a relative error of at most 0.017.
Values may be sent and summed in bfloat16 or wider, within the bound.
No kernel may reach another device: no remote copies, remote signals or barrier semaphores. Data moves between devices by JAX's collectives and lax.ppermute only.
A program may use at most 384 MiB of HBM per device.

```python
import math
import jax
import jax.numpy as jnp
from jax import lax

HEAD_DIM = 128
D = 2048
FF = 8192
TOK_DEV = 128
SEQ = 256
NSEQ = 16


def draw_lengths(key, part):
    key = jax.random.fold_in(key, 11)
    first_key, second_key = jax.random.split(key)
    drawn = jax.random.randint(first_key, (NSEQ,), SEQ - TOK_DEV + 1, SEQ + 1)
    chosen = jax.random.randint(second_key, (), 0, NSEQ)
    return jnp.where(jnp.arange(NSEQ) == chosen, SEQ, drawn).astype(jnp.int32)


def level_of(key, shape, cuts, smallest, high):
    level = 1.0
    for axis_at, shards_of in cuts:
        steps = jax.random.uniform(jax.random.fold_in(jax.random.fold_in(key, 6), axis_at), (shards_of,), jnp.float32, smallest / len(cuts), high / len(cuts))
        level = level * jnp.repeat(jnp.exp(steps), shape[axis_at] // shards_of).reshape((-1,) + (1,) * (len(shape) - 1 - axis_at))
    return level


def centred(rng, extent, spread, limit, cuts=(), kind=jnp.bfloat16):
    values = jax.random.normal(rng, extent, jnp.float32) * spread
    if len(cuts) > 0:
        values = level_of(rng, extent, cuts, -0.22, 0.18) * values
    return jnp.clip(values, min=-limit, max=limit).astype(kind)


def setup_inputs(seed: int = 0) -> dict:
    arg_keys = jax.random.split(jax.random.key(seed), 15)
    layer_input = centred(arg_keys[0], (NSEQ, SEQ, D), 1.0, 6.0, ((0, 16), (1, 2)))
    lengths = draw_lengths(jax.random.fold_in(arg_keys[14], 71), 0)
    w_query = centred(arg_keys[2], (D, D), D ** -0.5, 0.125, ((0, 32),))
    w_key = centred(arg_keys[3], (D, D), D ** -0.5, 0.125, ((0, 32),))
    w_value = centred(arg_keys[4], (D, D), D ** -0.5, 0.125, ((0, 32),))
    w_output = centred(arg_keys[5], (D, D), D ** -0.5, 0.125, ((0, 32),))
    query_gain = jnp.clip(1.0 + 0.18 * jax.random.normal(arg_keys[6], (D,), jnp.float32), 0.099609375, 1.8984375).astype(jnp.bfloat16)
    key_gain = jnp.clip(1.0 + 0.18 * jax.random.normal(arg_keys[7], (D,), jnp.float32), 0.099609375, 1.8984375).astype(jnp.bfloat16)
    attn_gain = jnp.clip(1.0 + 0.18 * jax.random.normal(arg_keys[8], (D,), jnp.float32), 0.099609375, 1.8984375).astype(jnp.bfloat16)
    mlp_gain = jnp.clip(1.0 + 0.18 * jax.random.normal(arg_keys[9], (D,), jnp.float32), 0.099609375, 1.8984375).astype(jnp.bfloat16)
    w_gate = centred(arg_keys[10], (D, FF), D ** -0.5, 0.125, ((0, 2), (1, 16)))
    w_up = centred(arg_keys[11], (D, FF), D ** -0.5, 0.125, ((0, 2), (1, 16)))
    w_down = centred(arg_keys[12], (D, FF), FF ** -0.5, 0.0625, ((0, 2), (1, 16)))
    grad_output = centred(arg_keys[13], (NSEQ, SEQ, D), 1.0, 6.0, ((0, 16), (1, 2)))
    return dict(layer_input=layer_input, lengths=lengths, w_query=w_query, w_key=w_key, w_value=w_value, w_output=w_output, query_gain=query_gain, key_gain=key_gain, attn_gain=attn_gain, mlp_gain=mlp_gain, w_gate=w_gate, w_up=w_up, w_down=w_down, grad_output=grad_output)


EPSILON = 1e-06
NEGATIVE = -1e+30

@jax.custom_vjp
def low(v):
    return lax.optimization_barrier(v.astype(jnp.bfloat16)).astype(jnp.float32)

@jax.custom_vjp
def low_back(v):
    return v

def low_keep(v):
    return (low(v), None)

def low_pass(kept, grad):
    return (grad,)

def back_keep(v):
    return (v, None)

def back_low(kept, grad):
    return (low(grad),)
low.defvjp(low_keep, low_pass)
low_back.defvjp(back_keep, back_low)

def highest_dot(left, right):
    return jnp.dot(left, right, precision=lax.Precision.HIGHEST)

def rms_scale(values, gain):
    return values * lax.rsqrt(lax.optimization_barrier(jnp.mean(values * values, axis=-1, keepdims=True)) + EPSILON) * gain

def rotate(values, positions):
    count = values.shape[0]
    half = HEAD_DIM // 2
    frequency = jnp.exp(jnp.arange(half, dtype=jnp.float32) * (-2.0 * math.log(500000.0) / HEAD_DIM))
    angles = positions.astype(jnp.float32)[:, None] * frequency[None, :]
    cosine = jnp.cos(angles)[:, None, :]
    sine = jnp.sin(angles)[:, None, :]
    heads_view = values.reshape(count, -1, HEAD_DIM)
    first = heads_view[..., :half]
    second = heads_view[..., half:]
    turned = jnp.concatenate([first * cosine - second * sine, second * cosine + first * sine], axis=-1)
    return turned.reshape(count, -1)

def layer(sequence, length, weights):
    w_query, w_key, w_value, w_output, query_gain, key_gain, attn_gain, mlp_gain, w_gate, w_up, w_down = weights
    span = sequence.shape[0]
    positions = jnp.arange(span, dtype=jnp.int32)
    query = low_back(highest_dot(sequence, w_query))
    key_proj = low_back(highest_dot(sequence, w_key))
    value = low_back(low(highest_dot(sequence, w_value)))
    query_rot = low_back(low(rotate(rms_scale(query, query_gain), positions)))
    key_rot = low_back(low(rotate(rms_scale(key_proj, key_gain), positions)))
    query_heads = query_rot.reshape(span, -1, HEAD_DIM)
    key_heads = key_rot.reshape(span, -1, HEAD_DIM)
    value_heads = value.reshape(span, -1, HEAD_DIM)
    logits = jnp.einsum('qhd,khd->hqk', query_heads, key_heads, precision=lax.Precision.HIGHEST) * HEAD_DIM ** (-0.5)
    valid = (positions[None, :] <= positions[:, None]) & (positions[None, :] < length)
    logits = low_back(jnp.where(valid[None], logits, NEGATIVE))
    peak = lax.optimization_barrier(jnp.max(logits, axis=-1, keepdims=True))
    powers = jnp.exp(logits - peak)
    chances = powers / lax.optimization_barrier(jnp.sum(powers, axis=-1, keepdims=True))
    mixed = jnp.einsum('hqk,khd->qhd', low(chances), value_heads, precision=lax.Precision.HIGHEST)
    attended = low_back(low(mixed.reshape(span, -1)))
    branch = low_back(highest_dot(attended, w_output))
    hidden_state = sequence + rms_scale(branch, attn_gain)
    mlp_in = low(hidden_state)
    gate = low_back(highest_dot(mlp_in, w_gate))
    up_proj = low_back(highest_dot(mlp_in, w_up))
    product = low(jax.nn.silu(gate) * up_proj)
    mlp_out = low_back(highest_dot(product, w_down.T))
    return hidden_state + rms_scale(mlp_out, mlp_gain)

def reference(layer_input, lengths, w_query, w_key, w_value, w_output, query_gain, key_gain, attn_gain, mlp_gain, w_gate, w_up, w_down, grad_output):
    params = tuple((weight.astype(jnp.float32) for weight in (w_query, w_key, w_value, w_output, query_gain, key_gain, attn_gain, mlp_gain, w_gate, w_up, w_down)))

    def forward(inputs, *weights):

        def single(pair):
            return layer(pair[0], pair[1], weights)
        return lax.map(jax.checkpoint(single), (inputs, lengths))
    output, backward = jax.vjp(forward, layer_input.astype(jnp.float32), *params)
    gradients = backward(grad_output.astype(jnp.float32))
    return (output.astype(jnp.bfloat16), gradients[0].astype(jnp.bfloat16), gradients[1], gradients[2], gradients[3], gradients[4], gradients[5], gradients[6], gradients[7], gradients[8], gradients[9], gradients[10], gradients[11])
```

```python
import math

import jax
import jax.numpy as jnp
from jax import lax
from jax.sharding import PartitionSpec as P

HEAD_DIM = 128
EPSILON = 1e-06
NEGATIVE = -1e30
BF16 = jnp.bfloat16
F32 = jnp.float32
AXES = ("blk", "wide")
NX, NY, NZ = 2, 2, 4


def rms_scale(values, gain):
    return values * lax.rsqrt(jnp.mean(values * values, axis=-1, keepdims=True) + EPSILON) * gain


def dot(left, right, left_dim, right_dim):
    return lax.dot_general(
        left, right, (((left_dim,), (right_dim,)), ((), ())), preferred_element_type=F32
    )


def flipped(values, axis, when):
    return jnp.where(when == 1, jnp.flip(values, axis), values)


def xored(values, axis, index):
    count = values.shape[axis]
    bits = count.bit_length() - 1
    shape = values.shape
    values = values.reshape(shape[:axis] + (2,) * bits + shape[axis + 1 :])
    for bit in range(bits):
        values = flipped(values, axis + bits - 1 - bit, (index >> bit) & 1)
    return values.reshape(shape)


def rolled(values, axis, start):
    size = values.shape[axis]
    return lax.dynamic_slice_in_dim(jnp.concatenate([values, values], axis), start, size, axis)


def make_body(wide):
    nc = wide // (NY * NZ)

    def send(value, x=0, y=0, z=0, c=0):
        pairs = []
        for sx in range(NX):
            for sz in range(NZ):
                for sy in range(NY):
                    for sc in range(nc):
                        source = sx * wide + (sz * NY + sy) * nc + sc
                        target = (sx ^ x) * wide
                        target += (((sz + z) % NZ) * NY + (sy ^ y)) * nc + (sc ^ c)
                        pairs.append((source, target))
        return lax.ppermute(value, AXES, pairs)

    def square_gather(first, second):
        first_x = send(first, x=1)
        second_y = send(second, y=1)
        first_y = send(first, y=1)
        second_x = send(second, x=1)
        first_xy = send(first_x, y=1)
        second_xy = send(second_y, x=1)
        return (
            ((first, first_y), (first_x, first_xy)),
            ((second, second_y), (second_x, second_xy)),
        )

    def square_scatter(first, second):
        def low(value):
            return value.astype(BF16)

        first_a = send(low(first[1][1]), x=1)
        second_a = send(low(second[1][1]), y=1)
        first_b = send(low(first[1][0]), x=1)
        second_b = send(low(second[0][1]), y=1)
        first_c = send(low(first[0][1].astype(F32) + first_a.astype(F32)), y=1)
        second_c = send(low(second[1][0].astype(F32) + second_a.astype(F32)), x=1)
        return (
            first[0][0].astype(F32) + first_b.astype(F32) + first_c.astype(F32),
            second[0][0].astype(F32) + second_b.astype(F32) + second_c.astype(F32),
        )

    def ring_gather(block):
        blocks = [block]
        for _ in range(NZ - 1):
            blocks.append(send(blocks[-1], z=-1))
        return blocks

    def core_gather(block):
        return [block] + [send(block, c=k) for k in range(1, nc)]

    def core_sum(parts):
        total = parts[0].astype(F32)
        for k in range(1, nc):
            total = total + send(parts[k].astype(BF16), c=k).astype(F32)
        return total

    def ring_sum(part_of):
        moving = None
        for s in list(range(1, NZ)) + [0]:
            total = part_of(s)
            if moving is not None:
                total = total + moving.astype(F32)
            if s == 0:
                return total
            moving = send(total.astype(BF16), z=-1)

    def body(
        layer_input,
        lengths,
        w_query,
        w_key,
        w_value,
        w_output,
        query_gain,
        key_gain,
        attn_gain,
        mlp_gain,
        w_gate,
        w_up,
        w_down,
        grad_output,
    ):
        x = lax.axis_index("blk")
        place = lax.axis_index("wide")
        z, y, c = place // (NY * nc), (place // nc) % NY, place % nc
        inputs = layer_input[0]
        tok, width = inputs.shape
        rows = w_query.shape[0]
        head_cols = NZ * HEAD_DIM
        group_tok = NX * NY * tok

        def pieces(weight):
            weight = weight.reshape(rows, NX, NZ, NY, HEAD_DIM)
            return flipped(flipped(weight, 1, x), 3, y)

        split = [pieces(weight) for weight in (w_query, w_key, w_value)]

        def piece(dx, dy):
            return jnp.concatenate(
                [part[:, dx, :, dy].reshape(rows, head_cols) for part in split], axis=1
            )

        received = [
            [piece(0, 0), send(piece(0, 1), y=1)],
            [send(piece(1, 0), x=1), send(piece(1, 1), x=1, y=1)],
        ]
        own_rows = jnp.stack([jnp.stack(row) for row in received])
        mine = rolled(inputs.reshape(tok, NX, NZ, NY * HEAD_DIM), 2, z).reshape(tok, width)
        upper, lower = square_gather(mine[: tok // 2], mine[tok // 2 :])

        def token_blocks(first, second):
            return jnp.concatenate(
                [
                    half
                    for dy in range(NY)
                    for dx in range(NX)
                    for half in (first[dx][dy], second[dx][dy])
                ],
                axis=0,
            )

        x_all = token_blocks(upper, lower).reshape(group_tok, NX, NZ, NY, HEAD_DIM)
        x_all = flipped(flipped(x_all, 1, x), 3, y)

        def x_part(s):
            return x_all[:, :, s].reshape(group_tok, NX * NY * HEAD_DIM)

        projected = 0.0
        w_parts = []
        for block in ring_gather(own_rows):
            w_part = jnp.stack(core_gather(block), axis=2)
            w_part = xored(w_part, 2, c).reshape(NX * NY * nc * rows, 3 * head_cols)
            w_parts.append(w_part)
        for s in range(NZ):
            projected = projected + dot(x_part(s), w_parts[s], 1, 0)
        query = projected[:, :head_cols]
        key_proj = projected[:, head_cols : 2 * head_cols]
        value_b = projected[:, 2 * head_cols :].astype(BF16)

        packed = jnp.stack([query_gain, key_gain, attn_gain, mlp_gain])
        by_z = jnp.stack([packed] + [send(packed, z=-s) for s in range(1, NZ)])
        by_z = rolled(by_z, 0, (NZ - z) % NZ)
        by_c = xored(jnp.stack(core_gather(by_z)), 0, c)
        group_gains = by_c.transpose(2, 1, 0, 3).reshape(4, head_cols).astype(F32)
        gain_query, gain_key = group_gains[0], group_gains[1]
        by_xy = jnp.stack(
            [
                jnp.stack([by_c, send(by_c, y=1)]),
                jnp.stack([send(by_c, x=1), send(by_c, x=1, y=1)]),
            ]
        )
        by_xy = flipped(flipped(by_xy, 0, x), 1, y)
        full_gains = by_xy.transpose(4, 0, 3, 1, 2, 5).reshape(4, width).astype(F32)
        gain_attn, gain_mlp = full_gains[2], full_gains[3]

        out_parts = [
            xored(jnp.stack(core_gather(block)), 0, c) for block in ring_gather(w_output)
        ]
        out_w = rolled(jnp.stack(out_parts), 0, (NZ - z) % NZ).reshape(head_cols, width)
        gate_parts, up_parts = square_gather(w_gate, w_up)
        half_hidden = w_down.shape[0] // 2
        down_first, down_second = square_gather(w_down[:half_hidden], w_down[half_hidden:])

        def joined(blocks):
            return jnp.concatenate([jnp.concatenate(row, axis=1) for row in blocks], axis=0)

        gate_w, up_w = joined(gate_parts), joined(up_parts)
        down_w = jnp.concatenate(
            [
                jnp.concatenate(row, axis=1)
                for dx in range(NX)
                for row in (down_first[dx], down_second[dx])
            ],
            axis=0,
        )

        positions = jnp.concatenate(
            [
                x * tok + jnp.arange(tok, dtype=jnp.int32),
                (1 - x) * tok + jnp.arange(tok, dtype=jnp.int32),
            ]
        )
        half = HEAD_DIM // 2
        frequency = jnp.exp(
            jnp.arange(half, dtype=F32) * (-2.0 * math.log(500000.0) / HEAD_DIM)
        )
        angles = positions.astype(F32)[:, None] * frequency[None, :]
        cosine = jnp.cos(angles)[None, :, None, :]
        sine = jnp.sin(angles)[None, :, None, :]

        def turn(values, sign):
            view = values.reshape(NY, NX * tok, NZ, HEAD_DIM)
            first, second = view[..., :half], view[..., half:]
            turned = jnp.concatenate(
                [first * cosine - sign * second * sine, second * cosine + sign * first * sine],
                axis=-1,
            )
            return turned.reshape(group_tok, head_cols)

        def group_sum(values):
            values = values.reshape(-1, NY, NX, tok)
            total = (
                values
                + jnp.flip(send(values, x=1), 2)
                + jnp.flip(send(values, y=1), 1)
                + jnp.flip(send(values, x=1, y=1), (1, 2))
            )
            return total.reshape(-1, group_tok)

        squares = group_sum(
            jnp.stack([jnp.sum(query * query, axis=1), jnp.sum(key_proj * key_proj, axis=1)])
        )
        scales = lax.rsqrt(squares / width + EPSILON)
        scale_q, scale_k = scales[0][:, None], scales[1][:, None]
        query_b = turn(query * scale_q * gain_query, 1.0).astype(BF16)
        key_b = turn(key_proj * scale_k * gain_key, 1.0).astype(BF16)

        def heads(values):
            return values.reshape(NY, NX * tok, NZ, HEAD_DIM)

        length = lengths.astype(F32)
        both = jnp.concatenate([length, send(length, y=1)]).astype(jnp.int32)
        valid = (positions[None, None, :] <= positions[None, :, None]) & (
            positions[None, None, :] < both[:, None, None]
        )
        logits = jnp.einsum(
            "sqhd,skhd->shqk", heads(query_b), heads(key_b), preferred_element_type=F32
        ) * HEAD_DIM ** (-0.5)
        logits = jnp.where(valid[:, None], logits, NEGATIVE)
        powers = jnp.exp(logits - jnp.max(logits, axis=-1, keepdims=True))
        chances = powers / jnp.sum(powers, axis=-1, keepdims=True)
        chances_b = chances.astype(BF16)
        attended = (
            jnp.einsum("shqk,skhd->sqhd", chances_b, heads(value_b), preferred_element_type=F32)
            .reshape(group_tok, head_cols)
            .astype(BF16)
        )

        branch_parts = dot(attended, out_w, 1, 0).astype(BF16).reshape(NY, NX, tok, width)

        def scatter_tokens(parts):
            return jnp.concatenate(
                square_scatter(
                    [[parts[dy, dx, : tok // 2] for dy in range(NY)] for dx in range(NX)],
                    [[parts[dy, dx, tok // 2 :] for dy in range(NY)] for dx in range(NX)],
                ),
                axis=0,
            )

        branch = scatter_tokens(branch_parts)
        normed, attn_back = jax.vjp(rms_scale, branch, gain_attn)
        hidden_state = inputs.astype(F32) + normed

        def half_order(values):
            return flipped(values.reshape(-1, NX, width // NX), 1, x).reshape(-1, width)

        def core_parts(values):
            values = values.reshape(nc, tok, width)
            return [values[k] for k in range(nc)]

        mlp_in = half_order(hidden_state.astype(BF16))
        mlp_blocks = []
        kept = []
        out_sums = []
        for block in ring_gather(mlp_in):
            block = jnp.concatenate(core_gather(block), axis=0)
            gate, up_proj = dot(block, gate_w, 1, 0), dot(block, up_w, 1, 0)
            product = (jax.nn.silu(gate) * up_proj).astype(BF16)
            mlp_blocks.append(block)
            kept.append((gate, up_proj, product))
            out_sums.append(core_sum(core_parts(dot(product, down_w, 1, 1))))
        mlp_out = half_order(ring_sum(lambda s: out_sums[s]))
        post, mlp_back = jax.vjp(rms_scale, mlp_out, gain_mlp)
        output = (hidden_state + post).astype(BF16)

        grad_out = grad_output[0].astype(F32)
        grad_mlp, grad_gain_mlp = mlp_back(grad_out)
        grad_blocks = []
        gate_grads = []
        up_grads = []
        mid_sums = []
        for s, block in enumerate(ring_gather(half_order(grad_mlp.astype(BF16)))):
            block = jnp.concatenate(core_gather(block), axis=0)
            gate, up_proj, product = kept[s]
            grad_prod = dot(block, down_w, 1, 0)
            chance = jax.nn.sigmoid(gate)
            grad_up = (grad_prod * gate * chance).astype(BF16)
            grad_gate = (
                grad_prod * up_proj * chance * (1.0 + gate * (1.0 - chance))
            ).astype(BF16)
            grad_blocks.append(block)
            gate_grads.append(grad_gate)
            up_grads.append(grad_up)
            mid_sums.append(
                core_sum(core_parts(dot(grad_gate, gate_w, 1, 1) + dot(grad_up, up_w, 1, 1)))
            )
        grad_mid = half_order(ring_sum(lambda s: mid_sums[s]))

        mlp_all = jnp.concatenate(mlp_blocks, axis=0)
        grad_all = jnp.concatenate(grad_blocks, axis=0)
        product_all = jnp.concatenate([entry[2] for entry in kept], axis=0)
        grad_wd = dot(grad_all, product_all, 0, 0).astype(BF16)
        grad_wg = dot(mlp_all, jnp.concatenate(gate_grads, axis=0), 0, 0).astype(BF16)
        grad_wu = dot(mlp_all, jnp.concatenate(up_grads, axis=0), 0, 0).astype(BF16)

        def quarters(values):
            height, span = values.shape[0] // NX, values.shape[1] // NY
            return [
                [
                    values[dx * height : (dx + 1) * height, dy * span : (dy + 1) * span]
                    for dy in range(NY)
                ]
                for dx in range(NX)
            ]

        grad_wd_parts = quarters(grad_wd)
        grad_wd = jnp.concatenate(
            square_scatter(
                [[part[:half_hidden] for part in row] for row in grad_wd_parts],
                [[part[half_hidden:] for part in row] for row in grad_wd_parts],
            ),
            axis=0,
        )
        grad_wg, grad_wu = square_scatter(quarters(grad_wg), quarters(grad_wu))

        grad_hidden = grad_out + grad_mid
        grad_branch, grad_gain_attn = attn_back(grad_hidden)
        branch_b = grad_branch.astype(BF16)
        branch_all = token_blocks(*square_gather(branch_b[: tok // 2], branch_b[tok // 2 :]))
        grad_att = dot(branch_all, out_w, 1, 1).astype(BF16)
        grad_wo = dot(attended, branch_all, 0, 0).astype(BF16).reshape(NZ, nc, rows, width)
        grad_wo = rolled(grad_wo, 0, z)
        grad_chances = jnp.einsum(
            "sqhd,skhd->shqk", heads(grad_att), heads(value_b), preferred_element_type=F32
        )
        grad_value = (
            jnp.einsum("shqk,sqhd->skhd", chances_b, heads(grad_att), preferred_element_type=F32)
            .reshape(group_tok, head_cols)
            .astype(BF16)
        )
        balance = jnp.sum(chances * grad_chances, axis=-1, keepdims=True)
        grad_logits = (chances * (grad_chances - balance)).astype(BF16)
        grad_query = jnp.einsum(
            "shqk,skhd->sqhd", grad_logits, heads(key_b), preferred_element_type=F32
        ).reshape(group_tok, head_cols) * HEAD_DIM ** (-0.5)
        grad_key = jnp.einsum(
            "shqk,sqhd->skhd", grad_logits, heads(query_b), preferred_element_type=F32
        ).reshape(group_tok, head_cols) * HEAD_DIM ** (-0.5)
        grad_query = turn(grad_query, -1.0)
        grad_key = turn(grad_key, -1.0)
        grad_gain_query = jnp.sum(grad_query * query * scale_q, axis=0)
        grad_gain_key = jnp.sum(grad_key * key_proj * scale_k, axis=0)
        grad_query = grad_query * gain_query
        grad_key = grad_key * gain_key
        means = (
            group_sum(
                jnp.stack(
                    [jnp.sum(grad_query * query, axis=1), jnp.sum(grad_key * key_proj, axis=1)]
                )
            )
            / width
        )
        grad_query = scale_q * (grad_query - query * (scale_q * scale_q * means[0][:, None]))
        grad_key = scale_k * (grad_key - key_proj * (scale_k * scale_k * means[1][:, None]))
        grads = jnp.concatenate(
            [grad_query.astype(BF16), grad_key.astype(BF16), grad_value], axis=1
        )

        grad_x = jnp.stack(
            [
                dot(grads, w_parts[s], 1, 1).astype(BF16).reshape(group_tok, NX, NY, HEAD_DIM)
                for s in range(NZ)
            ],
            axis=2,
        )
        grad_x = flipped(flipped(grad_x, 1, x), 3, y).reshape(NY, NX, tok, width)
        grad_x = scatter_tokens(grad_x).reshape(tok, NX, NZ, NY * HEAD_DIM)
        grad_x = rolled(grad_x, 2, (NZ - z) % NZ).reshape(tok, width)
        grad_input = (grad_hidden + grad_x).astype(BF16)

        def weight_part(s):
            part = dot(x_part(s), grads, 0, 0).astype(BF16)
            part = xored(part.reshape(NX * NY, nc, rows, 3 * head_cols), 1, c)
            return core_sum([part[:, k] for k in range(nc)])

        summed = ring_sum(weight_part).astype(BF16).reshape(NX, NY, rows, 3 * head_cols)
        blocks = jnp.stack(
            [
                jnp.stack([summed[0, 0], send(summed[0, 1], y=1)]),
                jnp.stack([send(summed[1, 0], x=1), send(summed[1, 1], x=1, y=1)]),
            ]
        )
        blocks = flipped(flipped(blocks, 0, x), 1, y)
        blocks = blocks.reshape(NX, NY, rows, 3, NZ, HEAD_DIM)
        blocks = blocks.transpose(3, 2, 0, 4, 1, 5)
        blocks = blocks.reshape(3, rows, width).astype(F32)

        def out_part(s):
            part = xored(grad_wo[s], 0, c)
            return core_sum([part[k] for k in range(nc)])

        grad_wo = ring_sum(out_part)

        wide_gains = jnp.stack([grad_gain_attn, grad_gain_mlp]).reshape(
            2, NX, NZ, NY, nc * rows
        )
        wide_gains = flipped(flipped(rolled(wide_gains, 2, z), 1, x), 3, y)
        own_gains = (
            wide_gains[:, 0, :, 0]
            + send(wide_gains[:, 1, :, 0], x=1)
            + send(wide_gains[:, 0, :, 1], y=1)
            + send(wide_gains[:, 1, :, 1], x=1, y=1)
        )
        head_gains = jnp.stack([grad_gain_query, grad_gain_key]).reshape(2, NZ, nc * rows)
        head_gains = rolled(head_gains, 1, z)
        gains = jnp.concatenate([head_gains, own_gains], axis=0).reshape(4, NZ, nc, rows)
        gains = xored(gains, 2, c)
        total = gains[:, :, 0]
        for k in range(1, nc):
            total = total + send(gains[:, :, k], c=k)
        gain_sums = total[:, 0]
        for s in range(1, NZ):
            gain_sums = gain_sums + send(total[:, s], z=s)

        return (
            output[None],
            grad_input[None],
            blocks[0],
            blocks[1],
            blocks[2],
            grad_wo,
            gain_sums[0],
            gain_sums[1],
            gain_sums[2],
            gain_sums[3],
            grad_wg,
            grad_wu,
            grad_wd,
        )

    return body


def solution(mesh):
    return jax.shard_map(
        make_body(mesh.shape["wide"]),
        mesh=mesh,
        in_specs=(
            P("wide", "blk", None),
            P("wide"),
            P(("blk", "wide"), None),
            P(("blk", "wide"), None),
            P(("blk", "wide"), None),
            P(("blk", "wide"), None),
            P(("blk", "wide")),
            P(("blk", "wide")),
            P(("blk", "wide")),
            P(("blk", "wide")),
            P("blk", "wide"),
            P("blk", "wide"),
            P("blk", "wide"),
            P("wide", "blk", None),
        ),
        out_specs=(
            P("wide", "blk", None),
            P("wide", "blk", None),
            P(("blk", "wide"), None),
            P(("blk", "wide"), None),
            P(("blk", "wide"), None),
            P(("blk", "wide"), None),
            P(("blk", "wide")),
            P(("blk", "wide")),
            P(("blk", "wide")),
            P(("blk", "wide")),
            P("blk", "wide"),
            P("blk", "wide"),
            P("blk", "wide"),
        ),
        check_vma=False,
    )
```

```python
import functools
import math

import jax
import jax.numpy as jnp
from jax import lax
from jax.experimental import pallas as pl
from jax.experimental.pallas import tpu as pltpu
from jax.sharding import PartitionSpec as P

HEAD_DIM = 128
EPSILON = 1e-06
NEGATIVE = -1e30
BF16 = jnp.bfloat16
F32 = jnp.float32
AXES = ("blk", "wide")
NX, NY, NZ = 2, 2, 4
GROUP = NX * NY
HEADS = NZ * HEAD_DIM
MIB = 1 << 20
SMEM = pl.BlockSpec(memory_space=pltpu.SMEM)
VMEM = pl.BlockSpec(memory_space=pltpu.VMEM)
ANY = pl.BlockSpec(memory_space=pl.ANY)
SQUARE = [(dx, dy) for dx in range(NX) for dy in range(NY)]
TOKEN_BLOCKS = [(dx, dy) for dy in range(NY) for dx in range(NX)]


def shaped(shape, dtype=BF16):
    return jax.ShapeDtypeStruct(tuple(shape), dtype)


def nn(left, right):
    return lax.dot_general(left, right, (((1,), (0,)), ((), ())), preferred_element_type=F32)


def nt(left, right):
    return lax.dot_general(left, right, (((1,), (1,)), ((), ())), preferred_element_type=F32)


def tn(left, right):
    return lax.dot_general(left, right, (((0,), (0,)), ((), ())), preferred_element_type=F32)


def run(body, outs, ins, specs=None, limit=32, **options):
    return pl.pallas_call(
        body,
        out_shape=outs,
        in_specs=specs or [VMEM] * len(ins),
        compiler_params=pltpu.CompilerParams(vmem_limit_bytes=limit * MIB),
        cost_estimate=pl.CostEstimate(flops=0, bytes_accessed=0, transcendentals=0),
        **options,
    )(*ins)


def place(pos):
    return pos[0], pos[1], pos[2], pos[3]


def column_of(x, z, y):
    return pl.multiple_of(((x * NZ + z) * NY + y) * HEAD_DIM, HEAD_DIM)


def split_kernel(pos, w_query, w_key, w_value, *outs):
    x, _, y, _ = place(pos)
    for (dx, dy), out in zip(SQUARE, outs):
        for i, weight in enumerate((w_query, w_key, w_value)):
            for head in range(NZ):
                start = column_of(x ^ dx, head, y ^ dy)
                at = i * HEADS + head * HEAD_DIM
                out[:, at : at + HEAD_DIM] = weight[:, pl.ds(start, HEAD_DIM)]


def join_kernel(*refs):
    *parts, out = refs
    rows = parts[0].shape[0]
    for i, part in enumerate(parts):
        out[i * rows : (i + 1) * rows] = part[...]


def gain_kernel(pos, *refs):
    *blocks, out = refs
    x, z, y, _ = place(pos)
    for (dx, dy), block in zip(SQUARE, blocks):
        for s in range(NZ):
            start = column_of(x ^ dx, (z + s) % NZ, y ^ dy)
            out[:, pl.ds(start, HEAD_DIM)] = block[s]


def row_stats(first, second):
    rows = lax.broadcasted_iota(jnp.int32, (8, first.shape[1]), 0)
    upper = jnp.where(rows < 4, 1.0, 0.0).astype(F32)
    high = functools.partial(
        lax.dot_general,
        dimension_numbers=(((1,), (1,)), ((), ())),
        preferred_element_type=F32,
        precision=lax.Precision.HIGHEST,
    )
    return high(upper, first) + high(1.0 - upper, second)


def group_total(stats, tok):
    blocks = []
    for dx, dy in TOKEN_BLOCKS:
        total = 0.0
        for (sx, sy), ref in zip(SQUARE, stats):
            at = ((dy ^ sy) * NX + (dx ^ sx)) * tok
            total = total + ref[:, at : at + tok]
        blocks.append(total)
    return jnp.concatenate(blocks, axis=1)


def project_kernel(nc, pos, *refs):
    x, z, y, c = place(pos)
    tokens, refs = refs[:GROUP], refs[GROUP:]
    weights, refs = refs[: NZ * nc], refs[NZ * nc :]
    query, key, value, stats, x_all, w_all, sems = refs
    tok = tokens[0].shape[0]
    rows = weights[0].shape[0] // GROUP
    copies = []
    for s in range(NZ):
        for k in range(nc):
            for i, (dx, dy) in enumerate(SQUARE):
                start = column_of(x ^ dx, (z + s) % NZ, y ^ dy) + (c ^ k) * rows
                copies.append(
                    pltpu.make_async_copy(
                        weights[s * nc + k].at[pl.ds(i * rows, rows)],
                        w_all.at[pl.ds(pl.multiple_of(start, rows), rows)],
                        sems.at[len(copies)],
                    )
                )
    for copy in copies:
        copy.start()
    for i, (dx, dy) in enumerate(TOKEN_BLOCKS):
        x_all[i * tok : (i + 1) * tok] = tokens[SQUARE.index((dx, dy))][...]
    for copy in copies:
        copy.wait()
    for out, at in ((query, 0), (key, HEADS), (value, 2 * HEADS)):
        for half in range(2):
            start = half * (HEADS // 2)
            columns = slice(at + start, at + start + HEADS // 2)
            result = nn(x_all[...], w_all[:, columns])
            out[:, start : start + HEADS // 2] = result.astype(out.dtype)
    stats[...] = row_stats(query[...] * query[...], key[...] * key[...])


def turn(values, cosine, sine):
    return values * cosine + pltpu.roll(values, HEAD_DIM // 2, 1) * sine


def valid_keys(x, length, tok):
    shape = (NX * tok, NX * tok)
    queries = lax.broadcasted_iota(jnp.int32, shape, 0)
    keys = lax.broadcasted_iota(jnp.int32, shape, 1)

    def at(index):
        return jnp.where(index < tok, x * tok + index, (1 - x) * tok + index - tok)

    return (at(keys) <= at(queries)) & (at(keys) < length)


def softmax(query, key, valid):
    logits = jnp.where(valid, nt(query, key) * HEAD_DIM ** (-0.5), NEGATIVE)
    powers = jnp.exp(logits - jnp.max(logits, axis=1, keepdims=True))
    return powers / jnp.sum(powers, axis=1, keepdims=True)


def attend_kernel(nc, pos, *refs):
    x, z, y, c = place(pos)
    stats, refs = refs[:GROUP], refs[GROUP:]
    query, key, value, gains, cosine, sine, *refs = refs
    out_parts, refs = refs[: NZ * nc], refs[NZ * nc :]
    query_r, key_r, scales, attended, out_w, *refs = refs
    pieces, sems = refs[:GROUP], refs[GROUP]
    tok = query.shape[0] // GROUP
    span = NX * tok
    rows = out_parts[0].shape[0]
    copies = []
    for s in range(NZ):
        for k in range(nc):
            start = ((z + s) % NZ) * HEAD_DIM + (c ^ k) * rows
            copies.append(
                pltpu.make_async_copy(
                    out_parts[s * nc + k],
                    out_w.at[pl.ds(pl.multiple_of(start, rows), rows)],
                    sems.at[len(copies)],
                )
            )
    for copy in copies:
        copy.start()
    width = out_w.shape[1]
    scale = lax.rsqrt(group_total(stats, tok) / width + EPSILON)
    scales[...] = scale
    for seq in range(NY):
        at = slice(seq * span, (seq + 1) * span)
        columns = jnp.transpose(scale[:, at])
        valid = valid_keys(x, pos[4 + seq], tok)
        for head in range(NZ):
            lanes = slice(head * HEAD_DIM, (head + 1) * HEAD_DIM)
            gain = pl.ds(column_of(x, head, y), HEAD_DIM)
            turned = []
            for row, (raw, out) in enumerate(((query, query_r), (key, key_r))):
                normed = raw[at, lanes] * columns[:, 4 * row : 4 * row + 1]
                normed = normed * gains[row : row + 1, gain]
                out[at, lanes] = turn(normed, cosine[...], sine[...]).astype(BF16)
            chances = softmax(query_r[at, lanes], key_r[at, lanes], valid)
            attended[at, lanes] = nn(chances.astype(BF16), value[at, lanes]).astype(BF16)
    for copy in copies:
        copy.wait()
    step = width // 4
    for part in range(4):
        columns = slice(part * step, (part + 1) * step)
        result = nn(attended[...], out_w[:, columns])
        for i, block in enumerate(TOKEN_BLOCKS):
            out = pieces[SQUARE.index(block)]
            out[:, columns] = result[i * tok : (i + 1) * tok].astype(out.dtype)


def in_halves(values, x, out):
    half = out.shape[1] // NX
    for dx in range(NX):
        start = pl.multiple_of((x ^ dx) * half, half)
        out[:, dx * half : (dx + 1) * half] = values[:, pl.ds(start, half)].astype(out.dtype)


def sum_of(refs):
    total = refs[0][...].astype(F32)
    for ref in refs[1:]:
        total = total + ref[...].astype(F32)
    return total


def branch_kernel(pos, *refs):
    parts, refs = refs[:GROUP], refs[GROUP:]
    inputs, gains, branch_out, hidden_out, mlp_in, scratch = refs
    branch = sum_of(parts)
    branch_out[...] = branch
    scale = lax.rsqrt(jnp.mean(branch * branch, axis=1, keepdims=True) + EPSILON)
    hidden = inputs[...].astype(F32) + branch * scale * gains[2:3, :]
    hidden_out[...] = hidden
    scratch[...] = hidden
    in_halves(scratch, pos[0], mlp_in)


def norm_back(values, gain, grad):
    scale = lax.rsqrt(jnp.mean(values * values, axis=1, keepdims=True) + EPSILON)
    normed = values * scale
    scaled = grad * gain
    mean = jnp.mean(scaled * normed, axis=1, keepdims=True)
    return scale * (scaled - normed * mean), jnp.sum(grad * normed, axis=0, keepdims=True)


def mlp_kernel(count, pos, *refs):
    parts, refs = refs[:count], refs[count:]
    hidden, gains, grad_output, output, grad_in, grad_gain, halves, mlp_out = refs
    halves[...] = sum_of(parts)
    in_halves(halves, pos[0], mlp_out)
    values = mlp_out[...]
    gain = gains[3:4, :]
    scale = lax.rsqrt(jnp.mean(values * values, axis=1, keepdims=True) + EPSILON)
    output[...] = (hidden[...] + values * scale * gain).astype(BF16)
    grad, by_gain = norm_back(values, gain, grad_output[...].astype(F32))
    halves[...] = grad
    in_halves(halves, pos[0], grad_in)
    grad_gain[...] = jnp.broadcast_to(by_gain, grad_gain.shape)


def branch_back_kernel(count, pos, *refs):
    parts, refs = refs[:count], refs[count:]
    branch, gains, grad_output, grad_hidden, grad_branch, grad_gain, halves, middle = refs
    halves[...] = sum_of(parts)
    in_halves(halves, pos[0], middle)
    total = grad_output[...].astype(F32) + middle[...]
    grad_hidden[...] = total
    grad, by_gain = norm_back(branch[...], gains[2:3, :], total)
    grad_branch[...] = grad.astype(BF16)
    grad_gain[...] = jnp.broadcast_to(by_gain, grad_gain.shape)


def attend_back_kernel(pos, *refs):
    blocks, refs = refs[:GROUP], refs[GROUP:]
    out_w, query_r, key_r, value, query, key, scales, gains, cosine, sine, *refs = refs
    branch_all, grad_query, grad_key, grad_value, stats, head_gains, grad_att = refs
    x, _, y, _ = place(pos)
    tok = blocks[0].shape[0]
    span = NX * tok
    for i, block in enumerate(TOKEN_BLOCKS):
        branch_all[i * tok : (i + 1) * tok] = blocks[SQUARE.index(block)][...]
    for half in range(2):
        lanes = slice(half * (HEADS // 2), (half + 1) * (HEADS // 2))
        grad_att[:, lanes] = nt(branch_all[...], out_w[lanes, :]).astype(BF16)
    head_gains[...] = jnp.zeros_like(head_gains)
    for seq in range(NY):
        at = slice(seq * span, (seq + 1) * span)
        columns = jnp.transpose(scales[:, at])
        valid = valid_keys(x, pos[4 + seq], tok)
        for head in range(NZ):
            lanes = slice(head * HEAD_DIM, (head + 1) * HEAD_DIM)
            gain = pl.ds(column_of(x, head, y), HEAD_DIM)
            queries, keys, values = query_r[at, lanes], key_r[at, lanes], value[at, lanes]
            chances = softmax(queries, keys, valid)
            incoming = grad_att[at, lanes]
            grad_chances = nt(incoming, values)
            grad_value[at, lanes] = tn(chances.astype(BF16), incoming).astype(BF16)
            balance = jnp.sum(chances * grad_chances, axis=1, keepdims=True)
            grad_logits = (chances * (grad_chances - balance)).astype(BF16)
            by_query = nn(grad_logits, keys) * HEAD_DIM ** (-0.5)
            by_key = tn(grad_logits, queries) * HEAD_DIM ** (-0.5)
            for row, (grad, raw, out) in enumerate(
                ((by_query, query, grad_query), (by_key, key, grad_key))
            ):
                back = turn(grad.astype(BF16).astype(F32), cosine[...], -sine[...])
                normed = raw[at, lanes] * columns[:, 4 * row : 4 * row + 1]
                head_gains[row : row + 1, lanes] += jnp.sum(back * normed, axis=0, keepdims=True)
                out[at, lanes] = back * gains[row : row + 1, gain]
    stats[...] = row_stats(grad_query[...] * query[...], grad_key[...] * key[...])


def input_back_kernel(*refs):
    stats, refs = refs[:GROUP], refs[GROUP:]
    grad_query, grad_key, grad_value, query, key, scales, w_all, *refs = refs
    grads, *pieces = refs
    tok = query.shape[0] // GROUP
    width = w_all.shape[0]
    means = jnp.transpose(group_total(stats, tok) / width)
    columns = jnp.transpose(scales[...])
    for row, (grad, raw) in enumerate(((grad_query, query), (grad_key, key))):
        scale = columns[:, 4 * row : 4 * row + 1]
        mean = means[:, 4 * row : 4 * row + 1]
        result = scale * (grad[...] - raw[...] * (scale * scale * mean))
        grads[:, row * HEADS : (row + 1) * HEADS] = result.astype(BF16)
    grads[:, 2 * HEADS :] = grad_value[...]
    step = width // 8
    for part in range(8):
        lanes = slice(part * step, (part + 1) * step)
        result = nt(grads[...], w_all[lanes, :])
        for i, block in enumerate(TOKEN_BLOCKS):
            out = pieces[SQUARE.index(block)]
            out[:, lanes] = result[i * tok : (i + 1) * tok].astype(out.dtype)


def weight_back_kernel(nc, s, pos, x_all, grads, *refs):
    *outs, columns, sums = refs
    x, z, y, c = place(pos)
    rows = outs[0].shape[0] // GROUP
    for i, (dx, dy) in enumerate(SQUARE):
        start = column_of(x ^ dx, (z + s) % NZ, y ^ dy)
        columns[:, i * HEAD_DIM : (i + 1) * HEAD_DIM] = x_all[:, pl.ds(start, HEAD_DIM)]
    step = grads.shape[1] // 3
    for part in range(3):
        lanes = slice(part * step, (part + 1) * step)
        sums[:, lanes] = tn(columns[...], grads[:, lanes]).astype(BF16)
    for k, out in enumerate(outs):
        for i in range(GROUP):
            start = pl.multiple_of(i * HEAD_DIM + (c ^ k) * rows, rows)
            out[i * rows : (i + 1) * rows] = sums[pl.ds(start, rows), :]


def pick_kernel(nc, pos, whole, *outs):
    _, z, _, c = place(pos)
    rows = outs[0].shape[0]
    for s in range(NZ):
        for k in range(nc):
            start = ((z + s) % NZ) * HEAD_DIM + (c ^ k) * rows
            outs[s * nc + k][...] = whole[pl.ds(pl.multiple_of(start, rows), rows), :]


def spread_kernel(pos, *refs):
    parts, outs = refs[:GROUP], refs[GROUP:]
    x, _, y, _ = place(pos)
    for (dx, dy), part in zip(SQUARE, parts):
        for i, out in enumerate(outs):
            for head in range(NZ):
                start = column_of(x ^ dx, head, y ^ dy)
                at = i * HEADS + head * HEAD_DIM
                out[:, pl.ds(start, HEAD_DIM)] = part[:, at : at + HEAD_DIM].astype(F32)


def gain_split_kernel(pos, attn, mlp, *outs):
    x, z, y, _ = place(pos)
    for (dx, dy), out in zip(SQUARE, outs):
        out[...] = jnp.zeros_like(out)
        for s in range(NZ):
            start = column_of(x ^ dx, (z + s) % NZ, y ^ dy)
            for row, grad in ((2, attn), (3, mlp)):
                out[s, row : row + 1, :] = grad[0:1, pl.ds(start, HEAD_DIM)]


def gain_sum_kernel(pos, *refs):
    parts, refs = refs[:GROUP], refs[GROUP:]
    heads, *outs = refs
    z = pos[1]
    for s, out in enumerate(outs):
        total = parts[0][s]
        for part in parts[1:]:
            total = total + part[s]
        out[...] = total
        start = pl.multiple_of(((z + s) % NZ) * HEAD_DIM, HEAD_DIM)
        out[0:2, :] = heads[0:2, pl.ds(start, HEAD_DIM)]


def mlp_forward_kernel(nc, per, *refs):
    blocks, refs = refs[:nc], refs[nc:]
    gates, ups, downs, refs = refs[:4], refs[4:8], refs[8:16], refs[16:]
    outs = refs[-(8 + nc + 1) :]
    products, by_gate, by_up, kept = outs[0:2], outs[2:4], outs[4:6], outs[6:8]
    sums, total = outs[8 : 8 + nc], outs[8 + nc]
    j = pl.program_id(0)
    tok = blocks[0].shape[0]
    half = kept[0].shape[1]

    @pl.when(j == 0)
    def _():
        for k, block in enumerate(blocks):
            for dx in range(NX):
                kept[dx][k * tok : (k + 1) * tok] = block[:, dx * half : (dx + 1) * half]

    for dy in range(NY):

        @pl.when(j // per == dy)
        def _(dy=dy):
            def through(weights):
                return nn(kept[0][...], weights[dy][...]) + nn(
                    kept[1][...], weights[NY + dy][...]
                )

            gate, up = through(gates), through(ups)
            chance = 1.0 / (1.0 + jnp.exp(-gate))
            silu = gate * chance
            product = (silu * up).astype(BF16)
            products[dy][...] = product
            by_up[dy][...] = silu.astype(BF16)
            by_gate[dy][...] = (up * (chance + silu * (1.0 - chance))).astype(BF16)
            quarter = half // 2
            for i in range(4):
                lanes = slice(i * quarter, (i + 1) * quarter)
                part = nt(product, downs[i * NY + dy][...])

                @pl.when(j == 0)
                def _(lanes=lanes, part=part):
                    total[:, lanes] = part

                @pl.when(j > 0)
                def _(lanes=lanes, part=part):
                    total[:, lanes] += part

    @pl.when(j == pl.num_programs(0) - 1)
    def _():
        for k, out in enumerate(sums):
            out[...] = total[k * tok : (k + 1) * tok].astype(out.dtype)


def mlp_back_kernel(nc, per, *refs):
    blocks, refs = refs[:nc], refs[nc:]
    gates, ups, downs, refs = refs[:4], refs[4:8], refs[8:16], refs[16:]
    by_gate, by_up = refs[0:2], refs[2:4]
    outs = refs[-(8 + nc + 1) :]
    grad_gates, grad_ups, kept = outs[0:2], outs[2:4], outs[4:8]
    sums, total = outs[8 : 8 + nc], outs[8 + nc]
    j = pl.program_id(0)
    tok = blocks[0].shape[0]
    quarter = kept[0].shape[1]

    @pl.when(j == 0)
    def _():
        for k, block in enumerate(blocks):
            for i in range(4):
                kept[i][k * tok : (k + 1) * tok] = block[:, i * quarter : (i + 1) * quarter]

    for dy in range(NY):

        @pl.when(j // per == dy)
        def _(dy=dy):
            grad = nn(kept[0][...], downs[dy][...])
            for i in range(1, 4):
                grad = grad + nn(kept[i][...], downs[i * NY + dy][...])
            grad_gate = (grad * by_gate[dy][...].astype(F32)).astype(BF16)
            grad_up = (grad * by_up[dy][...].astype(F32)).astype(BF16)
            grad_gates[dy][...] = grad_gate
            grad_ups[dy][...] = grad_up
            for i in range(4):
                lanes = slice(i * quarter, (i + 1) * quarter)
                dx, rows = i // 2, slice((i % 2) * quarter, (i % 2 + 1) * quarter)
                part = nt(grad_gate, gates[dx * NY + dy][rows, :]) + nt(
                    grad_up, ups[dx * NY + dy][rows, :]
                )

                @pl.when(j == 0)
                def _(lanes=lanes, part=part):
                    total[:, lanes] = part

                @pl.when(j > 0)
                def _(lanes=lanes, part=part):
                    total[:, lanes] += part

    @pl.when(j == pl.num_programs(0) - 1)
    def _():
        for k, out in enumerate(sums):
            out[...] = total[k * tok : (k + 1) * tok].astype(out.dtype)


def make_body(wide):
    nc = wide // (NY * NZ)

    def send(value, x=0, y=0, z=0, c=0):
        pairs = []
        for sx in range(NX):
            for sz in range(NZ):
                for sy in range(NY):
                    for sc in range(nc):
                        source = sx * wide + (sz * NY + sy) * nc + sc
                        target = (sx ^ x) * wide
                        target += (((sz + z) % NZ) * NY + (sy ^ y)) * nc + (sc ^ c)
                        pairs.append((source, target))
        return lax.ppermute(value, AXES, pairs)

    def square(parts):
        return [
            part if (dx, dy) == (0, 0) else send(part, x=dx, y=dy)
            for (dx, dy), part in zip(SQUARE, parts)
        ]

    def square_gather(first, second):
        first_x = send(first, x=1)
        second_y = send(second, y=1)
        first_y = send(first, y=1)
        second_x = send(second, x=1)
        first_xy = send(first_x, y=1)
        second_xy = send(second_y, x=1)
        return [first, first_y, first_x, first_xy], [second, second_y, second_x, second_xy]

    def square_scatter(first, second):
        first_a = send(first[3], x=1)
        second_a = send(second[3], y=1)
        first_b = send(first[2], x=1)
        second_b = send(second[1], y=1)
        first_c = send((first[1].astype(F32) + first_a.astype(F32)).astype(BF16), y=1)
        second_c = send((second[2].astype(F32) + second_a.astype(F32)).astype(BF16), x=1)
        return (
            first[0].astype(F32) + first_b.astype(F32) + first_c.astype(F32),
            second[0].astype(F32) + second_b.astype(F32) + second_c.astype(F32),
        )

    def ring_gather(block):
        blocks = [block]
        for _ in range(NZ - 1):
            blocks.append(send(blocks[-1], z=-1))
        return blocks

    def core_gather(block):
        return [block] + [send(block, c=k) for k in range(1, nc)]

    def core_parts(parts):
        return [parts[0]] + [send(parts[k], c=k) for k in range(1, nc)]

    def ring_parts(part_of):
        moving = []
        for s in list(range(1, NZ)) + [0]:
            parts = part_of(s) + moving
            if s == 0:
                return parts
            total = parts[0].astype(F32)
            for part in parts[1:]:
                total = total + part.astype(F32)
            moving = [send(total.astype(BF16), z=-1)]

    def body(
        layer_input,
        lengths,
        w_query,
        w_key,
        w_value,
        w_output,
        query_gain,
        key_gain,
        attn_gain,
        mlp_gain,
        w_gate,
        w_up,
        w_down,
        grad_output,
    ):
        x = lax.axis_index("blk")
        spot = lax.axis_index("wide")
        z, y, c = spot // (NY * nc), (spot // nc) % NY, spot % nc
        inputs = layer_input[0]
        tok, width = inputs.shape
        rows = w_query.shape[0]
        group_tok = GROUP * tok
        hidden = w_gate.shape[1]
        length = lengths.astype(F32)
        other = send(length, y=1)
        pos = jnp.concatenate(
            [jnp.stack([x, z, y, c]), length.astype(jnp.int32), other.astype(jnp.int32)]
        ).astype(jnp.int32)
        heads_shape = (group_tok, HEADS)

        pieces = run(
            split_kernel,
            [shaped((rows, 3 * HEADS))] * GROUP,
            (pos, w_query, w_key, w_value),
            [SMEM] + [VMEM] * 3,
        )
        own_rows = run(join_kernel, shaped((GROUP * rows, 3 * HEADS)), square(pieces))
        tokens = square([inputs] * GROUP)
        w_blocks = [part for block in ring_gather(own_rows) for part in core_gather(block)]
        query, key, value, stats, x_all, w_all = run(
            functools.partial(project_kernel, nc),
            [
                shaped(heads_shape, F32),
                shaped(heads_shape, F32),
                shaped(heads_shape),
                shaped((8, group_tok), F32),
                shaped((group_tok, width)),
                shaped((width, 3 * HEADS)),
            ],
            (pos, *tokens, *w_blocks),
            [SMEM] + [VMEM] * GROUP + [ANY] * len(w_blocks),
            scratch_shapes=[pltpu.SemaphoreType.DMA((GROUP * len(w_blocks),))],
        )

        packed = jnp.stack([query_gain, key_gain, attn_gain, mlp_gain]).astype(F32)
        by_c = jnp.stack(core_gather(packed))
        by_c = by_c[jnp.arange(nc) ^ c].transpose(1, 0, 2).reshape(4, HEAD_DIM)
        by_c = jnp.pad(by_c, ((0, 4), (0, 0)))
        by_z = jnp.stack([by_c] + [send(by_c, z=-s) for s in range(1, NZ)])
        gains = run(
            gain_kernel,
            shaped((8, width), F32),
            (pos, *square([by_z] * GROUP)),
            [SMEM] + [VMEM] * GROUP,
        )

        gate_w, up_w = square_gather(w_gate, w_up)
        down_rows = w_down.shape[0] // 2
        down_halves = square_gather(w_down[:down_rows], w_down[down_rows:])
        down_w = [
            down_halves[half][dx * NY + dy]
            for dx in range(NX)
            for half in range(2)
            for dy in range(NY)
        ]

        half = HEAD_DIM // 2
        order = jnp.concatenate([x * tok + jnp.arange(tok), (1 - x) * tok + jnp.arange(tok)])
        frequency = jnp.exp(
            jnp.arange(half, dtype=F32) * (-2.0 * math.log(500000.0) / HEAD_DIM)
        )
        angles = order.astype(F32)[:, None] * frequency[None, :]
        cosine = jnp.tile(jnp.cos(angles), (1, 2))
        sine = jnp.sin(angles)
        sine = jnp.concatenate([-sine, sine], axis=1)
        out_blocks = [part for block in ring_gather(w_output) for part in core_gather(block)]
        query_r, key_r, scales, attended, out_w, *parts = run(
            functools.partial(attend_kernel, nc),
            [
                shaped(heads_shape),
                shaped(heads_shape),
                shaped((8, group_tok), F32),
                shaped(heads_shape),
                shaped((HEADS, width)),
            ]
            + [shaped((tok, width))] * GROUP,
            (
                pos,
                *square([stats] * GROUP),
                query,
                key,
                value,
                gains,
                cosine,
                sine,
                *out_blocks,
            ),
            [SMEM] + [VMEM] * (GROUP + 6) + [ANY] * len(out_blocks),
            scratch_shapes=[pltpu.SemaphoreType.DMA((len(out_blocks),))],
        )
        branch, hidden_state, mlp_in = run(
            branch_kernel,
            [shaped((tok, width), F32), shaped((tok, width), F32), shaped((tok, width))],
            (pos, *square(parts), inputs, gains),
            [SMEM] + [VMEM] * (GROUP + 2),
            scratch_shapes=[pltpu.VMEM((tok, width), F32)],
        )

        m = nc * tok
        chunk = min(256, hidden)
        per = hidden // chunk
        steps = NY * per
        half_width = width // NX
        quarter = half_width // 2

        def chunk_of(dy):
            return lambda j: jnp.clip(j - dy * per, 0, per - 1)

        def weight_specs():
            specs = []
            for height, count in ((half_width, 4), (half_width, 4), (quarter, 8)):
                for i in range(count):
                    at = chunk_of(i % NY)
                    specs.append(pl.BlockSpec((height, chunk), lambda j, at=at: (0, at(j))))
            return specs

        def whole(shape):
            return pl.BlockSpec(shape, lambda j: (0, 0))

        def row_spec(s, dy):
            at = chunk_of(dy)
            return pl.BlockSpec((m, chunk), lambda j: (s, at(j)))

        def kept_spec(s, columns):
            return pl.BlockSpec((m, columns), lambda j: (s, 0))

        def mlp_call(kernel, s, block, extra, kept_columns, before):
            blocks = core_gather(block)
            ins = (*blocks, *gate_w, *up_w, *down_w, *extra)
            specs = [whole((tok, width))] * nc + weight_specs()
            specs += [row_spec(s, i % NY) for i in range(len(extra))]
            flat = 8 - len(kept_columns)
            outs = [shaped((NZ * m, hidden))] * flat
            outs += [shaped((NZ * m, columns)) for columns in kept_columns]
            aliases = {}
            if before is not None:
                aliases = {len(ins) + i: i for i in range(8)}
                ins = (*ins, *before)
                specs = specs + [ANY] * 8
            out_specs = [row_spec(s, i % NY) for i in range(flat)]
            out_specs += [kept_spec(s, columns) for columns in kept_columns]
            results = run(
                functools.partial(kernel, nc, per),
                outs + [shaped((tok, width), F32)] + [shaped((tok, width))] * (nc - 1),
                ins,
                specs,
                limit=56,
                grid=(steps,),
                out_specs=out_specs + [whole((tok, width))] * nc,
                input_output_aliases=aliases,
                scratch_shapes=[pltpu.VMEM((m, width), F32)],
            )
            return results[:8], core_parts(results[8:])

        kept = None
        sums = []
        for s, block in enumerate(ring_gather(mlp_in)):
            kept, parts = mlp_call(
                mlp_forward_kernel, s, block, (), (half_width, half_width), kept
            )
            sums.append(parts)
        products, by_gate, by_up, mlp_all = kept[0:2], kept[2:4], kept[4:6], kept[6:8]
        parts = ring_parts(lambda s: sums[s])
        output, grad_mlp, grad_gain_mlp = run(
            functools.partial(mlp_kernel, len(parts)),
            [shaped((tok, width)), shaped((tok, width)), shaped((8, width), F32)],
            (pos, *parts, hidden_state, gains, grad_output[0]),
            [SMEM] + [VMEM] * (len(parts) + 3),
            scratch_shapes=[pltpu.VMEM((tok, width), F32)] * 2,
        )
        kept = None
        sums = []
        for s, block in enumerate(ring_gather(grad_mlp)):
            kept, parts = mlp_call(
                mlp_back_kernel, s, block, (*by_gate, *by_up), (quarter,) * 4, kept
            )
            sums.append(parts)
        grad_gates, grad_ups, grad_all = kept[0:2], kept[2:4], kept[4:8]
        parts = ring_parts(lambda s: sums[s])
        grad_hidden, grad_branch, grad_gain_attn = run(
            functools.partial(branch_back_kernel, len(parts)),
            [shaped((tok, width), F32), shaped((tok, width)), shaped((8, width), F32)],
            (pos, *parts, branch, gains, grad_output[0]),
            [SMEM] + [VMEM] * (len(parts) + 3),
            scratch_shapes=[pltpu.VMEM((tok, width), F32)] * 2,
        )

        def products_of(left, right):
            return [tn(left[dx], right[dy]).astype(BF16) for dx, dy in SQUARE]

        grad_wg, grad_wu = square_scatter(
            products_of(mlp_all, grad_gates), products_of(mlp_all, grad_ups)
        )
        grad_wd = jnp.concatenate(
            square_scatter(
                products_of(grad_all[0::2], products), products_of(grad_all[1::2], products)
            ),
            axis=0,
        )

        branch_all, grad_query, grad_key, grad_value, stats, head_gains = run(
            attend_back_kernel,
            [
                shaped((group_tok, width)),
                shaped(heads_shape, F32),
                shaped(heads_shape, F32),
                shaped(heads_shape),
                shaped((8, group_tok), F32),
                shaped((8, HEADS), F32),
            ],
            (
                pos,
                *square([grad_branch] * GROUP),
                out_w,
                query_r,
                key_r,
                value,
                query,
                key,
                scales,
                gains,
                cosine,
                sine,
            ),
            [SMEM] + [VMEM] * (GROUP + 10),
            scratch_shapes=[pltpu.VMEM(heads_shape, BF16)],
        )
        grads, *parts = run(
            input_back_kernel,
            [shaped((group_tok, 3 * HEADS))] + [shaped((tok, width))] * GROUP,
            (
                *square([stats] * GROUP),
                grad_query,
                grad_key,
                grad_value,
                query,
                key,
                scales,
                w_all,
            ),
            limit=40,
        )
        grad_x = grad_hidden
        for part in square(parts):
            grad_x = grad_x + part.astype(F32)

        def weight_parts(s):
            return core_parts(
                run(
                    functools.partial(weight_back_kernel, nc, s),
                    [shaped((GROUP * rows, 3 * HEADS))] * nc,
                    (pos, x_all, grads),
                    [SMEM, VMEM, VMEM],
                    scratch_shapes=[
                        pltpu.VMEM((group_tok, GROUP * HEAD_DIM), BF16),
                        pltpu.VMEM((GROUP * HEAD_DIM, 3 * HEADS), BF16),
                    ],
                )
            )

        total = 0.0
        for part in ring_parts(weight_parts):
            total = total + part.astype(F32)
        total = total.astype(BF16).reshape(GROUP, rows, 3 * HEADS)
        grad_wq, grad_wk, grad_wv = run(
            spread_kernel,
            [shaped((rows, width), F32)] * 3,
            (pos, *square([total[i] for i in range(GROUP)])),
            [SMEM] + [VMEM] * GROUP,
        )
        picked = run(
            functools.partial(pick_kernel, nc),
            [shaped((rows, width))] * (NZ * nc),
            (pos, tn(attended, branch_all).astype(BF16)),
            [SMEM, VMEM],
        )
        grad_wo = 0.0
        for part in ring_parts(lambda s: core_parts(picked[s * nc : (s + 1) * nc])):
            grad_wo = grad_wo + part.astype(F32)

        wide_gains = run(
            gain_split_kernel,
            [shaped((NZ, 8, HEAD_DIM), F32)] * GROUP,
            (pos, grad_gain_attn, grad_gain_mlp),
            [SMEM, VMEM, VMEM],
        )
        gain_parts = run(
            gain_sum_kernel,
            [shaped((8, HEAD_DIM), F32)] * NZ,
            (pos, *square(wide_gains), head_gains),
            [SMEM] + [VMEM] * (GROUP + 1),
        )
        gain_sums = gain_parts[0]
        for s in range(1, NZ):
            gain_sums = gain_sums + send(gain_parts[s], z=s)
        total_gains = gain_sums
        for k in range(1, nc):
            total_gains = total_gains + send(gain_sums, c=k)
        total_gains = lax.dynamic_slice_in_dim(total_gains, c * rows, rows, 1)

        return (
            output[None],
            grad_x.astype(BF16)[None],
            grad_wq,
            grad_wk,
            grad_wv,
            grad_wo,
            total_gains[0],
            total_gains[1],
            total_gains[2],
            total_gains[3],
            grad_wg,
            grad_wu,
            grad_wd,
        )

    return body


def solution(mesh):
    return jax.shard_map(
        make_body(mesh.shape["wide"]),
        mesh=mesh,
        in_specs=(
            P("wide", "blk", None),
            P("wide"),
            P(("blk", "wide"), None),
            P(("blk", "wide"), None),
            P(("blk", "wide"), None),
            P(("blk", "wide"), None),
            P(("blk", "wide")),
            P(("blk", "wide")),
            P(("blk", "wide")),
            P(("blk", "wide")),
            P("blk", "wide"),
            P("blk", "wide"),
            P("blk", "wide"),
            P("wide", "blk", None),
        ),
        out_specs=(
            P("wide", "blk", None),
            P("wide", "blk", None),
            P(("blk", "wide"), None),
            P(("blk", "wide"), None),
            P(("blk", "wide"), None),
            P(("blk", "wide"), None),
            P(("blk", "wide")),
            P(("blk", "wide")),
            P(("blk", "wide")),
            P(("blk", "wide")),
            P("blk", "wide"),
            P("blk", "wide"),
            P("blk", "wide"),
        ),
        check_vma=False,
    )
```

```python
import functools
import math

import jax
import jax.numpy as jnp
from jax import lax
from jax.experimental import pallas as pl
from jax.experimental.pallas import tpu as pltpu
from jax.sharding import PartitionSpec as P

HEAD_DIM = 128
EPSILON = 1e-06
NEGATIVE = -1e30
BF16 = jnp.bfloat16
F32 = jnp.float32
AXES = ("blk", "wide")
NX, NY, NZ = 2, 2, 4
GROUP = NX * NY
HEADS = NZ * HEAD_DIM
MIB = 1 << 20
SMEM = pl.BlockSpec(memory_space=pltpu.SMEM)
VMEM = pl.BlockSpec(memory_space=pltpu.VMEM)
HBM = pl.BlockSpec(memory_space=pltpu.HBM)
EXTRA = 16
SQUARE = [(dx, dy) for dx in range(NX) for dy in range(NY)]
TOKEN_BLOCKS = [(dx, dy) for dy in range(NY) for dx in range(NX)]


def shaped(shape, dtype=BF16):
    return jax.ShapeDtypeStruct(tuple(shape), dtype)


def nn(left, right):
    return lax.dot_general(left, right, (((1,), (0,)), ((), ())), preferred_element_type=F32)


def nt(left, right):
    return lax.dot_general(left, right, (((1,), (1,)), ((), ())), preferred_element_type=F32)


def tn(left, right):
    return lax.dot_general(left, right, (((0,), (0,)), ((), ())), preferred_element_type=F32)


def auto(array):
    return pl.BlockSpec(array.shape, lambda i: (0,) * len(array.shape))


def run(body, outs, ins, limit=12, **options):
    return pl.pallas_call(
        body,
        grid=(1,),
        out_shape=[out for out, _ in outs],
        out_specs=[spec if isinstance(spec, pl.BlockSpec) else spec(out) for out, spec in outs],
        in_specs=[spec if isinstance(spec, pl.BlockSpec) else spec(array) for array, spec in ins],
        compiler_params=pltpu.CompilerParams(vmem_limit_bytes=limit * MIB),
        **options,
    )(*[array for array, _ in ins])


def each(arrays, spec):
    return [(array, spec) for array in arrays]


def after(value, *others):
    return lax.optimization_barrier((value, others))[0]


class Copies:
    def __init__(self, sems):
        self.sems, self.count = sems, 0

    def start(self, source, target):
        copy = pltpu.make_async_copy(source, target, self.sems.at[self.count])
        self.count += 1
        copy.start()
        return copy


def finish(copies):
    for copy in copies:
        copy.wait()


def place(pos):
    return pos[0], pos[1], pos[2], pos[3]


def gray(index):
    return index ^ (index >> 1)


def ring(r, s):
    return gray((r + s) % NZ)


def column_of(x, z, y):
    return pl.multiple_of(((x * NZ + z) * NY + y) * HEAD_DIM, HEAD_DIM)


def extra_rows(blocks):
    used = sum(block.shape[0] for block in blocks)
    if used < EXTRA:
        blocks = [*blocks, jnp.zeros((EXTRA - used, HEAD_DIM), F32)]
    return jnp.concatenate(blocks, axis=0)


def put_extra(out, start, values):
    out[start : start + EXTRA, :HEAD_DIM] = values.astype(BF16)
    out[start : start + EXTRA, HEAD_DIM:] = jnp.zeros((EXTRA, out.shape[1] - HEAD_DIM), BF16)


def split_kernel(pos, gains, w_query, w_key, w_value, *outs):
    x, _, y, _ = place(pos)
    rows = w_query.shape[0]
    own = gains[...].astype(F32)
    own = jnp.concatenate([own, jnp.zeros((4, HEAD_DIM - rows), F32)], axis=1)
    length = jnp.full((1, HEAD_DIM), pos[4]).astype(F32)
    for (dx, dy), out in zip(SQUARE, outs):
        for i, weight in enumerate((w_query, w_key, w_value)):
            for head in range(NZ):
                start = column_of(x ^ dx, head, y ^ dy)
                at = i * HEADS + head * HEAD_DIM
                out[:rows, at : at + HEAD_DIM] = weight[:, pl.ds(start, HEAD_DIM)]
        put_extra(out, rows, extra_rows([own, length]))


def join_kernel(*refs):
    *parts, out, lengths = refs
    rows = parts[0].shape[0] - EXTRA
    extras = []
    for i, part in enumerate(parts):
        out[i * rows : (i + 1) * rows] = part[:rows]
        extras.append(part[rows:, :HEAD_DIM].astype(F32))
    put_extra(out, GROUP * rows, extra_rows([extra[:4] for extra in extras]))
    lengths[...] = jnp.concatenate(
        [extras[0][4:5], extras[1][4:5], jnp.zeros((6, HEAD_DIM), F32)], axis=0
    )


def row_stats(first, second):
    shape = (first.shape[0], HEAD_DIM)
    upper = lax.broadcasted_iota(jnp.int32, shape, 1) < 4
    sums = jnp.where(
        upper,
        jnp.sum(first, axis=1, keepdims=True),
        jnp.sum(second, axis=1, keepdims=True),
    )
    return jnp.transpose(sums)[:8]


def group_total(stats, tok):
    blocks = []
    for dx, dy in TOKEN_BLOCKS:
        total = 0.0
        for (sx, sy), ref in zip(SQUARE, stats):
            at = ((dy ^ sy) * NX + (dx ^ sx)) * tok
            total = total + ref[:, at : at + tok]
        blocks.append(total)
    return jnp.concatenate(blocks, axis=1)


def gather_kernel(*refs):
    blocks, (whole, kept, sem) = refs[:GROUP], refs[GROUP:]
    tok = blocks[0].shape[0]
    for i, block in enumerate(TOKEN_BLOCKS):
        whole[i * tok : (i + 1) * tok] = blocks[SQUARE.index(block)][...]
    copy = pltpu.make_async_copy(whole, kept, sem)
    copy.start()
    copy.wait()


def out_rows_kernel(nc, pos, *refs):
    *parts, out_w, kept, sem = refs
    _, r, _, c = place(pos)
    rows = parts[0].shape[0]
    for s in range(NZ):
        for k in range(nc):
            start = ring(r, s) * HEAD_DIM + (c ^ k) * rows
            out_w[pl.ds(pl.multiple_of(start, rows), rows)] = parts[s * nc + k][...]
    copy = pltpu.make_async_copy(out_w, kept, sem)
    copy.start()
    copy.wait()


def project_kernel(nc, s, pos, x_all, *refs):
    weights, refs = refs[:nc], refs[nc:]
    if s > 0:
        refs = refs[2:] if s < NZ - 1 else (refs[0], *refs[2:])
    x, r, y, c = place(pos)
    rows = (weights[0].shape[0] - EXTRA) // GROUP
    if s < NZ - 1:
        total, gains, w_rows, columns, w_part, sems = refs
    else:
        before, gains, w_rows, query, key, value, query_h, key_h, value_h, stats, *refs = refs
        total, columns, w_part, sems = refs
    z = ring(r, s)
    extras = [weight[GROUP * rows :, :HEAD_DIM].astype(F32) for weight in weights]
    lanes = []
    for place_c in range(nc):
        chosen = 0.0
        for k, part in enumerate(extras):
            chosen = chosen + jnp.where((c ^ k) == place_c, part[:, :rows], 0.0)
        lanes.append(chosen)
    ordered = jnp.concatenate(lanes, axis=1)
    for i, (dx, dy) in enumerate(SQUARE):
        start = column_of(x ^ dx, z, y ^ dy)
        gains[:, pl.ds(start, HEAD_DIM)] = jnp.concatenate(
            [ordered[4 * i : 4 * i + 4], jnp.zeros((4, HEAD_DIM), F32)], axis=0
        )
        columns[:, i * HEAD_DIM : (i + 1) * HEAD_DIM] = x_all[:, pl.ds(start, HEAD_DIM)]
        for k, weight in enumerate(weights):
            at = pl.multiple_of(i * HEAD_DIM + (c ^ k) * rows, rows)
            w_part[pl.ds(at, rows)] = weight[i * rows : (i + 1) * rows]
    copies = Copies(sems)
    put = [copies.start(w_part, w_rows)]
    step = HEADS // 2
    for part in range(6):
        at = slice(part * step, (part + 1) * step)
        result = nn(columns[...], w_part[:, at])
        if s == 0:
            total[:, at] = result
        elif s < NZ - 1:
            total[:, at] += result
        else:
            result = before[:, at] + result
            out = (query, key, value)[part // 2]
            out[:, (part % 2) * step : (part % 2 + 1) * step] = result.astype(out.dtype)
    if s == NZ - 1:
        stats[...] = row_stats(query[...] * query[...], key[...] * key[...])
        put += [
            copies.start(*pair)
            for pair in ((query, query_h), (key, key_h), (value, value_h))
        ]
    finish(put)


def turn(values, cosine, sine):
    return values * cosine + pltpu.roll(values, HEAD_DIM // 2, 1) * sine


def valid_keys(x, length, tok):
    shape = (NX * tok, NX * tok)
    queries = lax.broadcasted_iota(jnp.int32, shape, 0)
    keys = lax.broadcasted_iota(jnp.int32, shape, 1)

    def at(index):
        return jnp.where(index < tok, x * tok + index, (1 - x) * tok + index - tok)

    return (at(keys) <= at(queries)) & (at(keys).astype(F32) < length)


def softmax(query, key, valid):
    logits = jnp.where(valid, nt(query, key) * HEAD_DIM ** (-0.5), NEGATIVE)
    powers = jnp.exp(logits - jnp.max(logits, axis=1, keepdims=True))
    return powers / jnp.sum(powers, axis=1, keepdims=True)


def attend_kernel(pos, *refs):
    x, _, y, _ = place(pos)
    stats, refs = refs[:GROUP], refs[GROUP:]
    lengths, gains, cosine, sine, query, key, value, out_w, *refs = refs
    query_out, key_out, attended_out, scales, *refs = refs
    pieces, refs = refs[:GROUP], refs[GROUP:]
    query_r, key_r, attended, sems = refs
    copies = Copies(sems)
    tok = query.shape[0] // GROUP
    span = NX * tok
    width = out_w.shape[1]
    scale = lax.rsqrt(group_total(stats, tok) / width + EPSILON)
    scales[...] = scale
    for seq in range(NY):
        at = slice(seq * span, (seq + 1) * span)
        columns = jnp.transpose(scale[:, at])
        valid = valid_keys(x, lengths[seq : seq + 1, 0:1], tok)
        for head in range(NZ):
            lanes = slice(head * HEAD_DIM, (head + 1) * HEAD_DIM)
            gain = pl.ds(column_of(x, head, y), HEAD_DIM)
            for row, (raw, out) in enumerate(((query, query_r), (key, key_r))):
                normed = raw[at, lanes] * columns[:, 4 * row : 4 * row + 1]
                normed = normed * gains[row : row + 1, gain]
                out[at, lanes] = turn(normed, cosine[...], sine[...]).astype(BF16)
            chances = softmax(query_r[at, lanes], key_r[at, lanes], valid)
            attended[at, lanes] = nn(chances.astype(BF16), value[at, lanes]).astype(BF16)
    put = [
        copies.start(*pair)
        for pair in ((query_r, query_out), (key_r, key_out), (attended, attended_out))
    ]
    step = width // 4
    for part in range(4):
        columns = slice(part * step, (part + 1) * step)
        result = nn(attended[...], out_w[:, columns])
        for i, block in enumerate(TOKEN_BLOCKS):
            out = pieces[SQUARE.index(block)]
            out[:, columns] = result[i * tok : (i + 1) * tok].astype(out.dtype)
    finish(put)


def in_halves(values, x, out):
    half = out.shape[1] // NX
    for dx in range(NX):
        start = pl.multiple_of((x ^ dx) * half, half)
        out[:, dx * half : (dx + 1) * half] = values[:, pl.ds(start, half)].astype(out.dtype)


def sum_of(refs):
    total = refs[0][...].astype(F32)
    for ref in refs[1:]:
        total = total + ref[...].astype(F32)
    return total


def branch_kernel(pos, *refs):
    parts, refs = refs[:GROUP], refs[GROUP:]
    inputs, gains, branch_out, hidden_out, mlp_in = refs
    branch = sum_of(parts)
    branch_out[...] = branch
    scale = lax.rsqrt(jnp.mean(branch * branch, axis=1, keepdims=True) + EPSILON)
    hidden_out[...] = inputs[...].astype(F32) + branch * scale * gains[2:3, :]
    in_halves(hidden_out, pos[0], mlp_in)


def norm_back(values, gain, grad):
    scale = lax.rsqrt(jnp.mean(values * values, axis=1, keepdims=True) + EPSILON)
    normed = values * scale
    scaled = grad * gain
    mean = jnp.mean(scaled * normed, axis=1, keepdims=True)
    return scale * (scaled - normed * mean), jnp.sum(grad * normed, axis=0, keepdims=True)


def mlp_kernel(count, pos, *refs):
    parts, refs = refs[:count], refs[count:]
    hidden, gains, grad_output, output, grad_in, grad_gain, halves, mlp_out = refs
    halves[...] = sum_of(parts)
    in_halves(halves, pos[0], mlp_out)
    values = mlp_out[...]
    gain = gains[3:4, :]
    scale = lax.rsqrt(jnp.mean(values * values, axis=1, keepdims=True) + EPSILON)
    output[...] = (hidden[...] + values * scale * gain).astype(BF16)
    grad, by_gain = norm_back(values, gain, grad_output[...].astype(F32))
    halves[...] = grad
    in_halves(halves, pos[0], grad_in)
    grad_gain[...] = jnp.broadcast_to(by_gain, grad_gain.shape)


def branch_back_kernel(count, pos, *refs):
    parts, refs = refs[:count], refs[count:]
    branch, gains, grad_output, grad_hidden, grad_branch, grad_gain, halves, middle = refs
    halves[...] = sum_of(parts)
    in_halves(halves, pos[0], middle)
    total = grad_output[...].astype(F32) + middle[...]
    grad_hidden[...] = total
    grad, by_gain = norm_back(branch[...], gains[2:3, :], total)
    grad_branch[...] = grad.astype(BF16)
    grad_gain[...] = jnp.broadcast_to(by_gain, grad_gain.shape)


def out_back_kernel(nc, pos, *refs):
    blocks, refs = refs[:GROUP], refs[GROUP:]
    attended, branch_all, *outs, sums = refs
    _, r, _, c = place(pos)
    tok = blocks[0].shape[0]
    rows = outs[0].shape[0] // NZ
    for i, block in enumerate(TOKEN_BLOCKS):
        branch_all[i * tok : (i + 1) * tok] = blocks[SQUARE.index(block)][...]
    for s in range(NZ):
        start = pl.multiple_of(ring(r, s) * HEAD_DIM, HEAD_DIM)
        sums[...] = tn(attended[:, pl.ds(start, HEAD_DIM)], branch_all[...]).astype(BF16)
        for k in range(nc):
            at = pl.ds(pl.multiple_of((c ^ k) * rows, rows), rows)
            outs[k][s * rows : (s + 1) * rows] = sums[at, :]


def attend_back_kernel(pos, *refs):
    lengths, scales, gains, cosine, sine, branch_all, out_w, *refs = refs
    held, refs = refs[:5], refs[5:]
    query_out, key_out, grad_value, stats, head_gains, *refs = refs
    query_r, key_r, value, query, key, *refs = refs
    grad_query, grad_key, grad_att, sems = refs
    x, _, y, _ = place(pos)
    tok = branch_all.shape[0] // GROUP
    span = NX * tok
    copies = Copies(sems)
    later = [
        copies.start(*pair) for pair in zip(held, (query_r, key_r, value, query, key))
    ]
    for half in range(2):
        lanes = slice(half * (HEADS // 2), (half + 1) * (HEADS // 2))
        grad_att[:, lanes] = nt(branch_all[...], out_w[lanes, :]).astype(BF16)
    head_gains[...] = jnp.zeros_like(head_gains)
    finish(later)
    for seq in range(NY):
        at = slice(seq * span, (seq + 1) * span)
        columns = jnp.transpose(scales[:, at])
        valid = valid_keys(x, lengths[seq : seq + 1, 0:1], tok)
        for head in range(NZ):
            lanes = slice(head * HEAD_DIM, (head + 1) * HEAD_DIM)
            gain = pl.ds(column_of(x, head, y), HEAD_DIM)
            queries, keys, values = query_r[at, lanes], key_r[at, lanes], value[at, lanes]
            chances = softmax(queries, keys, valid)
            incoming = grad_att[at, lanes]
            grad_chances = nt(incoming, values)
            grad_value[at, lanes] = tn(chances.astype(BF16), incoming).astype(BF16)
            balance = jnp.sum(chances * grad_chances, axis=1, keepdims=True)
            grad_logits = (chances * (grad_chances - balance)).astype(BF16)
            by_query = nn(grad_logits, keys) * HEAD_DIM ** (-0.5)
            by_key = tn(grad_logits, queries) * HEAD_DIM ** (-0.5)
            for row, (grad, raw, out) in enumerate(
                ((by_query, query, grad_query), (by_key, key, grad_key))
            ):
                back = turn(grad.astype(BF16).astype(F32), cosine[...], -sine[...])
                normed = raw[at, lanes] * columns[:, 4 * row : 4 * row + 1]
                head_gains[row : row + 1, lanes] += jnp.sum(back * normed, axis=0, keepdims=True)
                out[at, lanes] = back * gains[row : row + 1, gain]
    query_out[...] = grad_query[...]
    key_out[...] = grad_key[...]
    stats[...] = row_stats(grad_query[...] * query[...], grad_key[...] * key[...])


def project_back_kernel(*refs):
    stats, refs = refs[:GROUP], refs[GROUP:]
    scales, grad_query, grad_key, grad_value, query, key, grads = refs
    tok = query.shape[0] // GROUP
    width = NX * NY * HEADS
    means = jnp.transpose(group_total(stats, tok) / width)
    columns = jnp.transpose(scales[...])
    for row, (grad, raw) in enumerate(((grad_query, query), (grad_key, key))):
        scale = columns[:, 4 * row : 4 * row + 1]
        mean = means[:, 4 * row : 4 * row + 1]
        result = scale * (grad[...] - raw[...] * (scale * scale * mean))
        grads[:, row * HEADS : (row + 1) * HEADS] = result.astype(BF16)
    grads[:, 2 * HEADS :] = grad_value[...]


def input_back_kernel(pos, grads, *refs):
    weights, refs = refs[:NZ], refs[NZ:]
    *pieces, results = refs
    x, r, y, _ = place(pos)
    tok = grads.shape[0] // GROUP
    for s, weight in enumerate(weights):
        for half in range(2):
            result = nt(grads[...], weight[half * HEADS // 2 : (half + 1) * HEADS // 2, :])
            results[:, half * HEADS // 2 : (half + 1) * HEADS // 2] = result.astype(BF16)
        for j, (dx, dy) in enumerate(SQUARE):
            start = column_of(x ^ dx, ring(r, s), y ^ dy)
            for i, block in enumerate(TOKEN_BLOCKS):
                out = pieces[SQUARE.index(block)]
                out[:, pl.ds(start, HEAD_DIM)] = results[
                    i * tok : (i + 1) * tok, j * HEAD_DIM : (j + 1) * HEAD_DIM
                ]


def weight_back_kernel(nc, places, pos, *refs):
    for i, s in enumerate(places):
        weight_back_part(nc, s, i, pos, *refs)


def weight_back_part(nc, s, slot, pos, x_all, grads, attn_gain, mlp_gain, head_gains, *refs):
    *outs, columns, sums = refs
    x, r, y, c = place(pos)
    rows = HEAD_DIM // nc
    base = slot * (GROUP * rows + EXTRA)
    z = ring(r, s)
    gains = []
    for i, (dx, dy) in enumerate(SQUARE):
        start = column_of(x ^ dx, z, y ^ dy)
        columns[:, i * HEAD_DIM : (i + 1) * HEAD_DIM] = x_all[:, pl.ds(start, HEAD_DIM)]
        if i == 0:
            heads = pl.ds(pl.multiple_of(z * HEAD_DIM, HEAD_DIM), HEAD_DIM)
            gains.append(head_gains[0:2, heads])
        else:
            gains.append(jnp.zeros((2, HEAD_DIM), F32))
        gains.append(attn_gain[0:1, pl.ds(start, HEAD_DIM)])
        gains.append(mlp_gain[0:1, pl.ds(start, HEAD_DIM)])
    gains = jnp.concatenate(gains, axis=0)
    step = grads.shape[1] // 3
    for part in range(3):
        lanes = slice(part * step, (part + 1) * step)
        sums[:, lanes] = tn(columns[...], grads[:, lanes]).astype(BF16)
    for k, out in enumerate(outs):
        for i in range(GROUP):
            start = pl.multiple_of(i * HEAD_DIM + (c ^ k) * rows, rows)
            out[base + i * rows : base + (i + 1) * rows] = sums[pl.ds(start, rows), :]
        chosen = 0.0
        for place_c in range(nc):
            part = gains[:, place_c * rows : (place_c + 1) * rows]
            chosen = chosen + jnp.where((c ^ k) == place_c, part, 0.0)
        chosen = jnp.concatenate([chosen, jnp.zeros((EXTRA, HEAD_DIM - rows), F32)], axis=1)
        put_extra(out, base + GROUP * rows, chosen)


def collect_kernel(count, *refs):
    parts, outs = refs[:count], refs[count:]
    rows = (parts[0].shape[0] - EXTRA) // GROUP

    def total(at, lanes=slice(None)):
        result = parts[0][at, lanes].astype(F32)
        for part in parts[1:]:
            result = result + part[at, lanes].astype(F32)
        return result

    extra = total(slice(GROUP * rows, GROUP * rows + EXTRA), slice(0, HEAD_DIM))
    for i, out in enumerate(outs):
        out[:rows] = total(slice(i * rows, (i + 1) * rows)).astype(BF16)
        put_extra(out, rows, extra_rows([extra[4 * i : 4 * i + 4]]))


def spread_kernel(pos, *refs):
    parts, (*outs, gains) = refs[:GROUP], refs[GROUP:]
    x, _, y, _ = place(pos)
    rows = parts[0].shape[0] - EXTRA
    total = 0.0
    for (dx, dy), part in zip(SQUARE, parts):
        total = total + part[rows:, :HEAD_DIM].astype(F32)
        for i, out in enumerate(outs):
            for head in range(NZ):
                start = column_of(x ^ dx, head, y ^ dy)
                at = i * HEADS + head * HEAD_DIM
                out[:, pl.ds(start, HEAD_DIM)] = part[:rows, at : at + HEAD_DIM].astype(F32)
    gains[...] = total[:8]


def mlp_forward_kernel(nc, *refs):
    blocks, refs = refs[:nc], refs[nc:]
    gates, ups, downs, refs = refs[:4], refs[4:8], refs[8:16], refs[16:]
    outs = refs[-(8 + nc + 1) :]
    products, by_gate, by_up, kept = outs[0:2], outs[2:4], outs[4:6], outs[6:8]
    sums, total = outs[8 : 8 + nc], outs[8 + nc]
    tok = blocks[0].shape[0]
    half = kept[0].shape[1]
    quarter = half // 2
    for k, block in enumerate(blocks):
        for dx in range(NX):
            kept[dx][k * tok : (k + 1) * tok] = block[:, dx * half : (dx + 1) * half]
    for dy in range(NY):

        def through(weights):
            return nn(kept[0][...], weights[dy][...]) + nn(kept[1][...], weights[NY + dy][...])

        gate, up = through(gates), through(ups)
        chance = 1.0 / (1.0 + jnp.exp(-gate))
        silu = gate * chance
        product = (silu * up).astype(BF16)
        products[dy][...] = product
        by_up[dy][...] = silu.astype(BF16)
        by_gate[dy][...] = (up * (chance + silu * (1.0 - chance))).astype(BF16)
        for i in range(4):
            lanes = slice(i * quarter, (i + 1) * quarter)
            part = nt(product, downs[i * NY + dy][...])
            if dy == 0:
                total[:, lanes] = part
            else:
                part = total[:, lanes] + part
                for k, out in enumerate(sums):
                    out[:, lanes] = part[k * tok : (k + 1) * tok].astype(out.dtype)


def mlp_back_kernel(nc, *refs):
    blocks, refs = refs[:nc], refs[nc:]
    gates, ups, downs, refs = refs[:4], refs[4:8], refs[8:16], refs[16:]
    by_gate, by_up = refs[0:2], refs[2:4]
    outs = refs[-(8 + nc + 1) :]
    grad_gates, grad_ups, kept = outs[0:2], outs[2:4], outs[4:8]
    sums, total = outs[8 : 8 + nc], outs[8 + nc]
    tok = blocks[0].shape[0]
    quarter = kept[0].shape[1]
    for k, block in enumerate(blocks):
        for i in range(4):
            kept[i][k * tok : (k + 1) * tok] = block[:, i * quarter : (i + 1) * quarter]
    for dy in range(NY):
        grad = nn(kept[0][...], downs[dy][...])
        for i in range(1, 4):
            grad = grad + nn(kept[i][...], downs[i * NY + dy][...])
        grad_gate = (grad * by_gate[dy][...].astype(F32)).astype(BF16)
        grad_up = (grad * by_up[dy][...].astype(F32)).astype(BF16)
        grad_gates[dy][...] = grad_gate
        grad_ups[dy][...] = grad_up
        for i in range(4):
            lanes = slice(i * quarter, (i + 1) * quarter)
            dx, rows = i // 2, slice((i % 2) * quarter, (i % 2 + 1) * quarter)
            part = nt(grad_gate, gates[dx * NY + dy][rows, :]) + nt(
                grad_up, ups[dx * NY + dy][rows, :]
            )
            if dy == 0:
                total[:, lanes] = part
            else:
                part = total[:, lanes] + part
                for k, out in enumerate(sums):
                    out[:, lanes] = part[k * tok : (k + 1) * tok].astype(out.dtype)


def make_body(wide):
    nc = wide // (NY * NZ)

    def send(value, x=0, y=0, r=0, c=0):
        pairs = []
        for sx in range(NX):
            for sz in range(NZ):
                for sy in range(NY):
                    for sc in range(nc):
                        source = sx * wide + (sz * NY + sy) * nc + sc
                        target = (sx ^ x) * wide
                        target += (ring(gray(sz), r) * NY + (sy ^ y)) * nc + (sc ^ c)
                        pairs.append((source, target))
        return lax.ppermute(value, AXES, pairs)

    def square(parts):
        return [
            part if (dx, dy) == (0, 0) else send(part, x=dx, y=dy)
            for (dx, dy), part in zip(SQUARE, parts)
        ]

    def square_gather(first, second):
        first_x = send(first, x=1)
        second_y = send(second, y=1)
        first_y = send(first, y=1)
        second_x = send(second, x=1)
        first_xy = send(first_x, y=1)
        second_xy = send(second_y, x=1)
        return [first, first_y, first_x, first_xy], [second, second_y, second_x, second_xy]

    def scatter_far(first, second):
        return send(first[3], x=1), send(second[3], y=1)

    def scatter_near(first, second):
        return send(first[2], x=1), send(second[1], y=1)

    def scatter_rest(first, second, far, near):
        first_c = send((first[1].astype(F32) + far[0].astype(F32)).astype(BF16), y=1)
        second_c = send((second[2].astype(F32) + far[1].astype(F32)).astype(BF16), x=1)
        return (
            first[0].astype(F32) + near[0].astype(F32) + first_c.astype(F32),
            second[0].astype(F32) + near[1].astype(F32) + second_c.astype(F32),
        )

    def ring_gather(block):
        blocks = [block]
        for _ in range(NZ - 1):
            blocks.append(send(blocks[-1], r=-1))
        return blocks

    def core_gather(block):
        return [block] + [send(block, c=k) for k in range(1, nc)]

    def core_parts(parts):
        return [parts[0]] + [send(parts[k], c=k) for k in range(1, nc)]

    def ring_parts(part_of, hold=None):
        moving, sent = [], []
        for s in list(range(1, NZ)) + [0]:
            parts = part_of(s)
            if moving and hold is not None:
                moving = [after(moving[0], hold(s))]
            parts = parts + moving
            if s == 0:
                return parts, sent
            total = parts[0].astype(F32)
            for part in parts[1:]:
                total = total + part.astype(F32)
            sent.append(total.astype(BF16))
            moving = [send(sent[-1], r=-1)]

    def body(
        layer_input,
        lengths,
        w_query,
        w_key,
        w_value,
        w_output,
        query_gain,
        key_gain,
        attn_gain,
        mlp_gain,
        w_gate,
        w_up,
        w_down,
        grad_output,
    ):
        x = lax.axis_index("blk")
        spot = lax.axis_index("wide")
        z, y, c = spot // (NY * nc), (spot // nc) % NY, spot % nc
        inputs, grad_out = layer_input[0], grad_output[0]
        tok, width = inputs.shape
        rows = w_query.shape[0]
        group_tok = GROUP * tok
        hidden = w_gate.shape[1]
        pos = jnp.stack([x, gray(z), y, c, lengths[0]]).astype(jnp.int32)
        wide_small = shaped((8, width), F32)
        by_head = shaped((group_tok, HEADS))
        by_head_wide = shaped((group_tok, HEADS), F32)
        by_token = shaped((8, group_tok), F32)
        tokens_shape = shaped((tok, width))
        tokens_wide = shaped((tok, width), F32)
        message = shaped((GROUP * rows + EXTRA, 3 * HEADS))
        piece = shaped((rows + EXTRA, 3 * HEADS))

        def dma(count):
            return pltpu.SemaphoreType.DMA((count,))

        def held(shape):
            return pltpu.VMEM(shape.shape, shape.dtype)

        gains = jnp.stack([query_gain, key_gain, attn_gain, mlp_gain])
        pieces = run(
            split_kernel,
            each([piece] * GROUP, VMEM),
            [(pos, SMEM), (gains, VMEM), (w_query, auto), (w_key, auto), (w_value, auto)],
        )
        out_ring = [w_output, send(after(w_output, pieces), r=-1)]
        down_rows = w_down.shape[0] // 2
        down_halves = after(w_down, pieces)
        down_halves = down_halves[:down_rows], down_halves[down_rows:]
        far_down = send(down_halves[0], x=1), send(down_halves[1], y=1)
        received = square(pieces)
        own_rows, lengths_row = run(
            join_kernel,
            [(message, VMEM), (shaped((8, HEAD_DIM), F32), VMEM)],
            each(received, VMEM),
        )
        half = HEAD_DIM // 2
        order = jnp.concatenate([x * tok + jnp.arange(tok), (1 - x) * tok + jnp.arange(tok)])
        frequency = jnp.exp(
            jnp.arange(half, dtype=F32) * (-2.0 * math.log(500000.0) / HEAD_DIM)
        )
        angles = order.astype(F32)[:, None] * frequency[None, :]
        cosine = jnp.tile(jnp.cos(angles), (1, 2))
        sine = jnp.sin(angles)
        sine = jnp.concatenate([-sine, sine], axis=1)
        tokens = square([after(inputs, own_rows)] * GROUP)
        w_ring = [own_rows, send(own_rows, r=-1)]
        out_ring.append(send(out_ring[1], r=-1))
        ready = cosine, sine, far_down, out_ring[2], tokens[1], tokens[2]
        w_ring.append(send(after(w_ring[1], ready), r=-1))
        x_all, x_kept = run(
            gather_kernel,
            [(shaped((group_tok, width)), VMEM), (shaped((group_tok, width)), HBM)],
            each(tokens, VMEM),
            scratch_shapes=[pltpu.SemaphoreType.DMA],
        )
        far_gate = send(after(w_gate, x_all), x=1)
        far_up = send(after(w_up, x_all), y=1)
        near_gate = send(after(w_gate, far_gate), y=1)
        near_up = send(after(w_up, far_up), x=1)
        total, gains = None, None
        totals = []
        w_parts = []
        w_shape = shaped((GROUP * HEAD_DIM, 3 * HEADS))
        for s in range(NZ):
            if s == NZ - 1:
                w_ring.append(send(after(w_ring[2], totals[1]), r=-1))
                out_ring.append(send(after(out_ring[2], w_ring[3]), r=-1))
            blocks = core_gather(w_ring[s])
            ins = [(pos, SMEM), (x_all, VMEM), *each(blocks, VMEM)]
            outs = [(wide_small, VMEM), (w_shape, HBM)]
            aliases = {}
            if s > 0:
                if s == NZ - 1:
                    total, gains = after((total, gains), far_gate, far_up)
                aliases = {len(ins) + 1: 1 if s < NZ - 1 else 0}
                ins += [(total, VMEM), (gains, VMEM)]
            if s < NZ - 1:
                outs = [(shaped((group_tok, 3 * HEADS), F32), VMEM)] + outs
                if s > 0:
                    aliases[len(ins) - 2] = 0
            else:
                outs += [(by_head_wide, VMEM), (by_head_wide, VMEM), (by_head, VMEM)]
                outs += [(by_head_wide, HBM), (by_head_wide, HBM), (by_head, HBM)]
                outs += [(by_token, VMEM)]
            results = run(
                functools.partial(project_kernel, nc, s),
                outs,
                ins,
                input_output_aliases=aliases,
                scratch_shapes=([pltpu.VMEM((8, HEAD_DIM), F32)] if s == NZ - 1 else [])
                + [
                    pltpu.VMEM((group_tok, GROUP * HEAD_DIM), BF16),
                    pltpu.VMEM((GROUP * HEAD_DIM, 3 * HEADS), BF16),
                    dma(4),
                ],
            )
            if s < NZ - 1:
                total, gains, w_part = results
                totals.append(total)
            else:
                gains, w_part, query, key, value, query_h, key_h, value_h, stats = results
            w_parts.append(w_part)
        out_w, out_kept = run(
            functools.partial(out_rows_kernel, nc),
            [(shaped((HEADS, width)), VMEM), (shaped((HEADS, width)), HBM)],
            [
                (pos, SMEM),
                *each([part for block in out_ring for part in core_gather(block)], VMEM),
            ],
            scratch_shapes=[pltpu.SemaphoreType.DMA],
        )
        group_stats = square([stats] * GROUP)
        last_gate = send(after(far_gate, group_stats), y=1)
        last_up = send(after(far_up, group_stats), x=1)
        gate_w = [w_gate, near_gate, far_gate, last_gate]
        up_w = [w_up, far_up, near_up, last_up]

        query_r, key_r, attended, scales, *parts = run(
            attend_kernel,
            [(by_head, HBM)] * 3 + [(by_token, VMEM)] + [(tokens_shape, VMEM)] * GROUP,
            [
                (pos, SMEM),
                *each(group_stats, VMEM),
                *each((lengths_row, gains, cosine, sine), VMEM),
                *each((query, key, value, out_w), VMEM),
            ],
            scratch_shapes=[held(by_head), held(by_head), held(by_head), dma(3)],
        )
        parts = square(after(parts, gate_w, up_w))
        first, second = after(down_halves, parts)
        first_x, second_y = after(far_down, parts)
        down_first = first, send(first, y=1), first_x, send(first_x, y=1)
        down_second = second, second_y, send(second, x=1), send(second_y, x=1)
        down_w = [
            half[dx * NY + dy]
            for dx in range(NX)
            for half in (down_first, down_second)
            for dy in range(NY)
        ]
        branch, hidden_state, mlp_in = run(
            branch_kernel,
            [(tokens_wide, auto), (tokens_wide, auto), (tokens_shape, VMEM)],
            [(pos, SMEM), *each(parts, auto), (inputs, auto), (gains, VMEM)],
        )

        half_width = width // NX
        quarter = half_width // 2
        m = nc * tok

        def mlp_call(kernel, s, block, extra, kept_columns, before):
            def rows_of(array):
                return pl.BlockSpec((m, array.shape[1]), lambda i: (s, 0))

            ins = each(core_gather(block), auto)
            ins += each((*gate_w, *up_w, *down_w), VMEM) + each(extra, rows_of)
            columns = [hidden] * (8 - len(kept_columns)) + list(kept_columns)
            outs = each([shaped((NZ * m, count)) for count in columns], rows_of)
            outs += [(tokens_wide, VMEM)] + [(tokens_shape, VMEM)] * (nc - 1)
            aliases = {}
            if before is not None:
                aliases = {len(ins) + i: i for i in range(8)}
                ins += each(before, HBM)
            results = run(
                functools.partial(kernel, nc),
                outs,
                ins,
                limit=20 if nc == 2 else 56,
                input_output_aliases=aliases,
                scratch_shapes=[pltpu.VMEM((m, width), F32)],
            )
            return results[:8], core_parts(results[8:])

        kept = None
        sums = []
        for s, block in enumerate(ring_gather(mlp_in)):
            kept, parts = mlp_call(
                mlp_forward_kernel, s, block, (), (half_width, half_width), kept
            )
            sums.append(parts)

        def hold(s):
            return sums[(s + 1) % NZ][0]

        products, by_gate, by_up, mlp_all = kept[0:2], kept[2:4], kept[4:6], kept[6:8]
        parts, _ = ring_parts(lambda s: sums[s], hold)
        output, grad_mlp, grad_gain_mlp = run(
            functools.partial(mlp_kernel, len(parts)),
            [(tokens_shape, auto), (tokens_shape, VMEM), (wide_small, VMEM)],
            [
                (pos, SMEM),
                *each(parts, auto),
                (hidden_state, auto),
                (gains, VMEM),
                (grad_out, auto),
            ],
            scratch_shapes=[held(tokens_wide)] * 2,
        )
        kept = None
        sums = []
        for s, block in enumerate(ring_gather(grad_mlp)):
            kept, parts = mlp_call(
                mlp_back_kernel, s, block, (*by_gate, *by_up), (quarter,) * 4, kept
            )
            sums.append(parts)
        grad_gates, grad_ups, grad_all = kept[0:2], kept[2:4], kept[4:8]
        parts, sent = ring_parts(lambda s: sums[s], hold)
        grad_hidden, grad_branch, grad_gain_attn = run(
            functools.partial(branch_back_kernel, len(parts)),
            [(tokens_wide, auto), (tokens_shape, VMEM), (wide_small, VMEM)],
            [
                (pos, SMEM),
                *each(parts, auto),
                (branch, auto),
                (gains, VMEM),
                (grad_out, auto),
            ],
            scratch_shapes=[held(tokens_wide)] * 2,
        )

        def products_of(left, right):
            return [tn(left[dx], right[dy]).astype(BF16) for dx, dy in SQUARE]

        grad_all = after(grad_all, sent[1])
        wd_pair = products_of(grad_all[0::2], products), products_of(grad_all[1::2], products)
        wd_far = scatter_far(*wd_pair)
        wd_near = scatter_near(*after(wd_pair, wd_far))
        grad_branch = after(grad_branch, wd_far)
        grad_wd = jnp.concatenate(scatter_rest(*wd_pair, wd_far, wd_near), axis=0)
        mlp_all = after(mlp_all, sent[2])
        grad_wg = products_of(mlp_all, grad_gates)
        grad_wu = products_of(mlp_all, grad_ups)

        blocks = square([grad_branch] * GROUP)
        w_pair = after((grad_wg, grad_wu), blocks)
        w_far = scatter_far(*w_pair)
        branch_all, *picked = run(
            functools.partial(out_back_kernel, nc),
            [(shaped((group_tok, width)), VMEM)] + [(shaped((NZ * rows, width)), VMEM)] * nc,
            [(pos, SMEM), *each(blocks, VMEM), (attended, VMEM)],
            scratch_shapes=[pltpu.VMEM((HEAD_DIM, width), BF16)],
        )
        picked = core_parts(picked)

        def out_part(s):
            return [part[s * rows : (s + 1) * rows] for part in picked]

        def summed(parts):
            total = parts[0].astype(F32)
            for part in parts[1:]:
                total = total + part.astype(F32)
            return total

        out_moving = send(summed(out_part(1)).astype(BF16), r=-1)
        branch_all = after(branch_all, w_pair)
        grad_query, grad_key, grad_value, stats, head_gains = run(
            attend_back_kernel,
            [
                (by_head_wide, VMEM),
                (by_head_wide, VMEM),
                (by_head, VMEM),
                (by_token, VMEM),
                (shaped((8, HEADS), F32), VMEM),
            ],
            [
                (pos, SMEM),
                *each((lengths_row, scales, gains, cosine, sine, branch_all, out_kept), VMEM),
                *each((query_r, key_r, value_h, query_h, key_h), HBM),
            ],
            limit=16,
            scratch_shapes=[
                held(by_head),
                held(by_head),
                held(by_head),
                held(by_head_wide),
                held(by_head_wide),
                held(by_head_wide),
                held(by_head_wide),
                held(by_head),
                dma(5),
            ],
        )
        (grads,) = run(
            project_back_kernel,
            [(shaped((group_tok, 3 * HEADS)), VMEM)],
            [
                *each(square([stats] * GROUP), VMEM),
                (scales, VMEM),
                *each((grad_query, grad_key, grad_value, query_h, key_h), VMEM),
            ],
        )
        grads = after(grads, out_moving)
        w_near = scatter_near(*after(w_pair, grads))

        def weight_parts(places):
            height = message.shape[0]
            results = run(
                functools.partial(weight_back_kernel, nc, places),
                [(shaped((len(places) * height, 3 * HEADS)), VMEM)] * nc,
                [
                    (pos, SMEM),
                    (x_kept, VMEM),
                    *each((grads, grad_gain_attn, grad_gain_mlp, head_gains), VMEM),
                ],
                scratch_shapes=[
                    pltpu.VMEM((group_tok, GROUP * HEAD_DIM), BF16),
                    pltpu.VMEM((GROUP * HEAD_DIM, 3 * HEADS), BF16),
                ],
            )
            results = core_parts(results)
            return [
                [part[i * height : (i + 1) * height] for part in results]
                for i in range(len(places))
            ]

        (first,) = weight_parts((1,))
        out_second = summed(out_part(2) + [out_moving]).astype(BF16)
        w_moving = send(after(summed(first).astype(BF16), w_far, out_second), r=-1)
        out_moving = send(out_second, r=-1)
        second, third, own = weight_parts((2, 3, 0))
        out_third = summed(out_part(3) + [out_moving]).astype(BF16)
        sent = summed(second + [w_moving]).astype(BF16)
        w_moving = send(after(sent, own, out_third, w_near), r=-1)
        out_moving = send(out_third, r=-1)
        grad_wg, grad_wu = scatter_rest(*w_pair, *after((w_far, w_near), sent))
        sent = summed(third + [w_moving]).astype(BF16)
        w_moving = send(sent, r=-1)
        parts = own + [w_moving]
        messages = run(
            functools.partial(collect_kernel, len(parts)),
            [(piece, VMEM)] * GROUP,
            each(parts, auto),
        )
        grad_wq, grad_wk, grad_wv, total_gains = run(
            spread_kernel,
            [(shaped((rows, width), F32), auto)] * 3 + [(shaped((8, HEAD_DIM), F32), VMEM)],
            [(pos, SMEM), *each(square(messages), auto)],
        )
        grad_wo = summed(out_part(0) + [out_moving])

        parts = run(
            input_back_kernel,
            [(tokens_shape, VMEM)] * GROUP,
            [(pos, SMEM), (after(grads, sent), VMEM), *each(w_parts, VMEM)],
            scratch_shapes=[pltpu.VMEM((group_tok, GROUP * HEAD_DIM), BF16)],
        )
        grad_x = summed([grad_hidden, *square(parts)])

        return (
            output[None],
            grad_x.astype(BF16)[None],
            grad_wq,
            grad_wk,
            grad_wv,
            grad_wo,
            total_gains[0, :rows],
            total_gains[1, :rows],
            total_gains[2, :rows],
            total_gains[3, :rows],
            grad_wg,
            grad_wu,
            grad_wd,
        )

    return body


def solution(mesh):
    return jax.shard_map(
        make_body(mesh.shape["wide"]),
        mesh=mesh,
        in_specs=(
            P("wide", "blk", None),
            P("wide"),
            P(("blk", "wide"), None),
            P(("blk", "wide"), None),
            P(("blk", "wide"), None),
            P(("blk", "wide"), None),
            P(("blk", "wide")),
            P(("blk", "wide")),
            P(("blk", "wide")),
            P(("blk", "wide")),
            P("blk", "wide"),
            P("blk", "wide"),
            P("blk", "wide"),
            P("wide", "blk", None),
        ),
        out_specs=(
            P("wide", "blk", None),
            P("wide", "blk", None),
            P(("blk", "wide"), None),
            P(("blk", "wide"), None),
            P(("blk", "wide"), None),
            P(("blk", "wide"), None),
            P(("blk", "wide")),
            P(("blk", "wide")),
            P(("blk", "wide")),
            P(("blk", "wide")),
            P("blk", "wide"),
            P("blk", "wide"),
            P("blk", "wide"),
        ),
        check_vma=False,
    )
```

```python
import functools
import math

import jax
import jax.numpy as jnp
from jax import lax
from jax.experimental import pallas as pl
from jax.experimental.pallas import tpu as pltpu
from jax.sharding import PartitionSpec as P

HEAD_DIM = 128
EPSILON = 1e-06
NEGATIVE = -1e30
BF16 = jnp.bfloat16
F32 = jnp.float32
AXES = ("blk", "wide")
NX, NY, NZ = 2, 2, 4
GROUP = NX * NY
HEADS = NZ * HEAD_DIM
MIB = 1 << 20
SMEM = pl.BlockSpec(memory_space=pltpu.SMEM)
VMEM = pl.BlockSpec(memory_space=pltpu.VMEM)
HBM = pl.BlockSpec(memory_space=pltpu.HBM)
EXTRA = 16
SQUARE = [(dx, dy) for dx in range(NX) for dy in range(NY)]
TOKEN_BLOCKS = [(dx, dy) for dy in range(NY) for dx in range(NX)]


def shaped(shape, dtype=BF16):
    return jax.ShapeDtypeStruct(tuple(shape), dtype)


def nn(left, right):
    return lax.dot_general(left, right, (((1,), (0,)), ((), ())), preferred_element_type=F32)


def nt(left, right):
    return lax.dot_general(left, right, (((1,), (1,)), ((), ())), preferred_element_type=F32)


def tn(left, right):
    return lax.dot_general(left, right, (((0,), (0,)), ((), ())), preferred_element_type=F32)


def auto(array):
    return pl.BlockSpec(array.shape, lambda i: (0,) * len(array.shape))


def run(body, outs, ins, limit=12, **options):
    return pl.pallas_call(
        body,
        grid=(1,),
        out_shape=[
            pltpu.HBM(out.shape, out.dtype) if spec is HBM else out for out, spec in outs
        ],
        out_specs=[spec if isinstance(spec, pl.BlockSpec) else spec(out) for out, spec in outs],
        in_specs=[spec if isinstance(spec, pl.BlockSpec) else spec(array) for array, spec in ins],
        compiler_params=pltpu.CompilerParams(vmem_limit_bytes=limit * MIB),
        **options,
    )(*[array for array, _ in ins])


def each(arrays, spec):
    return [(array, spec) for array in arrays]


def after(value, *others):
    return lax.optimization_barrier((value, others))[0]


class Copies:
    def __init__(self, sems):
        self.sems, self.count = sems, 0

    def start(self, source, target):
        copy = pltpu.make_async_copy(source, target, self.sems.at[self.count])
        self.count += 1
        copy.start()
        return copy


def finish(copies):
    for copy in copies:
        copy.wait()


def place(pos):
    return pos[0], pos[1], pos[2], pos[3]


def gray(index):
    return index ^ (index >> 1)


def ring(r, s):
    return gray((r + s) % NZ)


def column_of(x, z, y):
    return pl.multiple_of(((x * NZ + z) * NY + y) * HEAD_DIM, HEAD_DIM)


def extra_rows(blocks):
    used = sum(block.shape[0] for block in blocks)
    if used < EXTRA:
        blocks = [*blocks, jnp.zeros((EXTRA - used, HEAD_DIM), F32)]
    return jnp.concatenate(blocks, axis=0)


def put_extra(out, start, values):
    out[start : start + EXTRA, :HEAD_DIM] = values.astype(BF16)
    out[start : start + EXTRA, HEAD_DIM:] = jnp.zeros((EXTRA, out.shape[1] - HEAD_DIM), BF16)


def split_kernel(pos, gains, w_query, w_key, w_value, *outs):
    x, _, y, _ = place(pos)
    rows = w_query.shape[0]
    own = gains[...].astype(F32)
    own = jnp.concatenate([own, jnp.zeros((4, HEAD_DIM - rows), F32)], axis=1)
    length = jnp.full((1, HEAD_DIM), pos[4]).astype(F32)
    for (dx, dy), out in zip(SQUARE, outs):
        for i, weight in enumerate((w_query, w_key, w_value)):
            for head in range(NZ):
                start = column_of(x ^ dx, head, y ^ dy)
                at = i * HEADS + head * HEAD_DIM
                out[:rows, at : at + HEAD_DIM] = weight[:, pl.ds(start, HEAD_DIM)]
        put_extra(out, rows, extra_rows([own, length]))


def join_kernel(*refs):
    *parts, w_output, out, lengths = refs
    rows = parts[0].shape[0] - EXTRA
    extras = []
    for i, part in enumerate(parts):
        for j in range(3):
            at = (j * GROUP + i) * rows
            out[at : at + rows] = part[:rows, j * HEADS : (j + 1) * HEADS]
        at = (3 * GROUP + i) * rows
        out[at : at + rows] = w_output[:, i * HEADS : (i + 1) * HEADS]
        extras.append(part[rows:, :HEAD_DIM].astype(F32))
    put_extra(out, 4 * GROUP * rows, extra_rows([extra[:4] for extra in extras]))
    lengths[...] = jnp.concatenate(
        [extras[0][4:5], extras[1][4:5], jnp.zeros((6, HEAD_DIM), F32)], axis=0
    )


def row_stats(first, second):
    shape = (first.shape[0], HEAD_DIM)
    upper = lax.broadcasted_iota(jnp.int32, shape, 1) < 4
    sums = jnp.where(
        upper,
        jnp.sum(first, axis=1, keepdims=True),
        jnp.sum(second, axis=1, keepdims=True),
    )
    return jnp.transpose(sums)[:8]


def gather_kernel(*refs):
    blocks, (whole, kept, sem) = refs[:-3], refs[-3:]
    start = 0
    for block in blocks:
        whole[start : start + block.shape[0]] = block[...]
        start += block.shape[0]
    copy = pltpu.make_async_copy(whole, kept, sem)
    copy.start()
    copy.wait()


def project_kernel(nc, places, pos, x_all, *refs):
    weights, refs = refs[: nc * len(places)], refs[nc * len(places) :]
    last = places[-1] == NZ - 1
    if last:
        before, _, _, *refs = refs
    gains, out_w, *refs = refs
    w_rows, refs = refs[: len(places)], refs[len(places) :]
    if last:
        query, key, value, query_h, key_h, value_h, out_kept, stats, *refs = refs
    else:
        total, *refs = refs
    columns, w_part, sems = refs
    x, r, y, c = place(pos)
    rows = (weights[0].shape[0] - EXTRA) // (4 * GROUP)
    copies = Copies(sems)
    put = []
    for slot, s in enumerate(places):
        blocks = weights[slot * nc : (slot + 1) * nc]
        z = ring(r, s)
        extras = [block[4 * GROUP * rows :, :HEAD_DIM].astype(F32) for block in blocks]
        lanes = []
        for place_c in range(nc):
            chosen = 0.0
            for k, part in enumerate(extras):
                chosen = chosen + jnp.where((c ^ k) == place_c, part[:, :rows], 0.0)
            lanes.append(chosen)
        ordered = jnp.concatenate(lanes, axis=1)
        base = slot * GROUP * HEAD_DIM
        for i, (dx, dy) in enumerate(SQUARE):
            start = column_of(x ^ dx, z, y ^ dy)
            gains[:, pl.ds(start, HEAD_DIM)] = jnp.concatenate(
                [ordered[4 * i : 4 * i + 4], jnp.zeros((4, HEAD_DIM), F32)], axis=0
            )
            to = base + i * HEAD_DIM
            columns[:, to : to + HEAD_DIM] = x_all[:, pl.ds(start, HEAD_DIM)]
            for k, block in enumerate(blocks):
                at = pl.multiple_of(to + (c ^ k) * rows, rows)
                for j in range(3):
                    got = (j * GROUP + i) * rows
                    lanes = slice(j * HEADS, (j + 1) * HEADS)
                    w_part[pl.ds(at, rows), lanes] = block[got : got + rows]
                got = (3 * GROUP + i) * rows
                at = pl.multiple_of(z * HEAD_DIM + (c ^ k) * rows, rows)
                lanes = slice(i * HEADS, (i + 1) * HEADS)
                out_w[pl.ds(at, rows), lanes] = block[got : got + rows]
        put.append(
            copies.start(w_part.at[pl.ds(base, GROUP * HEAD_DIM)], w_rows[slot])
        )
    step = HEADS // 2
    for part in range(6):
        at = slice(part * step, (part + 1) * step)
        result = nn(columns[...], w_part[:, at])
        if last:
            result = before[:, at] + result
            out = (query, key, value)[part // 2]
            out[:, (part % 2) * step : (part % 2 + 1) * step] = result.astype(out.dtype)
        else:
            total[:, at] = result
    if last:
        stats[...] = row_stats(query[...] * query[...], key[...] * key[...])
        put += [
            copies.start(*pair)
            for pair in ((query, query_h), (key, key_h), (value, value_h), (out_w, out_kept))
        ]
    finish(put)


def turn(values, cosine, sine):
    return values * cosine + pltpu.roll(values, HEAD_DIM // 2, 1) * sine


def valid_keys(x, length, tok):
    shape = (NX * tok, NX * tok)
    queries = lax.broadcasted_iota(jnp.int32, shape, 0)
    keys = lax.broadcasted_iota(jnp.int32, shape, 1)

    def at(index):
        return jnp.where(index < tok, x * tok + index, (1 - x) * tok + index - tok)

    return (at(keys) <= at(queries)) & (at(keys).astype(F32) < length)


def softmax(query, key, valid):
    logits = jnp.where(valid, nt(query, key) * HEAD_DIM ** (-0.5), NEGATIVE)
    powers = jnp.exp(logits - jnp.max(logits, axis=1, keepdims=True))
    return powers / jnp.sum(powers, axis=1, keepdims=True)


def attend_kernel(pos, *refs):
    x, _, y, _ = place(pos)
    stats, *refs = refs
    lengths, gains, cosine, sine, query, key, value, out_w, *refs = refs
    query_out, key_out, attended_out, scales, *refs = refs
    pieces, refs = refs[:GROUP], refs[GROUP:]
    query_r, key_r, attended, sems = refs
    copies = Copies(sems)
    tok = query.shape[0] // GROUP
    span = NX * tok
    width = out_w.shape[1]
    scale = lax.rsqrt(stats[...] / width + EPSILON)
    scales[...] = scale
    for seq in range(NY):
        at = slice(seq * span, (seq + 1) * span)
        columns = jnp.transpose(scale[:, at])
        valid = valid_keys(x, lengths[seq : seq + 1, 0:1], tok)
        for head in range(NZ):
            lanes = slice(head * HEAD_DIM, (head + 1) * HEAD_DIM)
            gain = pl.ds(column_of(x, head, y), HEAD_DIM)
            for row, (raw, out) in enumerate(((query, query_r), (key, key_r))):
                normed = raw[at, lanes] * columns[:, 4 * row : 4 * row + 1]
                normed = normed * gains[row : row + 1, gain]
                out[at, lanes] = turn(normed, cosine[...], sine[...]).astype(BF16)
            chances = softmax(query_r[at, lanes], key_r[at, lanes], valid)
            attended[at, lanes] = nn(chances.astype(BF16), value[at, lanes]).astype(BF16)
    put = [
        copies.start(*pair)
        for pair in ((query_r, query_out), (key_r, key_out), (attended, attended_out))
    ]
    step = width // 4
    for part in range(4):
        columns = slice(part * step, (part + 1) * step)
        result = nn(attended[...], out_w[:, columns])
        for i, block in enumerate(TOKEN_BLOCKS):
            out = pieces[SQUARE.index(block)]
            out[:, columns] = result[i * tok : (i + 1) * tok].astype(out.dtype)
    finish(put)


def in_halves(values, x, out):
    half = out.shape[1] // NX
    for dx in range(NX):
        start = pl.multiple_of((x ^ dx) * half, half)
        out[:, dx * half : (dx + 1) * half] = values[:, pl.ds(start, half)].astype(out.dtype)


def sum_of(refs):
    total = refs[0][...].astype(F32)
    for ref in refs[1:]:
        total = total + ref[...].astype(F32)
    return total


def branch_kernel(pos, *refs):
    parts, refs = refs[:GROUP], refs[GROUP:]
    inputs, gains, branch_out, hidden_out, mlp_in = refs
    branch = sum_of(parts)
    branch_out[...] = branch
    scale = lax.rsqrt(jnp.mean(branch * branch, axis=1, keepdims=True) + EPSILON)
    hidden_out[...] = inputs[...].astype(F32) + branch * scale * gains[2:3, :]
    in_halves(hidden_out, pos[0], mlp_in)


def norm_back(values, gain, grad):
    scale = lax.rsqrt(jnp.mean(values * values, axis=1, keepdims=True) + EPSILON)
    normed = values * scale
    scaled = grad * gain
    mean = jnp.mean(scaled * normed, axis=1, keepdims=True)
    return scale * (scaled - normed * mean), jnp.sum(grad * normed, axis=0, keepdims=True)


def mlp_kernel(count, pos, *refs):
    parts, refs = refs[:count], refs[count:]
    hidden, gains, grad_output, output, grad_in, grad_gain, halves, mlp_out = refs
    halves[...] = sum_of(parts)
    in_halves(halves, pos[0], mlp_out)
    values = mlp_out[...]
    gain = gains[3:4, :]
    scale = lax.rsqrt(jnp.mean(values * values, axis=1, keepdims=True) + EPSILON)
    output[...] = (hidden[...] + values * scale * gain).astype(BF16)
    grad, by_gain = norm_back(values, gain, grad_output[...].astype(F32))
    halves[...] = grad
    in_halves(halves, pos[0], grad_in)
    grad_gain[...] = jnp.broadcast_to(by_gain, grad_gain.shape)


def branch_back_kernel(count, pos, *refs):
    parts, refs = refs[:count], refs[count:]
    branch, gains, grad_output, grad_hidden, grad_branch, grad_gain, halves, middle = refs
    halves[...] = sum_of(parts)
    in_halves(halves, pos[0], middle)
    total = grad_output[...].astype(F32) + middle[...]
    grad_hidden[...] = total
    grad, by_gain = norm_back(branch[...], gains[2:3, :], total)
    grad_branch[...] = grad.astype(BF16)
    grad_gain[...] = jnp.broadcast_to(by_gain, grad_gain.shape)


def attend_back_kernel(pos, *refs):
    lengths, scales, gains, cosine, sine, out_w, *refs = refs
    blocks, refs = refs[:GROUP], refs[GROUP:]
    held, refs = refs[:5], refs[5:]
    query_out, key_out, grad_value, stats, head_gains, branch_all, *refs = refs
    query_r, key_r, value, query, key, *refs = refs
    grad_query, grad_key, grad_att, sems = refs
    x, _, y, _ = place(pos)
    tok = blocks[0].shape[0]
    span = NX * tok
    copies = Copies(sems)
    later = [
        copies.start(*pair) for pair in zip(held, (query_r, key_r, value, query, key))
    ]
    for i, block in enumerate(TOKEN_BLOCKS):
        branch_all[i * tok : (i + 1) * tok] = blocks[SQUARE.index(block)][...]
    for half in range(2):
        lanes = slice(half * (HEADS // 2), (half + 1) * (HEADS // 2))
        grad_att[:, lanes] = nt(branch_all[...], out_w[lanes, :]).astype(BF16)
    head_gains[...] = jnp.zeros_like(head_gains)
    finish(later)
    for seq in range(NY):
        at = slice(seq * span, (seq + 1) * span)
        columns = jnp.transpose(scales[:, at])
        valid = valid_keys(x, lengths[seq : seq + 1, 0:1], tok)
        for head in range(NZ):
            lanes = slice(head * HEAD_DIM, (head + 1) * HEAD_DIM)
            gain = pl.ds(column_of(x, head, y), HEAD_DIM)
            queries, keys, values = query_r[at, lanes], key_r[at, lanes], value[at, lanes]
            chances = softmax(queries, keys, valid)
            incoming = grad_att[at, lanes]
            grad_chances = nt(incoming, values)
            grad_value[at, lanes] = tn(chances.astype(BF16), incoming).astype(BF16)
            balance = jnp.sum(chances * grad_chances, axis=1, keepdims=True)
            grad_logits = (chances * (grad_chances - balance)).astype(BF16)
            by_query = nn(grad_logits, keys) * HEAD_DIM ** (-0.5)
            by_key = tn(grad_logits, queries) * HEAD_DIM ** (-0.5)
            for row, (grad, raw, out) in enumerate(
                ((by_query, query, grad_query), (by_key, key, grad_key))
            ):
                back = turn(grad.astype(BF16).astype(F32), cosine[...], -sine[...])
                normed = raw[at, lanes] * columns[:, 4 * row : 4 * row + 1]
                head_gains[row : row + 1, lanes] += jnp.sum(back * normed, axis=0, keepdims=True)
                out[at, lanes] = back * gains[row : row + 1, gain]
    query_out[...] = grad_query[...]
    key_out[...] = grad_key[...]
    stats[...] = row_stats(grad_query[...] * query[...], grad_key[...] * key[...])


def project_back_kernel(*refs):
    stats, *refs = refs
    scales, grad_query, grad_key, grad_value, query, key, grads = refs
    width = NX * NY * HEADS
    means = jnp.transpose(stats[...] / width)
    columns = jnp.transpose(scales[...])
    for row, (grad, raw) in enumerate(((grad_query, query), (grad_key, key))):
        scale = columns[:, 4 * row : 4 * row + 1]
        mean = means[:, 4 * row : 4 * row + 1]
        result = scale * (grad[...] - raw[...] * (scale * scale * mean))
        grads[:, row * HEADS : (row + 1) * HEADS] = result.astype(BF16)
    grads[:, 2 * HEADS :] = grad_value[...]


def input_back_kernel(pos, grads, *refs):
    weights, refs = refs[:NZ], refs[NZ:]
    *pieces, results = refs
    x, r, y, _ = place(pos)
    tok = grads.shape[0] // GROUP
    for s, weight in enumerate(weights):
        for half in range(2):
            result = nt(grads[...], weight[half * HEADS // 2 : (half + 1) * HEADS // 2, :])
            results[:, half * HEADS // 2 : (half + 1) * HEADS // 2] = result.astype(BF16)
        for j, (dx, dy) in enumerate(SQUARE):
            start = column_of(x ^ dx, ring(r, s), y ^ dy)
            for i, block in enumerate(TOKEN_BLOCKS):
                out = pieces[SQUARE.index(block)]
                out[:, pl.ds(start, HEAD_DIM)] = results[
                    i * tok : (i + 1) * tok, j * HEAD_DIM : (j + 1) * HEAD_DIM
                ]


def weight_back_kernel(nc, places, pos, *refs):
    for i, s in enumerate(places):
        weight_back_part(nc, s, i, pos, *refs)


def weight_back_part(nc, s, slot, pos, x_all, grads, attended, branch_all, *refs):
    attn_gain, mlp_gain, head_gains, *outs, columns, sums, out_sums = refs
    x, r, y, c = place(pos)
    rows = HEAD_DIM // nc
    base = slot * (4 * GROUP * rows + EXTRA)
    z = ring(r, s)
    gains = []
    for i, (dx, dy) in enumerate(SQUARE):
        start = column_of(x ^ dx, z, y ^ dy)
        columns[:, i * HEAD_DIM : (i + 1) * HEAD_DIM] = x_all[:, pl.ds(start, HEAD_DIM)]
        if i == 0:
            heads = pl.ds(pl.multiple_of(z * HEAD_DIM, HEAD_DIM), HEAD_DIM)
            gains.append(head_gains[0:2, heads])
        else:
            gains.append(jnp.zeros((2, HEAD_DIM), F32))
        gains.append(attn_gain[0:1, pl.ds(start, HEAD_DIM)])
        gains.append(mlp_gain[0:1, pl.ds(start, HEAD_DIM)])
    gains = jnp.concatenate(gains, axis=0)
    step = grads.shape[1] // 3
    for part in range(3):
        lanes = slice(part * step, (part + 1) * step)
        sums[:, lanes] = tn(columns[...], grads[:, lanes]).astype(BF16)
    heads = pl.ds(pl.multiple_of(z * HEAD_DIM, HEAD_DIM), HEAD_DIM)
    out_sums[...] = tn(attended[:, heads], branch_all[...]).astype(BF16)
    for k, out in enumerate(outs):
        for i in range(GROUP):
            start = pl.multiple_of(i * HEAD_DIM + (c ^ k) * rows, rows)
            for j in range(3):
                at = base + (j * GROUP + i) * rows
                lanes = slice(j * HEADS, (j + 1) * HEADS)
                out[at : at + rows] = sums[pl.ds(start, rows), lanes]
            start = pl.multiple_of((c ^ k) * rows, rows)
            at = base + (3 * GROUP + i) * rows
            lanes = slice(i * HEADS, (i + 1) * HEADS)
            out[at : at + rows] = out_sums[pl.ds(start, rows), lanes]
        chosen = 0.0
        for place_c in range(nc):
            part = gains[:, place_c * rows : (place_c + 1) * rows]
            chosen = chosen + jnp.where((c ^ k) == place_c, part, 0.0)
        chosen = jnp.concatenate([chosen, jnp.zeros((EXTRA, HEAD_DIM - rows), F32)], axis=1)
        put_extra(out, base + 4 * GROUP * rows, chosen)


def collect_kernel(count, *refs):
    parts, (grad_wo, *outs) = refs[:count], refs[count:]
    rows = (parts[0].shape[0] - EXTRA) // (4 * GROUP)

    def total(at, height, lanes=slice(None)):
        result = parts[0][at : at + height, lanes].astype(F32)
        for part in parts[1:]:
            result = result + part[at : at + height, lanes].astype(F32)
        return result

    extra = total(4 * GROUP * rows, EXTRA, slice(0, HEAD_DIM))
    for i, out in enumerate(outs):
        for j in range(3):
            part = total((j * GROUP + i) * rows, rows)
            out[:rows, j * HEADS : (j + 1) * HEADS] = part.astype(BF16)
        grad_wo[:, i * HEADS : (i + 1) * HEADS] = total((3 * GROUP + i) * rows, rows)
        put_extra(out, rows, extra_rows([extra[4 * i : 4 * i + 4]]))


def spread_kernel(pos, *refs):
    parts, (*outs, gains) = refs[:GROUP], refs[GROUP:]
    x, _, y, _ = place(pos)
    rows = parts[0].shape[0] - EXTRA
    total = 0.0
    for (dx, dy), part in zip(SQUARE, parts):
        total = total + part[rows:, :HEAD_DIM].astype(F32)
        for i, out in enumerate(outs):
            for head in range(NZ):
                start = column_of(x ^ dx, head, y ^ dy)
                at = i * HEADS + head * HEAD_DIM
                out[:, pl.ds(start, HEAD_DIM)] = part[:rows, at : at + HEAD_DIM].astype(F32)
    gains[...] = total[:8]


def mlp_forward_kernel(nc, *refs):
    blocks, refs = refs[:nc], refs[nc:]
    gates, ups, downs, refs = refs[:4], refs[4:8], refs[8:16], refs[16:]
    outs = refs[-(8 + nc + 1) :]
    products, by_gate, by_up, kept = outs[0:2], outs[2:4], outs[4:6], outs[6:8]
    sums, total = outs[8 : 8 + nc], outs[8 + nc]
    tok = blocks[0].shape[0]
    half = kept[0].shape[1]
    quarter = half // 2
    for k, block in enumerate(blocks):
        for dx in range(NX):
            kept[dx][k * tok : (k + 1) * tok] = block[:, dx * half : (dx + 1) * half]
    for dy in range(NY):

        def through(weights):
            return nn(kept[0][...], weights[dy][...]) + nn(kept[1][...], weights[NY + dy][...])

        gate, up = through(gates), through(ups)
        chance = 1.0 / (1.0 + jnp.exp(-gate))
        silu = gate * chance
        product = (silu * up).astype(BF16)
        products[dy][...] = product
        by_up[dy][...] = silu.astype(BF16)
        by_gate[dy][...] = (up * (chance + silu * (1.0 - chance))).astype(BF16)
        for i in range(4):
            lanes = slice(i * quarter, (i + 1) * quarter)
            part = nt(product, downs[i * NY + dy][...])
            if dy == 0:
                total[:, lanes] = part
            else:
                part = total[:, lanes] + part
                for k, out in enumerate(sums):
                    out[:, lanes] = part[k * tok : (k + 1) * tok].astype(out.dtype)


def mlp_back_kernel(nc, *refs):
    blocks, refs = refs[:nc], refs[nc:]
    gates, ups, downs, refs = refs[:4], refs[4:8], refs[8:16], refs[16:]
    by_gate, by_up = refs[0:2], refs[2:4]
    outs = refs[-(8 + nc + 1) :]
    grad_gates, grad_ups, kept = outs[0:2], outs[2:4], outs[4:8]
    sums, total = outs[8 : 8 + nc], outs[8 + nc]
    tok = blocks[0].shape[0]
    quarter = kept[0].shape[1]
    for k, block in enumerate(blocks):
        for i in range(4):
            kept[i][k * tok : (k + 1) * tok] = block[:, i * quarter : (i + 1) * quarter]
    for dy in range(NY):
        grad = nn(kept[0][...], downs[dy][...])
        for i in range(1, 4):
            grad = grad + nn(kept[i][...], downs[i * NY + dy][...])
        grad_gate = (grad * by_gate[dy][...].astype(F32)).astype(BF16)
        grad_up = (grad * by_up[dy][...].astype(F32)).astype(BF16)
        grad_gates[dy][...] = grad_gate
        grad_ups[dy][...] = grad_up
        for i in range(4):
            lanes = slice(i * quarter, (i + 1) * quarter)
            dx, rows = i // 2, slice((i % 2) * quarter, (i % 2 + 1) * quarter)
            part = nt(grad_gate, gates[dx * NY + dy][rows, :]) + nt(
                grad_up, ups[dx * NY + dy][rows, :]
            )
            if dy == 0:
                total[:, lanes] = part
            else:
                part = total[:, lanes] + part
                for k, out in enumerate(sums):
                    out[:, lanes] = part[k * tok : (k + 1) * tok].astype(out.dtype)


def make_body(wide):
    nc = wide // (NY * NZ)

    def send(value, x=0, y=0, r=0, c=0):
        pairs = []
        for sx in range(NX):
            for sz in range(NZ):
                for sy in range(NY):
                    for sc in range(nc):
                        source = sx * wide + (sz * NY + sy) * nc + sc
                        target = (sx ^ x) * wide
                        target += (ring(gray(sz), r) * NY + (sy ^ y)) * nc + (sc ^ c)
                        pairs.append((source, target))
        return lax.ppermute(value, AXES, pairs)

    def square(parts):
        return [
            part if (dx, dy) == (0, 0) else send(part, x=dx, y=dy)
            for (dx, dy), part in zip(SQUARE, parts)
        ]

    def square_gather(first, second):
        first_x = send(first, x=1)
        second_y = send(second, y=1)
        first_y = send(first, y=1)
        second_x = send(second, x=1)
        first_xy = send(first_x, y=1)
        second_xy = send(second_y, x=1)
        return [first, first_y, first_x, first_xy], [second, second_y, second_x, second_xy]

    def scatter_far(first, second):
        return send(first[3], x=1), send(second[3], y=1)

    def scatter_near(first, second):
        return send(first[2], x=1), send(second[1], y=1)

    def scatter_rest(first, second, far, near):
        first_c = send((first[1].astype(F32) + far[0].astype(F32)).astype(BF16), y=1)
        second_c = send((second[2].astype(F32) + far[1].astype(F32)).astype(BF16), x=1)
        return (
            first[0].astype(F32) + near[0].astype(F32) + first_c.astype(F32),
            second[0].astype(F32) + near[1].astype(F32) + second_c.astype(F32),
        )

    def core_gather(block):
        return [block] + [send(block, c=k) for k in range(1, nc)]

    def core_parts(parts):
        return [parts[0]] + [send(parts[k], c=k) for k in range(1, nc)]

    def body(
        layer_input,
        lengths,
        w_query,
        w_key,
        w_value,
        w_output,
        query_gain,
        key_gain,
        attn_gain,
        mlp_gain,
        w_gate,
        w_up,
        w_down,
        grad_output,
    ):
        x = lax.axis_index("blk")
        spot = lax.axis_index("wide")
        z, y, c = spot // (NY * nc), (spot // nc) % NY, spot % nc
        inputs, grad_out = layer_input[0], grad_output[0]
        tok, width = inputs.shape
        rows = w_query.shape[0]
        group_tok = GROUP * tok
        hidden = w_gate.shape[1]
        pos = jnp.stack([x, gray(z), y, c, lengths[0]]).astype(jnp.int32)
        wide_small = shaped((8, width), F32)
        by_head = shaped((group_tok, HEADS))
        by_head_wide = shaped((group_tok, HEADS), F32)
        by_token = shaped((8, group_tok), F32)
        tokens_shape = shaped((tok, width))
        tokens_wide = shaped((tok, width), F32)
        message = shaped((4 * GROUP * rows + EXTRA, HEADS))
        piece = shaped((rows + EXTRA, 3 * HEADS))

        def group_sum(stats, *ready):
            blocks = [stats[:, i * tok : (i + 1) * tok] for i in range(GROUP)]
            for flip, way in ((1, {"x": 1}), (2, {"y": 1})):
                total = jnp.concatenate(blocks, axis=1)
                if flip == 2 and ready:
                    total = after(total, ready)
                got = send(total, **way)
                got = [got[:, i * tok : (i + 1) * tok] for i in range(GROUP)]
                blocks = [block + got[i ^ flip] for i, block in enumerate(blocks)]
            return jnp.concatenate(blocks, axis=1)

        def dma(count):
            return pltpu.SemaphoreType.DMA((count,))

        def held(shape):
            return pltpu.VMEM(shape.shape, shape.dtype)

        gains = jnp.stack([query_gain, key_gain, attn_gain, mlp_gain])
        pieces = run(
            split_kernel,
            each([piece] * GROUP, VMEM),
            [(pos, SMEM), (gains, VMEM), (w_query, auto), (w_key, auto), (w_value, auto)],
        )
        down_rows = w_down.shape[0] // 2
        down_halves = w_down[:down_rows], w_down[down_rows:]
        far_down = send(down_halves[0], x=1), send(down_halves[1], y=1)
        received = after(square(pieces), far_down)
        own_rows, lengths_row = run(
            join_kernel,
            [(message, VMEM), (shaped((8, HEAD_DIM), F32), VMEM)],
            each((*received, w_output), VMEM),
        )
        lane = jnp.arange(HEAD_DIM)[None, :]
        row = jnp.arange(NX * tok)[:, None]
        row = jnp.where(row < tok, x * tok + row, (1 - x) * tok + row - tok).astype(F32)
        half = HEAD_DIM // 2
        frequency = jnp.exp((lane % half).astype(F32) * (-2.0 * math.log(500000.0) / HEAD_DIM))
        cosine = jnp.cos(row * frequency)
        sine = jnp.sin(row * jnp.where(lane < half, -frequency, frequency))
        w_ring = [own_rows, send(own_rows, r=-1)]
        far_gate = send(after(w_gate, own_rows), x=1)
        far_up = send(after(w_up, own_rows), y=1)
        from_x = send(after(inputs, far_gate), x=1)
        from_y = send(after(inputs, far_up), y=1)
        half_tok = tok // 2
        from_xy = send(from_x[:half_tok], y=1), send(from_y[half_tok:], x=1)
        near_gate = send(after(w_gate, from_xy[0]), y=1)
        near_up = send(after(w_up, from_xy[1]), x=1)
        w_ring.append(send(after(w_ring[1], cosine, sine, far_gate, far_up), r=-1))
        w_ring.append(send(after(w_ring[2], from_xy), r=-1))
        x_all, x_kept = run(
            gather_kernel,
            [(shaped((group_tok, width)), VMEM), (shaped((group_tok, width)), HBM)],
            each([inputs, from_x, from_y, *from_xy], VMEM),
            scratch_shapes=[pltpu.SemaphoreType.DMA],
        )
        w_ring[3] = after(w_ring[3], near_gate, near_up)
        w_blocks = [core_gather(block) for block in w_ring]
        w_shape = shaped((GROUP * HEAD_DIM, 3 * HEADS))
        by_three = shaped((group_tok, 3 * HEADS), F32)
        out_shape = shaped((HEADS, width))

        def project(places, blocks, before, outs):
            ins = [(pos, SMEM), (x_all, VMEM), *each(blocks, VMEM), *each(before, VMEM)]
            depth = len(places) * GROUP * HEAD_DIM
            return run(
                functools.partial(project_kernel, nc, places),
                [(wide_small, VMEM), (out_shape, VMEM)] + [(w_shape, HBM)] * len(places) + outs,
                ins,
                limit=16,
                input_output_aliases={len(ins) - 2: 0, len(ins) - 1: 1} if before else {},
                scratch_shapes=[
                    pltpu.VMEM((group_tok, depth), BF16),
                    pltpu.VMEM((depth, 3 * HEADS), BF16),
                    dma(len(places) + 4),
                ],
            )

        blocks = w_blocks[0] + w_blocks[1] + w_blocks[2]
        gains, out_w, *w_parts, total = project((0, 1, 2), blocks, (), [(by_three, VMEM)])
        gains, out_w, w_part, query, key, value, query_h, key_h, value_h, out_kept, stats = project(
            (3,),
            w_blocks[3],
            (total, gains, out_w),
            [(by_head_wide, VMEM), (by_head_wide, VMEM), (by_head, VMEM)]
            + [(by_head_wide, HBM), (by_head_wide, HBM), (by_head, HBM)]
            + [(out_shape, HBM), (by_token, VMEM)],
        )
        w_parts.append(w_part)
        group_stats = group_sum(stats, near_gate, near_up)
        last_gate = send(after(far_gate, group_stats, near_gate), y=1)
        last_up = send(after(far_up, group_stats, near_up), x=1)
        gate_w = [w_gate, near_gate, far_gate, last_gate]
        up_w = [w_up, far_up, near_up, last_up]

        query_r, key_r, attended, scales, *parts = run(
            attend_kernel,
            [(by_head, HBM)] * 3 + [(by_token, VMEM)] + [(tokens_shape, VMEM)] * GROUP,
            [
                (pos, SMEM),
                (group_stats, VMEM),
                *each((lengths_row, gains, cosine, sine), VMEM),
                *each((query, key, value, out_w), VMEM),
            ],
            scratch_shapes=[held(by_head), held(by_head), held(by_head), dma(3)],
        )
        parts = square(after(parts, gate_w, up_w))
        first, second = after(down_halves, parts)
        first_x, second_y = after(far_down, parts)
        down_first = first, send(first, y=1), first_x, send(first_x, y=1)
        down_second = second, second_y, send(second, x=1), send(second_y, x=1)
        down_w = [
            half[dx * NY + dy]
            for dx in range(NX)
            for half in (down_first, down_second)
            for dy in range(NY)
        ]
        branch, hidden_state, mlp_in = run(
            branch_kernel,
            [(tokens_wide, auto), (tokens_wide, auto), (tokens_shape, VMEM)],
            [(pos, SMEM), *each(parts, auto), (inputs, auto), (gains, VMEM)],
        )

        half_width = width // NX
        quarter = half_width // 2
        m = nc * tok

        def mlp_call(kernel, s, block, extra, kept_columns, before):
            def rows_of(array):
                return pl.BlockSpec((m, array.shape[1]), lambda i: (s, 0))

            ins = each(core_gather(block), auto)
            ins += each((*gate_w, *up_w, *down_w), VMEM) + each(extra, rows_of)
            columns = [hidden] * (8 - len(kept_columns)) + list(kept_columns)
            outs = each([shaped((NZ * m, count)) for count in columns], rows_of)
            outs += [(tokens_wide, VMEM)] + [(tokens_shape, VMEM)] * (nc - 1)
            aliases = {}
            if before is not None:
                aliases = {len(ins) + i: i for i in range(8)}
                ins += each(before, HBM)
            results = run(
                functools.partial(kernel, nc),
                outs,
                ins,
                limit=20 if nc == 2 else 56,
                input_output_aliases=aliases,
                scratch_shapes=[pltpu.VMEM((m, width), F32)],
            )
            return results[:8], core_parts(results[8:])

        def summed(parts):
            total = parts[0].astype(F32)
            for part in parts[1:]:
                total = total + part.astype(F32)
            return total

        def mlp_pass(kernel, block, extra, kept_columns):
            near = send(block, r=-1)
            kept, first = mlp_call(kernel, 1, near, extra, kept_columns, None)
            middle = send(near, r=-1)
            moving = send(summed(first).astype(BF16), r=-1)
            kept, own = mlp_call(kernel, 0, block, extra, kept_columns, kept)
            far = send(after(middle, first[0]), r=-1)
            kept, second = mlp_call(kernel, 2, middle, extra, kept_columns, kept)
            far = after(far, moving)
            kept, third = mlp_call(kernel, 3, far, extra, kept_columns, kept)
            sent = [summed(second + [moving]).astype(BF16)]
            sent.append(summed(third + [send(sent[0], r=-1)]).astype(BF16))
            return kept, own + [send(sent[1], r=-1)], sent

        kept, parts, _ = mlp_pass(mlp_forward_kernel, mlp_in, (), (half_width, half_width))

        products, by_gate, by_up, mlp_all = kept[0:2], kept[2:4], kept[4:6], kept[6:8]
        output, grad_mlp, grad_gain_mlp = run(
            functools.partial(mlp_kernel, len(parts)),
            [(tokens_shape, auto), (tokens_shape, VMEM), (wide_small, VMEM)],
            [
                (pos, SMEM),
                *each(parts, auto),
                (hidden_state, auto),
                (gains, VMEM),
                (grad_out, auto),
            ],
            scratch_shapes=[held(tokens_wide)] * 2,
        )
        extra = *by_gate, *by_up
        kept, parts, sent = mlp_pass(mlp_back_kernel, grad_mlp, extra, (quarter,) * 4)
        grad_gates, grad_ups, grad_all = kept[0:2], kept[2:4], kept[4:8]
        grad_hidden, grad_branch, grad_gain_attn = run(
            functools.partial(branch_back_kernel, len(parts)),
            [(tokens_wide, auto), (tokens_shape, VMEM), (wide_small, VMEM)],
            [
                (pos, SMEM),
                *each(parts, auto),
                (branch, auto),
                (gains, VMEM),
                (grad_out, auto),
            ],
            scratch_shapes=[held(tokens_wide)] * 2,
        )

        def products_of(left, right):
            return [tn(left[dx], right[dy]).astype(BF16) for dx, dy in SQUARE]

        grad_all = after(grad_all, sent[0])
        wd_pair = products_of(grad_all[0::2], products), products_of(grad_all[1::2], products)
        wd_far = scatter_far(*wd_pair)
        wd_near = scatter_near(*after(wd_pair, wd_far))
        grad_branch = after(grad_branch, wd_near)
        mlp_all = after(mlp_all, sent[1])
        grad_wg = products_of(mlp_all, grad_gates)
        grad_wu = products_of(mlp_all, grad_ups)

        blocks = square([grad_branch] * GROUP)
        w_pair = grad_wg, grad_wu
        blocks = after(blocks, w_pair)
        w_far = scatter_far(*after(w_pair, blocks))
        grad_query, grad_key, grad_value, stats, head_gains, branch_all = run(
            attend_back_kernel,
            [
                (by_head_wide, VMEM),
                (by_head_wide, VMEM),
                (by_head, VMEM),
                (by_token, VMEM),
                (shaped((8, HEADS), F32), VMEM),
                (shaped((group_tok, width)), VMEM),
            ],
            [
                (pos, SMEM),
                *each((lengths_row, scales, gains, cosine, sine, out_kept, *blocks), VMEM),
                *each((query_r, key_r, value_h, query_h, key_h), HBM),
            ],
            limit=16,
            scratch_shapes=[
                held(by_head),
                held(by_head),
                held(by_head),
                held(by_head_wide),
                held(by_head_wide),
                held(by_head_wide),
                held(by_head_wide),
                held(by_head),
                dma(5),
            ],
        )
        (grads,) = run(
            project_back_kernel,
            [(shaped((group_tok, 3 * HEADS)), VMEM)],
            [
                (after(group_sum(stats), w_far), VMEM),
                (scales, VMEM),
                *each((grad_query, grad_key, grad_value, query_h, key_h), VMEM),
            ],
        )
        w_near = scatter_near(*after(w_pair, grads))

        def weight_parts(places):
            height = message.shape[0]
            results = run(
                functools.partial(weight_back_kernel, nc, places),
                [(shaped((len(places) * height, HEADS)), VMEM)] * nc,
                [
                    (pos, SMEM),
                    *each((x_kept, grads, attended, branch_all), VMEM),
                    *each((grad_gain_attn, grad_gain_mlp, head_gains), VMEM),
                ],
                scratch_shapes=[
                    pltpu.VMEM((group_tok, GROUP * HEAD_DIM), BF16),
                    pltpu.VMEM((GROUP * HEAD_DIM, 3 * HEADS), BF16),
                    pltpu.VMEM((HEAD_DIM, width), BF16),
                ],
            )
            results = core_parts(results)
            return [
                [part[i * height : (i + 1) * height] for part in results]
                for i in range(len(places))
            ]

        (first,) = weight_parts((1,))
        w_moving = send(after(summed(first).astype(BF16), w_far), r=-1)
        grads = after(grads, first)
        second, third, own = weight_parts((2, 3, 0))
        sent = summed(second + [w_moving]).astype(BF16)
        w_moving = send(after(sent, own, w_near), r=-1)
        grad_wg, grad_wu = scatter_rest(*w_pair, *after((w_far, w_near), sent))
        wd_far, wd_near = after((wd_far, wd_near), grad_wg, grad_wu)
        grad_wd = jnp.concatenate(scatter_rest(*wd_pair, wd_far, wd_near), axis=0)
        sent = summed(third + [w_moving]).astype(BF16)
        w_moving = send(sent, r=-1)
        parts = own + [w_moving]
        grad_wo, *messages = run(
            functools.partial(collect_kernel, len(parts)),
            [(shaped((rows, width), F32), auto)] + [(piece, VMEM)] * GROUP,
            each(parts, auto),
        )
        grad_wq, grad_wk, grad_wv, total_gains = run(
            spread_kernel,
            [(shaped((rows, width), F32), auto)] * 3 + [(shaped((8, HEAD_DIM), F32), VMEM)],
            [(pos, SMEM), *each(square(messages), auto)],
        )
        parts = run(
            input_back_kernel,
            [(tokens_shape, VMEM)] * GROUP,
            [(pos, SMEM), (after(grads, sent), VMEM), *each(w_parts, VMEM)],
            scratch_shapes=[pltpu.VMEM((group_tok, GROUP * HEAD_DIM), BF16)],
        )
        grad_x = summed([grad_hidden, *square(after(parts, messages))])

        return (
            output[None],
            grad_x.astype(BF16)[None],
            grad_wq,
            grad_wk,
            grad_wv,
            grad_wo,
            total_gains[0, :rows],
            total_gains[1, :rows],
            total_gains[2, :rows],
            total_gains[3, :rows],
            grad_wg,
            grad_wu,
            grad_wd,
        )

    return body


def solution(mesh):
    return jax.shard_map(
        make_body(mesh.shape["wide"]),
        mesh=mesh,
        in_specs=(
            P("wide", "blk", None),
            P("wide"),
            P(("blk", "wide"), None),
            P(("blk", "wide"), None),
            P(("blk", "wide"), None),
            P(("blk", "wide"), None),
            P(("blk", "wide")),
            P(("blk", "wide")),
            P(("blk", "wide")),
            P(("blk", "wide")),
            P("blk", "wide"),
            P("blk", "wide"),
            P("blk", "wide"),
            P("wide", "blk", None),
        ),
        out_specs=(
            P("wide", "blk", None),
            P("wide", "blk", None),
            P(("blk", "wide"), None),
            P(("blk", "wide"), None),
            P(("blk", "wide"), None),
            P(("blk", "wide"), None),
            P(("blk", "wide")),
            P(("blk", "wide")),
            P(("blk", "wide")),
            P(("blk", "wide")),
            P("blk", "wide"),
            P("blk", "wide"),
            P("blk", "wide"),
        ),
        check_vma=False,
    )
```

```python
import functools
import math

import jax
import jax.numpy as jnp
from jax import lax
from jax.experimental import pallas as pl
from jax.experimental.pallas import tpu as pltpu
from jax.sharding import PartitionSpec as P

HEAD_DIM = 128
EPSILON = 1e-06
NEGATIVE = -1e30
BF16 = jnp.bfloat16
F32 = jnp.float32
AXES = ("blk", "wide")
NX, NY, NZ = 2, 2, 4
GROUP = NX * NY
HEADS = NZ * HEAD_DIM
MIB = 1 << 20
SMEM = pl.BlockSpec(memory_space=pltpu.SMEM)
VMEM = pl.BlockSpec(memory_space=pltpu.VMEM)
HBM = pl.BlockSpec(memory_space=pltpu.HBM)
EXTRA = 16
PLAN = {'far_down': 'join', 'turns': 'w2', 'far': 'w3', 'tokens': 'w2', 'tokens_xy': 'w2', 'near': 'c3', 'own_gate_c': 'w3', 'own_down_c': 'c3', 'far_c': 'c3', 'far_down_c': 'stats', 'total': 'c3', 'near_down': 'k4', 'near_c': 'rs', 'last_from': 'stats', 'last': 'rs', 'last_c': 'f1', 'near_down_c': 'rs', 'f_lead': 0, 'f_out': 0, 'f_hold': 0, 'b_lead': 0, 'b_out': 0, 'b_hold': 0, 'products_from': 1, 'products': 'b1', 'products_xy': 'b2', 'near_grads': 'b3', 'near_grads_xy': 'b4', 'dots_from': 'block', 'dots': 'blocks', 'far_grads_from': 'sent', 'far_grads': 'ag', 'far_grads_xy': 'g1', 'sums_late': 1, 'sums': 'g1', 'w_far_late': 1, 'w_far': 't2', 'w_near': 't3', 'w_last': 'collect', 'w_last_late': 1, 'factors': 'collect', 'grad_wd': 'collect', 'x_parts': 't3', 'x_from': 'near', 'x_sums': 'spread', 'tokens_first': 1, 'far_from': 'xy', 'second_after': 'first', 'x_last_from': 'messages'}
SQUARE = [(dx, dy) for dx in range(NX) for dy in range(NY)]
TOKEN_BLOCKS = [(dx, dy) for dy in range(NY) for dx in range(NX)]


def shaped(shape, dtype=BF16):
    return jax.ShapeDtypeStruct(tuple(shape), dtype)


def nn(left, right):
    return lax.dot_general(left, right, (((1,), (0,)), ((), ())), preferred_element_type=F32)


def nt(left, right):
    return lax.dot_general(left, right, (((1,), (1,)), ((), ())), preferred_element_type=F32)


def tn(left, right):
    return lax.dot_general(left, right, (((0,), (0,)), ((), ())), preferred_element_type=F32)


def auto(array):
    return pl.BlockSpec(array.shape, lambda i: (0,) * len(array.shape))


def run(body, outs, ins, limit=12, **options):
    return pl.pallas_call(
        body,
        grid=(1,),
        out_shape=[
            pltpu.HBM(out.shape, out.dtype) if spec is HBM else out for out, spec in outs
        ],
        out_specs=[spec if isinstance(spec, pl.BlockSpec) else spec(out) for out, spec in outs],
        in_specs=[spec if isinstance(spec, pl.BlockSpec) else spec(array) for array, spec in ins],
        compiler_params=pltpu.CompilerParams(vmem_limit_bytes=limit * MIB),
        **options,
    )(*[array for array, _ in ins])


def each(arrays, spec):
    return [(array, spec) for array in arrays]


def after(value, *others):
    return lax.optimization_barrier((value, others))[0]


class Copies:
    def __init__(self, sems):
        self.sems, self.count = sems, 0

    def start(self, source, target):
        copy = pltpu.make_async_copy(source, target, self.sems.at[self.count])
        self.count += 1
        copy.start()
        return copy


def finish(copies):
    for copy in copies:
        copy.wait()


def place(pos):
    return pos[0], pos[1], pos[2], pos[3]


def gray(index):
    return index ^ (index >> 1)


def ring(r, s):
    return gray((r + s) % NZ)


def column_of(x, z, y):
    return pl.multiple_of(((x * NZ + z) * NY + y) * HEAD_DIM, HEAD_DIM)


def extra_rows(blocks):
    used = sum(block.shape[0] for block in blocks)
    if used < EXTRA:
        blocks = [*blocks, jnp.zeros((EXTRA - used, HEAD_DIM), F32)]
    return jnp.concatenate(blocks, axis=0)


def put_extra(out, start, values):
    out[start : start + EXTRA, :HEAD_DIM] = values.astype(BF16)
    out[start : start + EXTRA, HEAD_DIM:] = jnp.zeros((EXTRA, out.shape[1] - HEAD_DIM), BF16)


def split_kernel(pos, gains, w_query, w_key, w_value, *outs):
    x, _, y, _ = place(pos)
    rows = w_query.shape[0]
    own = gains[...].astype(F32)
    own = jnp.concatenate([own, jnp.zeros((4, HEAD_DIM - rows), F32)], axis=1)
    length = jnp.full((1, HEAD_DIM), pos[4]).astype(F32)
    for (dx, dy), out in zip(SQUARE, outs):
        for i, weight in enumerate((w_query, w_key, w_value)):
            for head in range(NZ):
                start = column_of(x ^ dx, head, y ^ dy)
                at = i * HEADS + head * HEAD_DIM
                out[:rows, at : at + HEAD_DIM] = weight[:, pl.ds(start, HEAD_DIM)]
        put_extra(out, rows, extra_rows([own, length]))


def join_kernel(*refs):
    *parts, w_output, out, lengths = refs
    rows = parts[0].shape[0] - EXTRA
    extras = []
    for i, part in enumerate(parts):
        for j in range(3):
            at = (j * GROUP + i) * rows
            out[at : at + rows] = part[:rows, j * HEADS : (j + 1) * HEADS]
        at = (3 * GROUP + i) * rows
        out[at : at + rows] = w_output[:, i * HEADS : (i + 1) * HEADS]
        extras.append(part[rows:, :HEAD_DIM].astype(F32))
    put_extra(out, 4 * GROUP * rows, extra_rows([extra[:4] for extra in extras]))
    lengths[...] = jnp.concatenate(
        [extras[0][4:5], extras[1][4:5], jnp.zeros((6, HEAD_DIM), F32)], axis=0
    )


def row_stats(first, second):
    shape = (first.shape[0], HEAD_DIM)
    upper = lax.broadcasted_iota(jnp.int32, shape, 1) < 4
    sums = jnp.where(
        upper,
        jnp.sum(first, axis=1, keepdims=True),
        jnp.sum(second, axis=1, keepdims=True),
    )
    return jnp.transpose(sums)[:8]


def gather_kernel(*refs):
    blocks, (whole, kept, sem) = refs[:-3], refs[-3:]
    start = 0
    for block in blocks:
        whole[start : start + block.shape[0]] = block[...]
        start += block.shape[0]
    copy = pltpu.make_async_copy(whole, kept, sem)
    copy.start()
    copy.wait()


def project_kernel(nc, places, pos, x_all, *refs):
    weights, refs = refs[: nc * len(places)], refs[nc * len(places) :]
    last = places[-1] == NZ - 1
    if last:
        before, _, _, *refs = refs
    gains, out_w, *refs = refs
    w_rows, refs = refs[: len(places)], refs[len(places) :]
    if last:
        query, key, value, query_h, key_h, value_h, out_kept, stats, *refs = refs
    else:
        total, *refs = refs
    columns, w_part, sems = refs
    x, r, y, c = place(pos)
    rows = (weights[0].shape[0] - EXTRA) // (4 * GROUP)
    copies = Copies(sems)
    put = []
    for slot, s in enumerate(places):
        blocks = weights[slot * nc : (slot + 1) * nc]
        z = ring(r, s)
        extras = [block[4 * GROUP * rows :, :HEAD_DIM].astype(F32) for block in blocks]
        lanes = []
        for place_c in range(nc):
            chosen = 0.0
            for k, part in enumerate(extras):
                chosen = chosen + jnp.where((c ^ k) == place_c, part[:, :rows], 0.0)
            lanes.append(chosen)
        ordered = jnp.concatenate(lanes, axis=1)
        base = slot * GROUP * HEAD_DIM
        for i, (dx, dy) in enumerate(SQUARE):
            start = column_of(x ^ dx, z, y ^ dy)
            gains[:, pl.ds(start, HEAD_DIM)] = jnp.concatenate(
                [ordered[4 * i : 4 * i + 4], jnp.zeros((4, HEAD_DIM), F32)], axis=0
            )
            to = base + i * HEAD_DIM
            columns[:, to : to + HEAD_DIM] = x_all[:, pl.ds(start, HEAD_DIM)]
            for k, block in enumerate(blocks):
                at = pl.multiple_of(to + (c ^ k) * rows, rows)
                for j in range(3):
                    got = (j * GROUP + i) * rows
                    lanes = slice(j * HEADS, (j + 1) * HEADS)
                    w_part[pl.ds(at, rows), lanes] = block[got : got + rows]
                got = (3 * GROUP + i) * rows
                at = pl.multiple_of(z * HEAD_DIM + (c ^ k) * rows, rows)
                lanes = slice(i * HEADS, (i + 1) * HEADS)
                out_w[pl.ds(at, rows), lanes] = block[got : got + rows]
        put.append(
            copies.start(w_part.at[pl.ds(base, GROUP * HEAD_DIM)], w_rows[slot])
        )
    step = HEADS // 2
    for part in range(6):
        at = slice(part * step, (part + 1) * step)
        result = nn(columns[...], w_part[:, at])
        if last:
            result = before[:, at] + result
            out = (query, key, value)[part // 2]
            out[:, (part % 2) * step : (part % 2 + 1) * step] = result.astype(out.dtype)
        else:
            total[:, at] = result
    if last:
        stats[...] = row_stats(query[...] * query[...], key[...] * key[...])
        put += [
            copies.start(*pair)
            for pair in ((query, query_h), (key, key_h), (value, value_h), (out_w, out_kept))
        ]
    finish(put)


def turn(values, cosine, sine):
    return values * cosine + pltpu.roll(values, HEAD_DIM // 2, 1) * sine


def valid_keys(x, length, tok):
    shape = (NX * tok, NX * tok)
    queries = lax.broadcasted_iota(jnp.int32, shape, 0)
    keys = lax.broadcasted_iota(jnp.int32, shape, 1)

    def at(index):
        return jnp.where(index < tok, x * tok + index, (1 - x) * tok + index - tok)

    return (at(keys) <= at(queries)) & (at(keys).astype(F32) < length)


def softmax(query, key, valid):
    logits = jnp.where(valid, nt(query, key) * HEAD_DIM ** (-0.5), NEGATIVE)
    powers = jnp.exp(logits - jnp.max(logits, axis=1, keepdims=True))
    return powers / jnp.sum(powers, axis=1, keepdims=True)


def attend_kernel(pos, *refs):
    x, _, y, _ = place(pos)
    stats, *refs = refs
    lengths, gains, cosine, sine, query, key, value, out_w, *refs = refs
    query_out, key_out, attended_out, scales, *refs = refs
    pieces, refs = refs[:GROUP], refs[GROUP:]
    query_r, key_r, attended, sems = refs
    copies = Copies(sems)
    tok = query.shape[0] // GROUP
    span = NX * tok
    width = out_w.shape[1]
    scale = lax.rsqrt(stats[...] / width + EPSILON)
    scales[...] = scale
    for seq in range(NY):
        at = slice(seq * span, (seq + 1) * span)
        columns = jnp.transpose(scale[:, at])
        valid = valid_keys(x, lengths[seq : seq + 1, 0:1], tok)
        for head in range(NZ):
            lanes = slice(head * HEAD_DIM, (head + 1) * HEAD_DIM)
            gain = pl.ds(column_of(x, head, y), HEAD_DIM)
            for row, (raw, out) in enumerate(((query, query_r), (key, key_r))):
                normed = raw[at, lanes] * columns[:, 4 * row : 4 * row + 1]
                normed = normed * gains[row : row + 1, gain]
                out[at, lanes] = turn(normed, cosine[...], sine[...]).astype(BF16)
            chances = softmax(query_r[at, lanes], key_r[at, lanes], valid)
            attended[at, lanes] = nn(chances.astype(BF16), value[at, lanes]).astype(BF16)
    put = [
        copies.start(*pair)
        for pair in ((query_r, query_out), (key_r, key_out), (attended, attended_out))
    ]
    step = width // 4
    for part in range(4):
        columns = slice(part * step, (part + 1) * step)
        result = nn(attended[...], out_w[:, columns])
        for i, block in enumerate(TOKEN_BLOCKS):
            out = pieces[SQUARE.index(block)]
            out[:, columns] = result[i * tok : (i + 1) * tok].astype(out.dtype)
    finish(put)


def in_halves(values, x, out):
    half = out.shape[1] // NX
    for dx in range(NX):
        start = pl.multiple_of((x ^ dx) * half, half)
        out[:, dx * half : (dx + 1) * half] = values[:, pl.ds(start, half)].astype(out.dtype)


def sum_of(refs):
    total = refs[0][...].astype(F32)
    for ref in refs[1:]:
        total = total + ref[...].astype(F32)
    return total


def branch_kernel(pos, *refs):
    parts, refs = refs[:GROUP], refs[GROUP:]
    inputs, gains, branch_out, hidden_out, mlp_in = refs
    branch = sum_of(parts)
    branch_out[...] = branch
    scale = lax.rsqrt(jnp.mean(branch * branch, axis=1, keepdims=True) + EPSILON)
    hidden_out[...] = inputs[...].astype(F32) + branch * scale * gains[2:3, :]
    in_halves(hidden_out, pos[0], mlp_in)


def norm_back(values, gain, grad):
    scale = lax.rsqrt(jnp.mean(values * values, axis=1, keepdims=True) + EPSILON)
    normed = values * scale
    scaled = grad * gain
    mean = jnp.mean(scaled * normed, axis=1, keepdims=True)
    return scale * (scaled - normed * mean), jnp.sum(grad * normed, axis=0, keepdims=True)


def mlp_kernel(count, pos, *refs):
    parts, refs = refs[:count], refs[count:]
    hidden, gains, grad_output, output, grad_in, grad_gain, halves, mlp_out = refs
    halves[...] = sum_of(parts)
    in_halves(halves, pos[0], mlp_out)
    values = mlp_out[...]
    gain = gains[3:4, :]
    scale = lax.rsqrt(jnp.mean(values * values, axis=1, keepdims=True) + EPSILON)
    output[...] = (hidden[...] + values * scale * gain).astype(BF16)
    grad, by_gain = norm_back(values, gain, grad_output[...].astype(F32))
    halves[...] = grad
    in_halves(halves, pos[0], grad_in)
    grad_gain[...] = jnp.broadcast_to(by_gain, grad_gain.shape)


def branch_back_kernel(count, pos, *refs):
    parts, refs = refs[:count], refs[count:]
    branch, gains, grad_output, grad_hidden, grad_branch, grad_gain, halves, middle = refs
    halves[...] = sum_of(parts)
    in_halves(halves, pos[0], middle)
    total = grad_output[...].astype(F32) + middle[...]
    grad_hidden[...] = total
    grad, by_gain = norm_back(branch[...], gains[2:3, :], total)
    grad_branch[...] = grad.astype(BF16)
    grad_gain[...] = jnp.broadcast_to(by_gain, grad_gain.shape)


def attend_back_kernel(pos, *refs):
    lengths, scales, gains, cosine, sine, out_w, *refs = refs
    blocks, refs = refs[:GROUP], refs[GROUP:]
    held, refs = refs[:5], refs[5:]
    query_out, key_out, grad_value, stats, head_gains, branch_all, *refs = refs
    query_r, key_r, value, query, key, *refs = refs
    grad_query, grad_key, grad_att, sems = refs
    x, _, y, _ = place(pos)
    tok = blocks[0].shape[0]
    span = NX * tok
    copies = Copies(sems)
    later = [
        copies.start(*pair) for pair in zip(held, (query_r, key_r, value, query, key))
    ]
    for i, block in enumerate(TOKEN_BLOCKS):
        branch_all[i * tok : (i + 1) * tok] = blocks[SQUARE.index(block)][...]
    for half in range(2):
        lanes = slice(half * (HEADS // 2), (half + 1) * (HEADS // 2))
        grad_att[:, lanes] = nt(branch_all[...], out_w[lanes, :]).astype(BF16)
    head_gains[...] = jnp.zeros_like(head_gains)
    finish(later)
    for seq in range(NY):
        at = slice(seq * span, (seq + 1) * span)
        columns = jnp.transpose(scales[:, at])
        valid = valid_keys(x, lengths[seq : seq + 1, 0:1], tok)
        for head in range(NZ):
            lanes = slice(head * HEAD_DIM, (head + 1) * HEAD_DIM)
            gain = pl.ds(column_of(x, head, y), HEAD_DIM)
            queries, keys, values = query_r[at, lanes], key_r[at, lanes], value[at, lanes]
            chances = softmax(queries, keys, valid)
            incoming = grad_att[at, lanes]
            grad_chances = nt(incoming, values)
            grad_value[at, lanes] = tn(chances.astype(BF16), incoming).astype(BF16)
            balance = jnp.sum(chances * grad_chances, axis=1, keepdims=True)
            grad_logits = (chances * (grad_chances - balance)).astype(BF16)
            by_query = nn(grad_logits, keys) * HEAD_DIM ** (-0.5)
            by_key = tn(grad_logits, queries) * HEAD_DIM ** (-0.5)
            for row, (grad, raw, out) in enumerate(
                ((by_query, query, grad_query), (by_key, key, grad_key))
            ):
                back = turn(grad.astype(BF16).astype(F32), cosine[...], -sine[...])
                normed = raw[at, lanes] * columns[:, 4 * row : 4 * row + 1]
                head_gains[row : row + 1, lanes] += jnp.sum(back * normed, axis=0, keepdims=True)
                out[at, lanes] = back * gains[row : row + 1, gain]
    query_out[...] = grad_query[...]
    key_out[...] = grad_key[...]
    stats[...] = row_stats(grad_query[...] * query[...], grad_key[...] * key[...])


def project_back_kernel(*refs):
    stats, *refs = refs
    scales, grad_query, grad_key, grad_value, query, key, grads = refs
    width = NX * NY * HEADS
    means = jnp.transpose(stats[...] / width)
    columns = jnp.transpose(scales[...])
    for row, (grad, raw) in enumerate(((grad_query, query), (grad_key, key))):
        scale = columns[:, 4 * row : 4 * row + 1]
        mean = means[:, 4 * row : 4 * row + 1]
        result = scale * (grad[...] - raw[...] * (scale * scale * mean))
        grads[:, row * HEADS : (row + 1) * HEADS] = result.astype(BF16)
    grads[:, 2 * HEADS :] = grad_value[...]


def input_back_kernel(pos, grads, *refs):
    weights, refs = refs[:NZ], refs[NZ:]
    *pieces, results = refs
    x, r, y, _ = place(pos)
    tok = grads.shape[0] // GROUP
    for s, weight in enumerate(weights):
        for half in range(2):
            result = nt(grads[...], weight[half * HEADS // 2 : (half + 1) * HEADS // 2, :])
            results[:, half * HEADS // 2 : (half + 1) * HEADS // 2] = result.astype(BF16)
        for j, (dx, dy) in enumerate(SQUARE):
            start = column_of(x ^ dx, ring(r, s), y ^ dy)
            for i, block in enumerate(TOKEN_BLOCKS):
                out = pieces[SQUARE.index(block)]
                out[:, pl.ds(start, HEAD_DIM)] = results[
                    i * tok : (i + 1) * tok, j * HEAD_DIM : (j + 1) * HEAD_DIM
                ]


def weight_back_kernel(nc, places, pos, *refs):
    for i, s in enumerate(places):
        weight_back_part(nc, s, i, pos, *refs)


def weight_back_part(nc, s, slot, pos, x_all, grads, attended, branch_all, *refs):
    attn_gain, mlp_gain, head_gains, *outs, columns, sums, out_sums = refs
    x, r, y, c = place(pos)
    rows = HEAD_DIM // nc
    base = slot * (4 * GROUP * rows + EXTRA)
    z = ring(r, s)
    gains = []
    for i, (dx, dy) in enumerate(SQUARE):
        start = column_of(x ^ dx, z, y ^ dy)
        columns[:, i * HEAD_DIM : (i + 1) * HEAD_DIM] = x_all[:, pl.ds(start, HEAD_DIM)]
        if i == 0:
            heads = pl.ds(pl.multiple_of(z * HEAD_DIM, HEAD_DIM), HEAD_DIM)
            gains.append(head_gains[0:2, heads])
        else:
            gains.append(jnp.zeros((2, HEAD_DIM), F32))
        gains.append(attn_gain[0:1, pl.ds(start, HEAD_DIM)])
        gains.append(mlp_gain[0:1, pl.ds(start, HEAD_DIM)])
    gains = jnp.concatenate(gains, axis=0)
    step = grads.shape[1] // 3
    for part in range(3):
        lanes = slice(part * step, (part + 1) * step)
        sums[:, lanes] = tn(columns[...], grads[:, lanes]).astype(BF16)
    heads = pl.ds(pl.multiple_of(z * HEAD_DIM, HEAD_DIM), HEAD_DIM)
    out_sums[...] = tn(attended[:, heads], branch_all[...]).astype(BF16)
    for k, out in enumerate(outs):
        for i in range(GROUP):
            start = pl.multiple_of(i * HEAD_DIM + (c ^ k) * rows, rows)
            for j in range(3):
                at = base + (j * GROUP + i) * rows
                lanes = slice(j * HEADS, (j + 1) * HEADS)
                out[at : at + rows] = sums[pl.ds(start, rows), lanes]
            start = pl.multiple_of((c ^ k) * rows, rows)
            at = base + (3 * GROUP + i) * rows
            lanes = slice(i * HEADS, (i + 1) * HEADS)
            out[at : at + rows] = out_sums[pl.ds(start, rows), lanes]
        chosen = 0.0
        for place_c in range(nc):
            part = gains[:, place_c * rows : (place_c + 1) * rows]
            chosen = chosen + jnp.where((c ^ k) == place_c, part, 0.0)
        chosen = jnp.concatenate([chosen, jnp.zeros((EXTRA, HEAD_DIM - rows), F32)], axis=1)
        put_extra(out, base + 4 * GROUP * rows, chosen)


def collect_kernel(count, *refs):
    parts, (grad_wo, *outs) = refs[:count], refs[count:]
    rows = (parts[0].shape[0] - EXTRA) // (4 * GROUP)

    def total(at, height, lanes=slice(None)):
        result = parts[0][at : at + height, lanes].astype(F32)
        for part in parts[1:]:
            result = result + part[at : at + height, lanes].astype(F32)
        return result

    extra = total(4 * GROUP * rows, EXTRA, slice(0, HEAD_DIM))
    for i, out in enumerate(outs):
        for j in range(3):
            part = total((j * GROUP + i) * rows, rows)
            out[:rows, j * HEADS : (j + 1) * HEADS] = part.astype(BF16)
        grad_wo[:, i * HEADS : (i + 1) * HEADS] = total((3 * GROUP + i) * rows, rows)
        put_extra(out, rows, extra_rows([extra[4 * i : 4 * i + 4]]))


def spread_kernel(pos, *refs):
    parts, (*outs, gains) = refs[:GROUP], refs[GROUP:]
    x, _, y, _ = place(pos)
    rows = parts[0].shape[0] - EXTRA
    total = 0.0
    for (dx, dy), part in zip(SQUARE, parts):
        total = total + part[rows:, :HEAD_DIM].astype(F32)
        for i, out in enumerate(outs):
            for head in range(NZ):
                start = column_of(x ^ dx, head, y ^ dy)
                at = i * HEADS + head * HEAD_DIM
                out[:, pl.ds(start, HEAD_DIM)] = part[:rows, at : at + HEAD_DIM].astype(F32)
    gains[...] = total[:8]


def take(refs, *counts):
    groups = []
    for count in counts:
        groups.append(refs[:count])
        refs = refs[count:]
    return *groups, refs


def put_columns(block, kept):
    width = kept[0].shape[1]
    for i, out in enumerate(kept):
        out[...] = block[:, i * width : (i + 1) * width]


def mlp_forward_kernel(nc, block, *refs):
    count = NY * nc
    gates, ups, downs, refs = take(refs, NX * count, NX * count, 4 * count)
    refs = refs[-(2 * nc + NY + NX + 2) :]
    products, by_gate, by_up, kept, (out, total) = take(refs, NY, nc, nc, NX)
    put_columns(block, kept)
    hidden = gates[0].shape[1]
    quarter = kept[0].shape[1] // 2
    for k in range(nc):
        for dy in range(NY):
            at = dy * nc + k
            lanes = slice(dy * hidden, (dy + 1) * hidden)

            def through(weights):
                return nn(kept[0][...], weights[at][...]) + nn(
                    kept[1][...], weights[count + at][...]
                )

            gate, up = through(gates), through(ups)
            chance = 1.0 / (1.0 + jnp.exp(-gate))
            silu = gate * chance
            product = (silu * up).astype(BF16)
            products[dy][:, k * hidden : (k + 1) * hidden] = product
            by_up[k][:, lanes] = silu.astype(BF16)
            by_gate[k][:, lanes] = (up * (chance + silu * (1.0 - chance))).astype(BF16)
            for i in range(4):
                columns = slice(i * quarter, (i + 1) * quarter)
                part = nt(product, downs[i * count + at][...])
                total[:, columns] = part if k + dy == 0 else total[:, columns] + part
    out[...] = total[...]


def mlp_back_kernel(nc, block, *refs):
    count = NY * nc
    gates, ups, downs, by_gate, by_up, refs = take(
        refs, NX * count, NX * count, 4 * count, nc, nc
    )
    refs = refs[-(2 * nc + NX + 2) :]
    grad_gates, grad_ups, kept, (out, total) = take(refs, nc, nc, NX)
    put_columns(block, kept)
    hidden = gates[0].shape[1]
    quarter = kept[0].shape[1] // 2
    for k in range(nc):
        for dy in range(NY):
            at = dy * nc + k
            lanes = slice(dy * hidden, (dy + 1) * hidden)
            grad = 0.0
            for i in range(4):
                columns = slice((i % 2) * quarter, (i % 2 + 1) * quarter)
                grad = grad + nn(kept[i // 2][:, columns], downs[i * count + at][...])
            grad_gate = (grad * by_gate[k][:, lanes].astype(F32)).astype(BF16)
            grad_up = (grad * by_up[k][:, lanes].astype(F32)).astype(BF16)
            grad_gates[k][:, lanes] = grad_gate
            grad_ups[k][:, lanes] = grad_up
            for i in range(4):
                columns = slice(i * quarter, (i + 1) * quarter)
                rows = slice((i % 2) * quarter, (i % 2 + 1) * quarter)
                weight = (i // 2) * count + at
                part = nt(grad_gate, gates[weight][rows, :]) + nt(grad_up, ups[weight][rows, :])
                total[:, columns] = part if k + dy == 0 else total[:, columns] + part
    out[...] = total[...]


def down_back_kernel(*refs):
    *parts, out = refs
    count = len(parts) // 3
    near, far, products, _ = take(parts, count, count, count)
    tok = near[0].shape[0]
    step = out.shape[0] // 2
    for i in range(2):
        rows = slice(i * step, (i + 1) * step)
        for j, product in enumerate(products):
            part = tn(near[j][:, rows], product[:tok]) + tn(far[j][:, rows], product[tok:])
            out[rows, :] = part if j == 0 else out[rows, :] + part


def make_body(wide):
    nc = wide // (NY * NZ)

    def send(value, x=0, y=0, r=0, c=0):
        pairs = []
        for sx in range(NX):
            for sz in range(NZ):
                for sy in range(NY):
                    for sc in range(nc):
                        source = sx * wide + (sz * NY + sy) * nc + sc
                        target = (sx ^ x) * wide
                        target += (ring(gray(sz), r) * NY + (sy ^ y)) * nc + (sc ^ c)
                        pairs.append((source, target))
        return lax.ppermute(value, AXES, pairs)

    def square(parts):
        return [
            part if (dx, dy) == (0, 0) else send(part, x=dx, y=dy)
            for (dx, dy), part in zip(SQUARE, parts)
        ]

    def square_gather(first, second):
        first_x = send(first, x=1)
        second_y = send(second, y=1)
        first_y = send(first, y=1)
        second_x = send(second, x=1)
        first_xy = send(first_x, y=1)
        second_xy = send(second_y, x=1)
        return [first, first_y, first_x, first_xy], [second, second_y, second_x, second_xy]

    def scatter_far(first, second):
        return send(first[3], x=1), send(second[3], y=1)

    def scatter_near(first, second):
        return send(first[2], x=1), send(second[1], y=1)

    def scatter_last(first, second, far, near):
        return (
            send((first[1].astype(F32) + far[0].astype(F32)).astype(BF16), y=1),
            send((second[2].astype(F32) + far[1].astype(F32)).astype(BF16), x=1),
        )

    def scatter_sum(first, second, near, last):
        return (
            first[0].astype(F32) + near[0].astype(F32) + last[0].astype(F32),
            second[0].astype(F32) + near[1].astype(F32) + last[1].astype(F32),
        )

    def core_gather(block):
        return [block] + [send(block, c=k) for k in range(1, nc)]

    def core_sums(blocks, hidden):
        sums = []
        for row in blocks:
            total = row[0].astype(F32)
            for k in range(1, nc):
                total = total + send(row[k], c=k).astype(F32)
            total = total.astype(BF16)
            sums += [total[:, dy * hidden : (dy + 1) * hidden] for dy in range(NY)]
        return sums

    def core_parts(parts):
        return [parts[0]] + [send(parts[k], c=k) for k in range(1, nc)]

    def body(
        layer_input,
        lengths,
        w_query,
        w_key,
        w_value,
        w_output,
        query_gain,
        key_gain,
        attn_gain,
        mlp_gain,
        w_gate,
        w_up,
        w_down,
        grad_output,
    ):
        due = {}

        def mark(name, value):
            due.setdefault(PLAN[name], []).append(value)
            return value

        def at(point, value):
            ready = due.pop(point, [])
            return after(value, ready) if ready else value

        x = lax.axis_index("blk")
        spot = lax.axis_index("wide")
        z, y, c = spot // (NY * nc), (spot // nc) % NY, spot % nc
        inputs, grad_out = layer_input[0], grad_output[0]
        tok, width = inputs.shape
        rows = w_query.shape[0]
        group_tok = GROUP * tok
        hidden = w_gate.shape[1]
        pos = jnp.stack([x, gray(z), y, c, lengths[0]]).astype(jnp.int32)
        wide_small = shaped((8, width), F32)
        by_head = shaped((group_tok, HEADS))
        by_head_wide = shaped((group_tok, HEADS), F32)
        by_token = shaped((8, group_tok), F32)
        tokens_shape = shaped((tok, width))
        tokens_wide = shaped((tok, width), F32)
        message = shaped((4 * GROUP * rows + EXTRA, HEADS))
        piece = shaped((rows + EXTRA, 3 * HEADS))

        def group_sum(stats, *ready):
            blocks = [stats[:, i * tok : (i + 1) * tok] for i in range(GROUP)]
            for flip, way in ((1, {"x": 1}), (2, {"y": 1})):
                total = jnp.concatenate(blocks, axis=1)
                if flip == 2 and ready:
                    total = after(total, ready)
                got = send(total, **way)
                got = [got[:, i * tok : (i + 1) * tok] for i in range(GROUP)]
                blocks = [block + got[i ^ flip] for i, block in enumerate(blocks)]
            return jnp.concatenate(blocks, axis=1)

        def dma(count):
            return pltpu.SemaphoreType.DMA((count,))

        def held(shape):
            return pltpu.VMEM(shape.shape, shape.dtype)

        gains = jnp.stack([query_gain, key_gain, attn_gain, mlp_gain])
        pieces = run(
            split_kernel,
            each([piece] * GROUP, VMEM),
            [(pos, SMEM), (gains, VMEM), (w_query, auto), (w_key, auto), (w_value, auto)],
        )
        down_rows = w_down.shape[0] // 2
        down_halves = w_down[:down_rows], w_down[down_rows:]
        far_down = send(down_halves[0], x=1), send(down_halves[1], y=1)
        mark("far_down", far_down)
        received = at("join", square(pieces))
        own_rows, lengths_row = run(
            join_kernel,
            [(message, VMEM), (shaped((8, HEAD_DIM), F32), VMEM)],
            each((*received, w_output), VMEM),
        )
        lane = jnp.arange(HEAD_DIM)[None, :]
        row = jnp.arange(NX * tok)[:, None]
        row = jnp.where(row < tok, x * tok + row, (1 - x) * tok + row - tok).astype(F32)
        half = HEAD_DIM // 2
        frequency = jnp.exp((lane % half).astype(F32) * (-2.0 * math.log(500000.0) / HEAD_DIM))
        cosine = jnp.cos(row * frequency)
        sine = jnp.sin(row * jnp.where(lane < half, -frequency, frequency))
        mark("turns", (cosine, sine))
        w_ring = [own_rows, send(own_rows, r=-1)]
        half_tok = tok // 2
        if PLAN["tokens_first"]:
            from_x = send(after(inputs, own_rows), x=1)
            from_y = send(after(inputs, own_rows), y=1)
            from_xy = send(from_x[:half_tok], y=1), send(from_y[half_tok:], x=1)
            early = {"xy": from_xy, "x": (from_x, from_y)}[PLAN["far_from"]]
            far_gate = send(after(w_gate, early), x=1)
            far_up = send(after(w_up, early), y=1)
            near_gate = send(after(w_gate, far_up), y=1)
            near_up = send(after(w_up, far_gate), x=1)
        else:
            far_gate = send(after(w_gate, own_rows), x=1)
            far_up = send(after(w_up, own_rows), y=1)
            from_x = send(after(inputs, far_gate), x=1)
            from_y = send(after(inputs, far_up), y=1)
            from_xy = send(from_x[:half_tok], y=1), send(from_y[half_tok:], x=1)
            near_gate = send(after(w_gate, from_xy[0]), y=1)
            near_up = send(after(w_up, from_xy[1]), x=1)
        mark("far", (far_gate, far_up))
        mark("tokens", (from_x, from_y))
        mark("tokens_xy", from_xy)
        mark("near", (near_gate, near_up))
        own_gate, own_up = core_gather(w_gate), core_gather(w_up)
        own_down = core_gather(w_down)
        far_gate, far_up = core_gather(far_gate), core_gather(far_up)
        far_down = core_gather(far_down[0]), core_gather(far_down[1])
        mark("own_gate_c", (own_gate, own_up))
        mark("own_down_c", own_down)
        mark("far_c", (far_gate, far_up))
        mark("far_down_c", far_down)
        first_blocks = core_gather(own_rows)
        w_ring.append(send(at("w2", w_ring[1]), r=-1))
        second_blocks = core_gather(w_ring[1])
        w_ring.append(send(at("w3", w_ring[2]), r=-1))
        x_all, x_kept = run(
            gather_kernel,
            [(shaped((group_tok, width)), VMEM), (shaped((group_tok, width)), HBM)],
            each([inputs, from_x, from_y, *from_xy], VMEM),
            scratch_shapes=[pltpu.SemaphoreType.DMA],
        )
        w_shape = shaped((GROUP * HEAD_DIM, 3 * HEADS))
        by_three = shaped((group_tok, 3 * HEADS), F32)
        out_shape = shaped((HEADS, width))

        def project(places, blocks, before, outs):
            ins = [(pos, SMEM), (x_all, VMEM), *each(blocks, VMEM), *each(before, VMEM)]
            depth = len(places) * GROUP * HEAD_DIM
            return run(
                functools.partial(project_kernel, nc, places),
                [(wide_small, VMEM), (out_shape, VMEM)] + [(w_shape, HBM)] * len(places) + outs,
                ins,
                limit=16,
                input_output_aliases={len(ins) - 2: 0, len(ins) - 1: 1} if before else {},
                scratch_shapes=[
                    pltpu.VMEM((group_tok, depth), BF16),
                    pltpu.VMEM((depth, 3 * HEADS), BF16),
                    dma(len(places) + 4),
                ],
            )

        blocks = first_blocks + second_blocks + core_gather(w_ring[2])
        gains, out_w, *w_parts, total = project((0, 1, 2), blocks, (), [(by_three, VMEM)])
        mark("total", total)
        last_block = core_gather(at("c3", w_ring[3]))
        near_down = (
            send(after(down_halves[0], near_gate), y=1),
            send(after(down_halves[1], near_up), x=1),
        )
        mark("near_down", near_down)
        near_gate, near_up = core_gather(near_gate), core_gather(near_up)
        mark("near_c", (near_gate, near_up))
        gains, out_w, w_part, query, key, value, query_h, key_h, value_h, out_kept, stats = project(
            (3,),
            last_block,
            (total, gains, out_w),
            [(by_head_wide, VMEM), (by_head_wide, VMEM), (by_head, VMEM)]
            + [(by_head_wide, HBM), (by_head_wide, HBM), (by_head, HBM)]
            + [(out_shape, HBM), (by_token, VMEM)],
        )
        w_parts.append(w_part)
        early = {"near": near_gate[0]}
        group_stats = at("stats2", group_sum(at("stats", stats)))
        early["stats"] = group_stats
        last_gate = send(after(far_gate[0], early[PLAN["last_from"]], near_gate[0]), y=1)
        last_up = send(after(far_up[0], early[PLAN["last_from"]], near_up[0]), x=1)
        mark("last", (last_gate, last_up))
        last_gate, last_up = core_gather(last_gate), core_gather(last_up)
        mark("last_c", (last_gate, last_up))
        gate_w = [*own_gate, *near_gate, *far_gate, *last_gate]
        up_w = [*own_up, *far_up, *near_up, *last_up]
        near_down = core_gather(near_down[0]), core_gather(near_down[1])
        mark("near_down_c", near_down)

        query_r, key_r, attended, scales, *parts = run(
            attend_kernel,
            [(by_head, HBM)] * 3 + [(by_token, VMEM)] + [(tokens_shape, VMEM)] * GROUP,
            [
                (pos, SMEM),
                (group_stats, VMEM),
                *each((lengths_row, gains, cosine, sine), VMEM),
                *each((query, key, value, out_w), VMEM),
            ],
            scratch_shapes=[held(by_head), held(by_head), held(by_head), dma(3)],
        )
        parts = square(at("rs", parts))
        first_x, second_y = far_down
        last_down = (
            core_gather(send(after(first_x[0], parts), y=1)),
            core_gather(send(after(second_y[0], parts), x=1)),
        )
        own_first = [part[:down_rows] for part in own_down]
        own_second = [part[down_rows:] for part in own_down]
        down_first = own_first, near_down[0], first_x, last_down[0]
        down_second = own_second, second_y, near_down[1], last_down[1]
        down_w = [
            piece
            for dx in range(NX)
            for half in (down_first, down_second)
            for dy in range(NY)
            for piece in half[dx * NY + dy]
        ]
        branch, hidden_state, mlp_in = run(
            branch_kernel,
            [(tokens_wide, auto), (tokens_wide, auto), (tokens_shape, VMEM)],
            [(pos, SMEM), *each(at("k4", parts), auto), (inputs, auto), (gains, VMEM)],
        )

        half_width = width // NX
        quarter = half_width // 2

        def mlp_call(kernel, s, block, extra, narrow, before):
            def rows_of(array):
                count = array.shape[0] // tok
                return pl.BlockSpec((tok, array.shape[1]), lambda i: (s % count, 0))

            ins = each((block, *gate_w, *up_w, *down_w), VMEM) + each(extra, rows_of)
            columns, height = narrow
            outs = [shaped((NZ * tok, count)) for count in columns]
            outs = each(outs + [shaped((height, half_width))] * NX, rows_of)
            aliases = {}
            if before is not None:
                aliases = {len(ins) + i: i for i in range(len(before))}
                ins += each(before, HBM)
            *kept, total = run(
                functools.partial(kernel, nc),
                [*outs, (tokens_wide, VMEM)],
                ins,
                input_output_aliases=aliases,
                scratch_shapes=[held(tokens_wide)],
            )
            return kept, total

        def summed(parts):
            total = parts[0].astype(F32)
            for part in parts[1:]:
                total = total + part.astype(F32)
            return total

        def mlp_pass(name, kernel, block, extra, columns, height):
            narrow = columns, height
            near = send(block, r=-1)
            middle = send(near, r=-1)
            kept, first = mlp_call(kernel, 1, at(name + "1", near), extra, narrow, None)
            far = send(after(middle, first) if PLAN[name + "_lead"] else middle, r=-1)
            sent = [first.astype(BF16)]
            moving = send(sent[0], r=-1)
            kept, own = mlp_call(kernel, 0, block, extra, narrow, kept)
            early = []
            if height < NZ * tok:
                early, kept = kept[-NX:], kept[:-NX]
                early = square([early[dx] for dx, dy in SQUARE])
                mark("near_grads", early[1:3])
                mark("near_grads_xy", early[3])
            middle = at(name + "2", middle)
            if PLAN[name + "_out"]:
                middle = after(middle, sent[0])
            kept, second = mlp_call(kernel, 2, middle, extra, narrow, kept)
            far = at(name + "3", far)
            if PLAN[name + "_hold"]:
                far = after(far, moving)
            kept, third = mlp_call(kernel, 3, far, extra, narrow, kept)
            sent.append(summed([second, moving]).astype(BF16))
            sent.append(summed([third, send(sent[1], r=-1)]).astype(BF16))
            parts = [own, send(at(name + "4", sent[2]), r=-1)]
            return kept, parts, sent, early

        columns = [nc * hidden] * NY + [NY * hidden] * 2 * nc
        kept, parts, sent, _ = mlp_pass(
            "f", mlp_forward_kernel, mlp_in, (), columns, NZ * tok
        )
        products, by_gate, by_up, mlp_all = take(kept, NY, nc, nc)

        got_products = square([after(products, sent[PLAN["products_from"]])[dy] for dx, dy in SQUARE])
        mark("products", got_products[1:3])
        mark("products_xy", got_products[3])
        output, grad_mlp, grad_gain_mlp = run(
            functools.partial(mlp_kernel, len(parts)),
            [(tokens_shape, auto), (tokens_shape, VMEM), (wide_small, VMEM)],
            [
                (pos, SMEM),
                *each(at("m1", parts), auto),
                (hidden_state, auto),
                (gains, VMEM),
                (grad_out, auto),
            ],
            scratch_shapes=[held(tokens_wide)] * 2,
        )
        extra = *by_gate, *by_up
        columns = [NY * hidden] * 2 * nc
        kept, parts, sent, near_grads = mlp_pass(
            "b", mlp_back_kernel, grad_mlp, extra, columns, 2 * tok
        )
        grad_gates, grad_ups, grad_all = take(kept, nc, nc)
        grad_hidden, grad_branch, grad_gain_attn = run(
            functools.partial(branch_back_kernel, len(parts)),
            [(tokens_wide, auto), (tokens_shape, VMEM), (wide_small, VMEM)],
            [
                (pos, SMEM),
                *each(at("k9", parts), auto),
                (branch, auto),
                (gains, VMEM),
                (grad_out, auto),
            ],
            scratch_shapes=[held(tokens_wide)] * 2,
        )

        def products_of(left, right):
            return [[tn(block, grad).astype(BF16) for grad in right] for block in left]

        early = {"branch": grad_branch, "sent": sent[2]}
        if PLAN["far_grads_from"] in early:
            far_grads = after(grad_all, early[PLAN["far_grads_from"]])
            far_grads = square([far_grads[dx] for dx, dy in SQUARE])
            mark("far_grads", far_grads[1:3])
            mark("far_grads_xy", far_grads[3])
        blocks = square([at("ag", grad_branch)] * GROUP)
        early.update({"block": blocks[1], "all": blocks})
        mlp_all = after(mlp_all, early[PLAN["dots_from"]])
        wg_blocks = products_of(mlp_all, grad_gates)
        wu_blocks = products_of(mlp_all, grad_ups)
        mark("dots", (wg_blocks, wu_blocks))
        if PLAN["far_grads_from"] in ("block", "all"):
            far_grads = after(grad_all, early[PLAN["far_grads_from"]])
            far_grads = square([far_grads[dx] for dx, dy in SQUARE])
            mark("far_grads", far_grads[1:3])
            mark("far_grads_xy", far_grads[3])
        blocks = at("blocks", blocks)
        if PLAN["sums_late"]:
            wg_blocks, wu_blocks = after((wg_blocks, wu_blocks), blocks)
        w_pair = core_sums(wg_blocks, hidden), core_sums(wu_blocks, hidden)
        mark("sums", w_pair)
        grad_query, grad_key, grad_value, stats, head_gains, branch_all = run(
            attend_back_kernel,
            [
                (by_head_wide, VMEM),
                (by_head_wide, VMEM),
                (by_head, VMEM),
                (by_token, VMEM),
                (shaped((8, HEADS), F32), VMEM),
                (shaped((group_tok, width)), VMEM),
            ],
            [
                (pos, SMEM),
                *each((lengths_row, scales, gains, cosine, sine, out_kept, *blocks), VMEM),
                *each((query_r, key_r, value_h, query_h, key_h), HBM),
            ],
            limit=16,
            scratch_shapes=[
                held(by_head),
                held(by_head),
                held(by_head),
                held(by_head_wide),
                held(by_head_wide),
                held(by_head_wide),
                held(by_head_wide),
                held(by_head),
                dma(5),
            ],
        )
        (grads,) = run(
            project_back_kernel,
            [(shaped((group_tok, 3 * HEADS)), VMEM)],
            [
                (at("g2", group_sum(at("g1", stats))), VMEM),
                (scales, VMEM),
                *each((grad_query, grad_key, grad_value, query_h, key_h), VMEM),
            ],
        )
        w_far = scatter_far(*(after(w_pair, grads) if PLAN["w_far_late"] else w_pair))
        w_near = scatter_near(*after(w_pair, w_far))
        w_last = scatter_last(*w_pair, after(w_far, w_near) if PLAN["w_last_late"] else w_far, w_near)
        mark("w_far", w_far)
        mark("w_near", w_near)
        mark("w_last", w_last)

        def weight_parts(places):
            height = message.shape[0]
            results = run(
                functools.partial(weight_back_kernel, nc, places),
                [(shaped((len(places) * height, HEADS)), VMEM)] * nc,
                [
                    (pos, SMEM),
                    *each((x_kept, grads, attended, branch_all), VMEM),
                    *each((grad_gain_attn, grad_gain_mlp, head_gains), VMEM),
                ],
                scratch_shapes=[
                    pltpu.VMEM((group_tok, GROUP * HEAD_DIM), BF16),
                    pltpu.VMEM((GROUP * HEAD_DIM, 3 * HEADS), BF16),
                    pltpu.VMEM((HEAD_DIM, width), BF16),
                ],
            )
            results = core_parts(results)
            return [
                [part[i * height : (i + 1) * height] for part in results]
                for i in range(len(places))
            ]

        (first,) = weight_parts((1,))
        factors = []
        for *grads_of, product in zip(near_grads, far_grads, got_products):
            for k in range(nc):
                pieces = *grads_of, product[:, k * hidden : (k + 1) * hidden]
                factors.append([send(piece, c=k) if k else piece for piece in pieces])
        mark("factors", factors)
        (grad_wd,) = run(
            down_back_kernel,
            [(shaped(w_down.shape, F32), VMEM)],
            each([entry[i] for i in range(3) for entry in factors], VMEM),
        )

        mark("grad_wd", grad_wd)
        w_moving = send(at("w1", summed(first).astype(BF16)), r=-1)
        early = {"first": first, "far": w_far, "none": (), "both": (first, w_far)}
        grads = after(grads, early[PLAN["second_after"]])
        second, third, own = weight_parts((2, 3, 0))
        x_parts = run(
            input_back_kernel,
            [(tokens_shape, VMEM)] * GROUP,
            [(pos, SMEM), (after(grads, own), VMEM), *each(w_parts, VMEM)],
            scratch_shapes=[pltpu.VMEM((group_tok, GROUP * HEAD_DIM), BF16)],
        )
        mark("x_parts", x_parts)
        early = {"parts": x_parts, "near": w_near, "last": w_last}
        from_x = [x_parts[0]] + square([x_parts[0], *after(x_parts[1:3], early[PLAN["x_from"]]), x_parts[3]])[1:3]
        mark("x_sums", from_x)
        sent = summed(second + [w_moving]).astype(BF16)
        w_moving = send(after(at("t2", sent), own), r=-1)
        sent = summed(third + [w_moving]).astype(BF16)
        w_moving = send(at("t3", sent), r=-1)
        grad_wg, grad_wu = scatter_sum(*w_pair, w_near, w_last)
        parts = at("collect", own + [w_moving])
        grad_wo, *messages = run(
            functools.partial(collect_kernel, len(parts)),
            [(shaped((rows, width), F32), auto)] + [(piece, VMEM)] * GROUP,
            each(parts, auto),
        )
        grad_wq, grad_wk, grad_wv, total_gains = run(
            spread_kernel,
            [(shaped((rows, width), F32), auto)] * 3 + [(shaped((8, HEAD_DIM), F32), VMEM)],
            [(pos, SMEM), *each(at("spread", square(messages)), auto)],
        )
        early = {"messages": messages, "parts": x_parts, "sent": from_x[1:]}
        last_x = send(after(x_parts[3], early[PLAN["x_last_from"]]), x=1, y=1)
        grad_x = summed([grad_hidden, *from_x, last_x])

        return (
            output[None],
            grad_x.astype(BF16)[None],
            grad_wq,
            grad_wk,
            grad_wv,
            grad_wo,
            total_gains[0, :rows],
            total_gains[1, :rows],
            total_gains[2, :rows],
            total_gains[3, :rows],
            grad_wg,
            grad_wu,
            grad_wd,
        )

    return body


def solution(mesh):
    return jax.shard_map(
        make_body(mesh.shape["wide"]),
        mesh=mesh,
        in_specs=(
            P("wide", "blk", None),
            P("wide"),
            P(("blk", "wide"), None),
            P(("blk", "wide"), None),
            P(("blk", "wide"), None),
            P(("blk", "wide"), None),
            P(("blk", "wide")),
            P(("blk", "wide")),
            P(("blk", "wide")),
            P(("blk", "wide")),
            P("blk", "wide"),
            P("blk", "wide"),
            P("blk", "wide"),
            P("wide", "blk", None),
        ),
        out_specs=(
            P("wide", "blk", None),
            P("wide", "blk", None),
            P(("blk", "wide"), None),
            P(("blk", "wide"), None),
            P(("blk", "wide"), None),
            P(("blk", "wide"), None),
            P(("blk", "wide")),
            P(("blk", "wide")),
            P(("blk", "wide")),
            P(("blk", "wide")),
            P("blk", "wide"),
            P("blk", "wide"),
            P("blk", "wide"),
        ),
        check_vma=False,
    )
```

```python
import enum
import functools
import math

import jax
import jax.numpy as jnp
from jax import lax
from jax.experimental import pallas as pl
from jax.experimental.pallas import tpu as pltpu
from jax.sharding import PartitionSpec as P

HEAD_DIM = 128
EPSILON = 1e-06
NEGATIVE = -1e30
BF16 = jnp.bfloat16
F32 = jnp.float32
AXES = ("blk", "wide")
NX, NY, NZ = 2, 2, 4
GROUP = NX * NY
HEADS = NZ * HEAD_DIM
MIB = 1 << 20
SMEM = pl.BlockSpec(memory_space=pltpu.SMEM)
VMEM = pl.BlockSpec(memory_space=pltpu.VMEM)
HBM = pl.BlockSpec(memory_space=pltpu.HBM)
EXTRA = 16
class Point(enum.IntEnum):
    JOIN = 0
    RING_2 = 1
    RING_3 = 2
    LAST_ROWS = 3
    STATS = 4
    SCALES = 5
    BRANCH_SEND = 6
    BRANCH = 7
    F1 = 8
    F2 = 9
    F3 = 10
    F4 = 11
    MLP_OUT = 12
    B1 = 13
    B2 = 14
    B3 = 15
    B4 = 16
    MIDDLE = 17
    BRANCH_BACK = 18
    ATTEND_BACK = 19
    STATS_BACK = 20
    PROJECT_BACK = 21
    SUM_1 = 22
    SUM_2 = 23
    SUM_3 = 24
    COLLECT = 25
    SPREAD = 26
    NEVER = 27


class Due:
    far_down = Point.JOIN
    turns = Point.RING_2
    far = Point.RING_3
    tokens = Point.RING_2
    tokens_xy = Point.RING_2
    near = Point.LAST_ROWS
    own_gate_c = Point.RING_3
    own_down_c = Point.LAST_ROWS
    far_c = Point.LAST_ROWS
    far_down_c = Point.STATS
    total = Point.LAST_ROWS
    near_down = Point.BRANCH
    near_c = Point.BRANCH_SEND
    last = Point.BRANCH_SEND
    last_c = Point.F1
    near_down_c = Point.BRANCH_SEND
    near_grads = Point.B3
    near_grads_xy = Point.B4
    products = Point.B1
    products_xy = Point.B2
    far_grads = Point.BRANCH_BACK
    far_grads_xy = Point.STATS_BACK
    dots = Point.ATTEND_BACK
    sums = Point.STATS_BACK
    w_far = Point.SUM_2
    w_near = Point.COLLECT
    w_last = Point.COLLECT
    factors = Point.COLLECT
    grad_wd = Point.COLLECT
    x_parts = Point.SUM_3
    x_sums = Point.SPREAD

SQUARE = [(dx, dy) for dx in range(NX) for dy in range(NY)]
TOKEN_BLOCKS = [(dx, dy) for dy in range(NY) for dx in range(NX)]


def shaped(shape, dtype=BF16):
    return jax.ShapeDtypeStruct(tuple(shape), dtype)


def nn(left, right):
    return lax.dot_general(left, right, (((1,), (0,)), ((), ())), preferred_element_type=F32)


def nt(left, right):
    return lax.dot_general(left, right, (((1,), (1,)), ((), ())), preferred_element_type=F32)


def tn(left, right):
    return lax.dot_general(left, right, (((0,), (0,)), ((), ())), preferred_element_type=F32)


def auto(array):
    return pl.BlockSpec(array.shape, lambda i: (0,) * len(array.shape))


def run(body, outs, ins, limit=12, **options):
    return pl.pallas_call(
        body,
        grid=(1,),
        out_shape=[
            pltpu.HBM(out.shape, out.dtype) if spec is HBM else out for out, spec in outs
        ],
        out_specs=[spec if isinstance(spec, pl.BlockSpec) else spec(out) for out, spec in outs],
        in_specs=[spec if isinstance(spec, pl.BlockSpec) else spec(array) for array, spec in ins],
        compiler_params=pltpu.CompilerParams(vmem_limit_bytes=limit * MIB),
        cost_estimate=pl.CostEstimate(flops=0, bytes_accessed=0, transcendentals=0),
        **options,
    )(*[array for array, _ in ins])


def each(arrays, spec):
    return [(array, spec) for array in arrays]


def after(value, *others):
    return lax.optimization_barrier((value, others))[0]


class Copies:
    def __init__(self, sems):
        self.sems, self.count = sems, 0

    def start(self, source, target):
        copy = pltpu.make_async_copy(source, target, self.sems.at[self.count])
        self.count += 1
        copy.start()
        return copy


def finish(copies):
    for copy in copies:
        copy.wait()


def place(pos):
    return pos[0], pos[1], pos[2], pos[3]


def gray(index):
    return index ^ (index >> 1)


def ring(r, s):
    return gray((r + s) % NZ)


def column_of(x, z, y):
    return pl.multiple_of(((x * NZ + z) * NY + y) * HEAD_DIM, HEAD_DIM)


def extra_rows(blocks):
    used = sum(block.shape[0] for block in blocks)
    if used < EXTRA:
        blocks = [*blocks, jnp.zeros((EXTRA - used, HEAD_DIM), F32)]
    return jnp.concatenate(blocks, axis=0)


def put_extra(out, start, values):
    out[start : start + EXTRA, :HEAD_DIM] = values.astype(BF16)
    out[start : start + EXTRA, HEAD_DIM:] = jnp.zeros((EXTRA, out.shape[1] - HEAD_DIM), BF16)


def split_kernel(pos, gains, w_query, w_key, w_value, *outs):
    x, _, y, _ = place(pos)
    rows = w_query.shape[0]
    own = gains[...].astype(F32)
    own = jnp.concatenate([own, jnp.zeros((4, HEAD_DIM - rows), F32)], axis=1)
    length = jnp.full((1, HEAD_DIM), pos[4]).astype(F32)
    for (dx, dy), out in zip(SQUARE, outs):
        for i, weight in enumerate((w_query, w_key, w_value)):
            for head in range(NZ):
                start = column_of(x ^ dx, head, y ^ dy)
                at = i * HEADS + head * HEAD_DIM
                out[:rows, at : at + HEAD_DIM] = weight[:, pl.ds(start, HEAD_DIM)]
        put_extra(out, rows, extra_rows([own, length]))


def join_kernel(*refs):
    *parts, w_output, out, lengths = refs
    rows = parts[0].shape[0] - EXTRA
    extras = []
    for i, part in enumerate(parts):
        for j in range(3):
            at = (j * GROUP + i) * rows
            out[at : at + rows] = part[:rows, j * HEADS : (j + 1) * HEADS]
        at = (3 * GROUP + i) * rows
        out[at : at + rows] = w_output[:, i * HEADS : (i + 1) * HEADS]
        extras.append(part[rows:, :HEAD_DIM].astype(F32))
    put_extra(out, 4 * GROUP * rows, extra_rows([extra[:4] for extra in extras]))
    lengths[...] = jnp.concatenate(
        [extras[0][4:5], extras[1][4:5], jnp.zeros((6, HEAD_DIM), F32)], axis=0
    )


def row_stats(first, second):
    shape = (first.shape[0], HEAD_DIM)
    upper = lax.broadcasted_iota(jnp.int32, shape, 1) < 4
    sums = jnp.where(
        upper,
        jnp.sum(first, axis=1, keepdims=True),
        jnp.sum(second, axis=1, keepdims=True),
    )
    return jnp.transpose(sums)[:8]


def gather_kernel(*refs):
    blocks, (whole, kept, sem) = refs[:-3], refs[-3:]
    start = 0
    for block in blocks:
        whole[start : start + block.shape[0]] = block[...]
        start += block.shape[0]
    copy = pltpu.make_async_copy(whole, kept, sem)
    copy.start()
    copy.wait()


def project_kernel(nc, places, pos, x_all, *refs):
    weights, refs = refs[: nc * len(places)], refs[nc * len(places) :]
    last = places[-1] == NZ - 1
    if last:
        before, _, _, *refs = refs
    gains, out_w, *refs = refs
    w_rows, refs = refs[: len(places)], refs[len(places) :]
    if last:
        query, key, value, query_h, key_h, value_h, out_kept, stats, *refs = refs
    else:
        total, *refs = refs
    columns, w_part, sems = refs
    x, r, y, c = place(pos)
    rows = (weights[0].shape[0] - EXTRA) // (4 * GROUP)
    copies = Copies(sems)
    put = []
    for slot, s in enumerate(places):
        blocks = weights[slot * nc : (slot + 1) * nc]
        z = ring(r, s)
        extras = [block[4 * GROUP * rows :, :HEAD_DIM].astype(F32) for block in blocks]
        lanes = []
        for place_c in range(nc):
            chosen = 0.0
            for k, part in enumerate(extras):
                chosen = chosen + jnp.where((c ^ k) == place_c, part[:, :rows], 0.0)
            lanes.append(chosen)
        ordered = jnp.concatenate(lanes, axis=1)
        base = slot * GROUP * HEAD_DIM
        for i, (dx, dy) in enumerate(SQUARE):
            start = column_of(x ^ dx, z, y ^ dy)
            gains[:, pl.ds(start, HEAD_DIM)] = jnp.concatenate(
                [ordered[4 * i : 4 * i + 4], jnp.zeros((4, HEAD_DIM), F32)], axis=0
            )
            to = base + i * HEAD_DIM
            columns[:, to : to + HEAD_DIM] = x_all[:, pl.ds(start, HEAD_DIM)]
            for k, block in enumerate(blocks):
                at = pl.multiple_of(to + (c ^ k) * rows, rows)
                for j in range(3):
                    got = (j * GROUP + i) * rows
                    lanes = slice(j * HEADS, (j + 1) * HEADS)
                    w_part[pl.ds(at, rows), lanes] = block[got : got + rows]
                got = (3 * GROUP + i) * rows
                at = pl.multiple_of(z * HEAD_DIM + (c ^ k) * rows, rows)
                lanes = slice(i * HEADS, (i + 1) * HEADS)
                out_w[pl.ds(at, rows), lanes] = block[got : got + rows]
        put.append(
            copies.start(w_part.at[pl.ds(base, GROUP * HEAD_DIM)], w_rows[slot])
        )
    step = HEADS // 2
    for part in range(6):
        at = slice(part * step, (part + 1) * step)
        result = nn(columns[...], w_part[:, at])
        if last:
            result = before[:, at] + result
            out = (query, key, value)[part // 2]
            out[:, (part % 2) * step : (part % 2 + 1) * step] = result.astype(out.dtype)
        else:
            total[:, at] = result
    if last:
        stats[...] = row_stats(query[...] * query[...], key[...] * key[...])
        put += [
            copies.start(*pair)
            for pair in ((query, query_h), (key, key_h), (value, value_h), (out_w, out_kept))
        ]
    finish(put)


def turn(values, cosine, sine):
    return values * cosine + pltpu.roll(values, HEAD_DIM // 2, 1) * sine


def valid_keys(x, length, tok):
    shape = (NX * tok, NX * tok)
    queries = lax.broadcasted_iota(jnp.int32, shape, 0)
    keys = lax.broadcasted_iota(jnp.int32, shape, 1)

    def at(index):
        return jnp.where(index < tok, x * tok + index, (1 - x) * tok + index - tok)

    return (at(keys) <= at(queries)) & (at(keys).astype(F32) < length)


def softmax(query, key, valid):
    logits = jnp.where(valid, nt(query, key) * HEAD_DIM ** (-0.5), NEGATIVE)
    powers = jnp.exp(logits - jnp.max(logits, axis=1, keepdims=True))
    return powers / jnp.sum(powers, axis=1, keepdims=True)


def attend_kernel(pos, *refs):
    x, _, y, _ = place(pos)
    stats, *refs = refs
    lengths, gains, cosine, sine, query, key, value, out_w, *refs = refs
    query_out, key_out, attended_out, scales, *refs = refs
    pieces, refs = refs[:GROUP], refs[GROUP:]
    query_r, key_r, attended, sems = refs
    copies = Copies(sems)
    tok = query.shape[0] // GROUP
    span = NX * tok
    width = out_w.shape[1]
    scale = lax.rsqrt(stats[...] / width + EPSILON)
    scales[...] = scale
    for seq in range(NY):
        at = slice(seq * span, (seq + 1) * span)
        columns = jnp.transpose(scale[:, at])
        valid = valid_keys(x, lengths[seq : seq + 1, 0:1], tok)
        for head in range(NZ):
            lanes = slice(head * HEAD_DIM, (head + 1) * HEAD_DIM)
            gain = pl.ds(column_of(x, head, y), HEAD_DIM)
            for row, (raw, out) in enumerate(((query, query_r), (key, key_r))):
                normed = raw[at, lanes] * columns[:, 4 * row : 4 * row + 1]
                normed = normed * gains[row : row + 1, gain]
                out[at, lanes] = turn(normed, cosine[...], sine[...]).astype(BF16)
            chances = softmax(query_r[at, lanes], key_r[at, lanes], valid)
            attended[at, lanes] = nn(chances.astype(BF16), value[at, lanes]).astype(BF16)
    put = [
        copies.start(*pair)
        for pair in ((query_r, query_out), (key_r, key_out), (attended, attended_out))
    ]
    step = width // 4
    for part in range(4):
        columns = slice(part * step, (part + 1) * step)
        result = nn(attended[...], out_w[:, columns])
        for i, block in enumerate(TOKEN_BLOCKS):
            out = pieces[SQUARE.index(block)]
            out[:, columns] = result[i * tok : (i + 1) * tok].astype(out.dtype)
    finish(put)


def in_halves(values, x, out):
    half = out.shape[1] // NX
    for dx in range(NX):
        start = pl.multiple_of((x ^ dx) * half, half)
        out[:, dx * half : (dx + 1) * half] = values[:, pl.ds(start, half)].astype(out.dtype)


def sum_of(refs):
    total = refs[0][...].astype(F32)
    for ref in refs[1:]:
        total = total + ref[...].astype(F32)
    return total


def branch_kernel(pos, *refs):
    parts, refs = refs[:GROUP], refs[GROUP:]
    inputs, gains, branch_out, hidden_out, mlp_in = refs
    branch = sum_of(parts)
    branch_out[...] = branch
    scale = lax.rsqrt(jnp.mean(branch * branch, axis=1, keepdims=True) + EPSILON)
    hidden_out[...] = inputs[...].astype(F32) + branch * scale * gains[2:3, :]
    in_halves(hidden_out, pos[0], mlp_in)


def norm_back(values, gain, grad):
    scale = lax.rsqrt(jnp.mean(values * values, axis=1, keepdims=True) + EPSILON)
    normed = values * scale
    scaled = grad * gain
    mean = jnp.mean(scaled * normed, axis=1, keepdims=True)
    return scale * (scaled - normed * mean), jnp.sum(grad * normed, axis=0, keepdims=True)


def mlp_kernel(count, pos, *refs):
    parts, refs = refs[:count], refs[count:]
    hidden, gains, grad_output, output, grad_in, grad_gain, halves, mlp_out = refs
    halves[...] = sum_of(parts)
    in_halves(halves, pos[0], mlp_out)
    values = mlp_out[...]
    gain = gains[3:4, :]
    scale = lax.rsqrt(jnp.mean(values * values, axis=1, keepdims=True) + EPSILON)
    output[...] = (hidden[...] + values * scale * gain).astype(BF16)
    grad, by_gain = norm_back(values, gain, grad_output[...].astype(F32))
    halves[...] = grad
    in_halves(halves, pos[0], grad_in)
    grad_gain[...] = jnp.broadcast_to(by_gain, grad_gain.shape)


def branch_back_kernel(count, pos, *refs):
    parts, refs = refs[:count], refs[count:]
    branch, gains, grad_output, grad_hidden, grad_branch, grad_gain, halves, middle = refs
    halves[...] = sum_of(parts)
    in_halves(halves, pos[0], middle)
    total = grad_output[...].astype(F32) + middle[...]
    grad_hidden[...] = total
    grad, by_gain = norm_back(branch[...], gains[2:3, :], total)
    grad_branch[...] = grad.astype(BF16)
    grad_gain[...] = jnp.broadcast_to(by_gain, grad_gain.shape)


def attend_back_kernel(pos, *refs):
    lengths, scales, gains, cosine, sine, out_w, *refs = refs
    blocks, refs = refs[:GROUP], refs[GROUP:]
    held, refs = refs[:5], refs[5:]
    query_out, key_out, grad_value, stats, head_gains, branch_all, *refs = refs
    query_r, key_r, value, query, key, *refs = refs
    grad_query, grad_key, grad_att, sems = refs
    x, _, y, _ = place(pos)
    tok = blocks[0].shape[0]
    span = NX * tok
    copies = Copies(sems)
    later = [
        copies.start(*pair) for pair in zip(held, (query_r, key_r, value, query, key))
    ]
    for i, block in enumerate(TOKEN_BLOCKS):
        branch_all[i * tok : (i + 1) * tok] = blocks[SQUARE.index(block)][...]
    for half in range(2):
        lanes = slice(half * (HEADS // 2), (half + 1) * (HEADS // 2))
        grad_att[:, lanes] = nt(branch_all[...], out_w[lanes, :]).astype(BF16)
    head_gains[...] = jnp.zeros_like(head_gains)
    finish(later)
    for seq in range(NY):
        at = slice(seq * span, (seq + 1) * span)
        columns = jnp.transpose(scales[:, at])
        valid = valid_keys(x, lengths[seq : seq + 1, 0:1], tok)
        for head in range(NZ):
            lanes = slice(head * HEAD_DIM, (head + 1) * HEAD_DIM)
            gain = pl.ds(column_of(x, head, y), HEAD_DIM)
            queries, keys, values = query_r[at, lanes], key_r[at, lanes], value[at, lanes]
            chances = softmax(queries, keys, valid)
            incoming = grad_att[at, lanes]
            grad_chances = nt(incoming, values)
            grad_value[at, lanes] = tn(chances.astype(BF16), incoming).astype(BF16)
            balance = jnp.sum(chances * grad_chances, axis=1, keepdims=True)
            grad_logits = (chances * (grad_chances - balance)).astype(BF16)
            by_query = nn(grad_logits, keys) * HEAD_DIM ** (-0.5)
            by_key = tn(grad_logits, queries) * HEAD_DIM ** (-0.5)
            for row, (grad, raw, out) in enumerate(
                ((by_query, query, grad_query), (by_key, key, grad_key))
            ):
                back = turn(grad.astype(BF16).astype(F32), cosine[...], -sine[...])
                normed = raw[at, lanes] * columns[:, 4 * row : 4 * row + 1]
                head_gains[row : row + 1, lanes] += jnp.sum(back * normed, axis=0, keepdims=True)
                out[at, lanes] = back * gains[row : row + 1, gain]
    query_out[...] = grad_query[...]
    key_out[...] = grad_key[...]
    stats[...] = row_stats(grad_query[...] * query[...], grad_key[...] * key[...])


def project_back_kernel(*refs):
    stats, *refs = refs
    scales, grad_query, grad_key, grad_value, query, key, grads = refs
    width = NX * NY * HEADS
    means = jnp.transpose(stats[...] / width)
    columns = jnp.transpose(scales[...])
    for row, (grad, raw) in enumerate(((grad_query, query), (grad_key, key))):
        scale = columns[:, 4 * row : 4 * row + 1]
        mean = means[:, 4 * row : 4 * row + 1]
        result = scale * (grad[...] - raw[...] * (scale * scale * mean))
        grads[:, row * HEADS : (row + 1) * HEADS] = result.astype(BF16)
    grads[:, 2 * HEADS :] = grad_value[...]


def input_back_kernel(pos, grads, *refs):
    weights, refs = refs[:NZ], refs[NZ:]
    *pieces, results = refs
    x, r, y, _ = place(pos)
    tok = grads.shape[0] // GROUP
    for s, weight in enumerate(weights):
        for half in range(2):
            result = nt(grads[...], weight[half * HEADS // 2 : (half + 1) * HEADS // 2, :])
            results[:, half * HEADS // 2 : (half + 1) * HEADS // 2] = result.astype(BF16)
        for j, (dx, dy) in enumerate(SQUARE):
            start = column_of(x ^ dx, ring(r, s), y ^ dy)
            for i, block in enumerate(TOKEN_BLOCKS):
                out = pieces[SQUARE.index(block)]
                out[:, pl.ds(start, HEAD_DIM)] = results[
                    i * tok : (i + 1) * tok, j * HEAD_DIM : (j + 1) * HEAD_DIM
                ]


def weight_back_kernel(nc, places, pos, *refs):
    for i, s in enumerate(places):
        weight_back_part(nc, s, i, pos, *refs)


def weight_back_part(nc, s, slot, pos, x_all, grads, attended, branch_all, *refs):
    attn_gain, mlp_gain, head_gains, *outs, columns, sums, out_sums = refs
    x, r, y, c = place(pos)
    rows = HEAD_DIM // nc
    base = slot * (4 * GROUP * rows + EXTRA)
    z = ring(r, s)
    gains = []
    for i, (dx, dy) in enumerate(SQUARE):
        start = column_of(x ^ dx, z, y ^ dy)
        columns[:, i * HEAD_DIM : (i + 1) * HEAD_DIM] = x_all[:, pl.ds(start, HEAD_DIM)]
        if i == 0:
            heads = pl.ds(pl.multiple_of(z * HEAD_DIM, HEAD_DIM), HEAD_DIM)
            gains.append(head_gains[0:2, heads])
        else:
            gains.append(jnp.zeros((2, HEAD_DIM), F32))
        gains.append(attn_gain[0:1, pl.ds(start, HEAD_DIM)])
        gains.append(mlp_gain[0:1, pl.ds(start, HEAD_DIM)])
    gains = jnp.concatenate(gains, axis=0)
    step = grads.shape[1] // 3
    for part in range(3):
        lanes = slice(part * step, (part + 1) * step)
        sums[:, lanes] = tn(columns[...], grads[:, lanes]).astype(BF16)
    heads = pl.ds(pl.multiple_of(z * HEAD_DIM, HEAD_DIM), HEAD_DIM)
    out_sums[...] = tn(attended[:, heads], branch_all[...]).astype(BF16)
    for k, out in enumerate(outs):
        for i in range(GROUP):
            start = pl.multiple_of(i * HEAD_DIM + (c ^ k) * rows, rows)
            for j in range(3):
                at = base + (j * GROUP + i) * rows
                lanes = slice(j * HEADS, (j + 1) * HEADS)
                out[at : at + rows] = sums[pl.ds(start, rows), lanes]
            start = pl.multiple_of((c ^ k) * rows, rows)
            at = base + (3 * GROUP + i) * rows
            lanes = slice(i * HEADS, (i + 1) * HEADS)
            out[at : at + rows] = out_sums[pl.ds(start, rows), lanes]
        chosen = 0.0
        for place_c in range(nc):
            part = gains[:, place_c * rows : (place_c + 1) * rows]
            chosen = chosen + jnp.where((c ^ k) == place_c, part, 0.0)
        chosen = jnp.concatenate([chosen, jnp.zeros((EXTRA, HEAD_DIM - rows), F32)], axis=1)
        put_extra(out, base + 4 * GROUP * rows, chosen)


def collect_kernel(count, *refs):
    parts, (grad_wo, *outs) = refs[:count], refs[count:]
    rows = (parts[0].shape[0] - EXTRA) // (4 * GROUP)

    def total(at, height, lanes=slice(None)):
        result = parts[0][at : at + height, lanes].astype(F32)
        for part in parts[1:]:
            result = result + part[at : at + height, lanes].astype(F32)
        return result

    extra = total(4 * GROUP * rows, EXTRA, slice(0, HEAD_DIM))
    for i, out in enumerate(outs):
        for j in range(3):
            part = total((j * GROUP + i) * rows, rows)
            out[:rows, j * HEADS : (j + 1) * HEADS] = part.astype(BF16)
        grad_wo[:, i * HEADS : (i + 1) * HEADS] = total((3 * GROUP + i) * rows, rows)
        put_extra(out, rows, extra_rows([extra[4 * i : 4 * i + 4]]))


def spread_kernel(pos, *refs):
    parts, (*outs, gains) = refs[:GROUP], refs[GROUP:]
    x, _, y, _ = place(pos)
    rows = parts[0].shape[0] - EXTRA
    total = 0.0
    for (dx, dy), part in zip(SQUARE, parts):
        total = total + part[rows:, :HEAD_DIM].astype(F32)
        for i, out in enumerate(outs):
            for head in range(NZ):
                start = column_of(x ^ dx, head, y ^ dy)
                at = i * HEADS + head * HEAD_DIM
                out[:, pl.ds(start, HEAD_DIM)] = part[:rows, at : at + HEAD_DIM].astype(F32)
    gains[...] = total[:8]


def take(refs, *counts):
    groups = []
    for count in counts:
        groups.append(refs[:count])
        refs = refs[count:]
    return *groups, refs


def put_columns(block, kept):
    width = kept[0].shape[1]
    for i, out in enumerate(kept):
        out[...] = block[:, i * width : (i + 1) * width]


def mlp_forward_kernel(nc, block, *refs):
    count = NY * nc
    gates, ups, downs, refs = take(refs, NX * count, NX * count, 4 * count)
    refs = refs[-(2 * nc + NY + NX + 2) :]
    products, by_gate, by_up, kept, (out, total) = take(refs, NY, nc, nc, NX)
    put_columns(block, kept)
    hidden = gates[0].shape[1]
    quarter = kept[0].shape[1] // 2
    for k in range(nc):
        for dy in range(NY):
            at = dy * nc + k
            lanes = slice(dy * hidden, (dy + 1) * hidden)

            def through(weights):
                return nn(kept[0][...], weights[at][...]) + nn(
                    kept[1][...], weights[count + at][...]
                )

            gate, up = through(gates), through(ups)
            chance = 1.0 / (1.0 + jnp.exp(-gate))
            silu = gate * chance
            product = (silu * up).astype(BF16)
            products[dy][:, k * hidden : (k + 1) * hidden] = product
            by_up[k][:, lanes] = silu.astype(BF16)
            by_gate[k][:, lanes] = (up * (chance + silu * (1.0 - chance))).astype(BF16)
            for i in range(4):
                columns = slice(i * quarter, (i + 1) * quarter)
                part = nt(product, downs[i * count + at][...])
                total[:, columns] = part if k + dy == 0 else total[:, columns] + part
    out[...] = total[...]


def mlp_back_kernel(nc, block, *refs):
    count = NY * nc
    gates, ups, downs, by_gate, by_up, refs = take(
        refs, NX * count, NX * count, 4 * count, nc, nc
    )
    refs = refs[-(2 * nc + NX + 2) :]
    grad_gates, grad_ups, kept, (out, total) = take(refs, nc, nc, NX)
    put_columns(block, kept)
    hidden = gates[0].shape[1]
    quarter = kept[0].shape[1] // 2
    for k in range(nc):
        for dy in range(NY):
            at = dy * nc + k
            lanes = slice(dy * hidden, (dy + 1) * hidden)
            grad = 0.0
            for i in range(4):
                columns = slice((i % 2) * quarter, (i % 2 + 1) * quarter)
                grad = grad + nn(kept[i // 2][:, columns], downs[i * count + at][...])
            grad_gate = (grad * by_gate[k][:, lanes].astype(F32)).astype(BF16)
            grad_up = (grad * by_up[k][:, lanes].astype(F32)).astype(BF16)
            grad_gates[k][:, lanes] = grad_gate
            grad_ups[k][:, lanes] = grad_up
            for i in range(4):
                columns = slice(i * quarter, (i + 1) * quarter)
                rows = slice((i % 2) * quarter, (i % 2 + 1) * quarter)
                weight = (i // 2) * count + at
                part = nt(grad_gate, gates[weight][rows, :]) + nt(grad_up, ups[weight][rows, :])
                total[:, columns] = part if k + dy == 0 else total[:, columns] + part
    out[...] = total[...]


def down_back_kernel(*refs):
    *parts, out = refs
    count = len(parts) // 3
    near, far, products, _ = take(parts, count, count, count)
    tok = near[0].shape[0]
    step = out.shape[0] // 2
    for i in range(2):
        rows = slice(i * step, (i + 1) * step)
        for j, product in enumerate(products):
            part = tn(near[j][:, rows], product[:tok]) + tn(far[j][:, rows], product[tok:])
            out[rows, :] = part if j == 0 else out[rows, :] + part


def make_body(wide):
    nc = wide // (NY * NZ)

    def send(value, x=0, y=0, r=0, c=0):
        pairs = []
        for sx in range(NX):
            for sz in range(NZ):
                for sy in range(NY):
                    for sc in range(nc):
                        source = sx * wide + (sz * NY + sy) * nc + sc
                        target = (sx ^ x) * wide
                        target += (ring(gray(sz), r) * NY + (sy ^ y)) * nc + (sc ^ c)
                        pairs.append((source, target))
        return lax.ppermute(value, AXES, pairs)

    def square(parts):
        return [
            part if (dx, dy) == (0, 0) else send(part, x=dx, y=dy)
            for (dx, dy), part in zip(SQUARE, parts)
        ]

    def square_gather(first, second):
        first_x = send(first, x=1)
        second_y = send(second, y=1)
        first_y = send(first, y=1)
        second_x = send(second, x=1)
        first_xy = send(first_x, y=1)
        second_xy = send(second_y, x=1)
        return [first, first_y, first_x, first_xy], [second, second_y, second_x, second_xy]

    def scatter_far(first, second):
        return send(first[3], x=1), send(second[3], y=1)

    def scatter_near(first, second):
        return send(first[2], x=1), send(second[1], y=1)

    def scatter_last(first, second, far, near):
        return (
            send((first[1].astype(F32) + far[0].astype(F32)).astype(BF16), y=1),
            send((second[2].astype(F32) + far[1].astype(F32)).astype(BF16), x=1),
        )

    def scatter_sum(first, second, near, last):
        return (
            first[0].astype(F32) + near[0].astype(F32) + last[0].astype(F32),
            second[0].astype(F32) + near[1].astype(F32) + last[1].astype(F32),
        )

    def core_gather(block):
        return [block] + [send(block, c=k) for k in range(1, nc)]

    def core_sums(blocks, hidden):
        sums = []
        for row in blocks:
            total = row[0].astype(F32)
            for k in range(1, nc):
                total = total + send(row[k], c=k).astype(F32)
            total = total.astype(BF16)
            sums += [total[:, dy * hidden : (dy + 1) * hidden] for dy in range(NY)]
        return sums

    def core_parts(parts):
        return [parts[0]] + [send(parts[k], c=k) for k in range(1, nc)]

    def body(
        layer_input,
        lengths,
        w_query,
        w_key,
        w_value,
        w_output,
        query_gain,
        key_gain,
        attn_gain,
        mlp_gain,
        w_gate,
        w_up,
        w_down,
        grad_output,
    ):
        due = {}

        def mark(point, value):
            due.setdefault(point, []).append(value)

        def at(point, value):
            ready = due.pop(point, [])
            return after(value, ready) if ready else value

        x = lax.axis_index("blk")
        spot = lax.axis_index("wide")
        z, y, c = spot // (NY * nc), (spot // nc) % NY, spot % nc
        inputs, grad_out = layer_input[0], grad_output[0]
        tok, width = inputs.shape
        rows = w_query.shape[0]
        group_tok = GROUP * tok
        hidden = w_gate.shape[1]
        pos = jnp.stack([x, gray(z), y, c, lengths[0]]).astype(jnp.int32)
        wide_small = shaped((8, width), F32)
        by_head = shaped((group_tok, HEADS))
        by_head_wide = shaped((group_tok, HEADS), F32)
        by_token = shaped((8, group_tok), F32)
        tokens_shape = shaped((tok, width))
        tokens_wide = shaped((tok, width), F32)
        message = shaped((4 * GROUP * rows + EXTRA, HEADS))
        piece = shaped((rows + EXTRA, 3 * HEADS))

        def group_sum(stats, *ready):
            blocks = [stats[:, i * tok : (i + 1) * tok] for i in range(GROUP)]
            for flip, way in ((1, {"x": 1}), (2, {"y": 1})):
                total = jnp.concatenate(blocks, axis=1)
                if flip == 2 and ready:
                    total = after(total, ready)
                got = send(total, **way)
                got = [got[:, i * tok : (i + 1) * tok] for i in range(GROUP)]
                blocks = [block + got[i ^ flip] for i, block in enumerate(blocks)]
            return jnp.concatenate(blocks, axis=1)

        def dma(count):
            return pltpu.SemaphoreType.DMA((count,))

        def held(shape):
            return pltpu.VMEM(shape.shape, shape.dtype)

        gains = jnp.stack([query_gain, key_gain, attn_gain, mlp_gain])
        pieces = run(
            split_kernel,
            each([piece] * GROUP, VMEM),
            [(pos, SMEM), (gains, VMEM), (w_query, auto), (w_key, auto), (w_value, auto)],
        )
        down_rows = w_down.shape[0] // 2
        down_halves = w_down[:down_rows], w_down[down_rows:]
        far_down = send(down_halves[0], x=1), send(down_halves[1], y=1)
        mark(Due.far_down, far_down)
        received = at(Point.JOIN, square(pieces))
        own_rows, lengths_row = run(
            join_kernel,
            [(message, VMEM), (shaped((8, HEAD_DIM), F32), VMEM)],
            each((*received, w_output), VMEM),
        )
        lane = jnp.arange(HEAD_DIM)[None, :]
        row = jnp.arange(NX * tok)[:, None]
        row = jnp.where(row < tok, x * tok + row, (1 - x) * tok + row - tok).astype(F32)
        half = HEAD_DIM // 2
        frequency = jnp.exp((lane % half).astype(F32) * (-2.0 * math.log(500000.0) / HEAD_DIM))
        cosine = jnp.cos(row * frequency)
        sine = jnp.sin(row * jnp.where(lane < half, -frequency, frequency))
        mark(Due.turns, (cosine, sine))
        w_ring = [own_rows, send(own_rows, r=-1)]
        half_tok = tok // 2
        from_x = send(after(inputs, own_rows), x=1)
        from_y = send(after(inputs, own_rows), y=1)
        from_xy = send(from_x[:half_tok], y=1), send(from_y[half_tok:], x=1)
        far_gate = send(after(w_gate, from_xy), x=1)
        far_up = send(after(w_up, from_xy), y=1)
        near_gate = send(after(w_gate, far_up), y=1)
        near_up = send(after(w_up, far_gate), x=1)
        mark(Due.far, (far_gate, far_up))
        mark(Due.tokens, (from_x, from_y))
        mark(Due.tokens_xy, from_xy)
        mark(Due.near, (near_gate, near_up))
        own_gate, own_up = core_gather(w_gate), core_gather(w_up)
        own_down = core_gather(w_down)
        far_gate, far_up = core_gather(far_gate), core_gather(far_up)
        far_down = core_gather(far_down[0]), core_gather(far_down[1])
        mark(Due.own_gate_c, (own_gate, own_up))
        mark(Due.own_down_c, own_down)
        mark(Due.far_c, (far_gate, far_up))
        mark(Due.far_down_c, far_down)
        first_blocks = core_gather(own_rows)
        w_ring.append(send(at(Point.RING_2, w_ring[1]), r=-1))
        second_blocks = core_gather(w_ring[1])
        w_ring.append(send(at(Point.RING_3, w_ring[2]), r=-1))
        x_all, x_kept = run(
            gather_kernel,
            [(shaped((group_tok, width)), VMEM), (shaped((group_tok, width)), HBM)],
            each([inputs, from_x, from_y, *from_xy], VMEM),
            scratch_shapes=[pltpu.SemaphoreType.DMA],
        )
        w_shape = shaped((GROUP * HEAD_DIM, 3 * HEADS))
        by_three = shaped((group_tok, 3 * HEADS), F32)
        out_shape = shaped((HEADS, width))

        def project(places, blocks, before, outs):
            ins = [(pos, SMEM), (x_all, VMEM), *each(blocks, VMEM), *each(before, VMEM)]
            depth = len(places) * GROUP * HEAD_DIM
            return run(
                functools.partial(project_kernel, nc, places),
                [(wide_small, VMEM), (out_shape, VMEM)] + [(w_shape, HBM)] * len(places) + outs,
                ins,
                limit=16,
                input_output_aliases={len(ins) - 2: 0, len(ins) - 1: 1} if before else {},
                scratch_shapes=[
                    pltpu.VMEM((group_tok, depth), BF16),
                    pltpu.VMEM((depth, 3 * HEADS), BF16),
                    dma(len(places) + 4),
                ],
            )

        blocks = first_blocks + second_blocks + core_gather(w_ring[2])
        gains, out_w, *w_parts, total = project((0, 1, 2), blocks, (), [(by_three, VMEM)])
        mark(Due.total, total)
        last_block = core_gather(at(Point.LAST_ROWS, w_ring[3]))
        near_down = (
            send(after(down_halves[0], near_gate), y=1),
            send(after(down_halves[1], near_up), x=1),
        )
        mark(Due.near_down, near_down)
        near_gate, near_up = core_gather(near_gate), core_gather(near_up)
        mark(Due.near_c, (near_gate, near_up))
        gains, out_w, w_part, query, key, value, query_h, key_h, value_h, out_kept, stats = project(
            (3,),
            last_block,
            (total, gains, out_w),
            [(by_head_wide, VMEM), (by_head_wide, VMEM), (by_head, VMEM)]
            + [(by_head_wide, HBM), (by_head_wide, HBM), (by_head, HBM)]
            + [(out_shape, HBM), (by_token, VMEM)],
        )
        w_parts.append(w_part)
        group_stats = at(Point.SCALES, group_sum(at(Point.STATS, stats)))
        last_gate = send(after(far_gate[0], group_stats, near_gate[0]), y=1)
        last_up = send(after(far_up[0], group_stats, near_up[0]), x=1)
        mark(Due.last, (last_gate, last_up))
        last_gate, last_up = core_gather(last_gate), core_gather(last_up)
        mark(Due.last_c, (last_gate, last_up))
        gate_w = [*own_gate, *near_gate, *far_gate, *last_gate]
        up_w = [*own_up, *far_up, *near_up, *last_up]
        near_down = core_gather(near_down[0]), core_gather(near_down[1])
        mark(Due.near_down_c, near_down)

        query_r, key_r, attended, scales, *parts = run(
            attend_kernel,
            [(by_head, HBM)] * 3 + [(by_token, VMEM)] + [(tokens_shape, VMEM)] * GROUP,
            [
                (pos, SMEM),
                (group_stats, VMEM),
                *each((lengths_row, gains, cosine, sine), VMEM),
                *each((query, key, value, out_w), VMEM),
            ],
            scratch_shapes=[held(by_head), held(by_head), held(by_head), dma(3)],
        )
        parts = square(at(Point.BRANCH_SEND, parts))
        first_x, second_y = far_down
        last_down = (
            core_gather(send(after(first_x[0], parts), y=1)),
            core_gather(send(after(second_y[0], parts), x=1)),
        )
        own_first = [part[:down_rows] for part in own_down]
        own_second = [part[down_rows:] for part in own_down]
        down_first = own_first, near_down[0], first_x, last_down[0]
        down_second = own_second, second_y, near_down[1], last_down[1]
        down_w = [
            piece
            for dx in range(NX)
            for half in (down_first, down_second)
            for dy in range(NY)
            for piece in half[dx * NY + dy]
        ]
        branch, hidden_state, mlp_in = run(
            branch_kernel,
            [(tokens_wide, auto), (tokens_wide, auto), (tokens_shape, VMEM)],
            [(pos, SMEM), *each(at(Point.BRANCH, parts), auto), (inputs, auto), (gains, VMEM)],
        )

        half_width = width // NX
        quarter = half_width // 2

        def mlp_call(kernel, s, block, extra, narrow, before):
            def rows_of(array):
                count = array.shape[0] // tok
                return pl.BlockSpec((tok, array.shape[1]), lambda i: (s % count, 0))

            ins = each((block, *gate_w, *up_w, *down_w), VMEM) + each(extra, rows_of)
            columns, height = narrow
            outs = [shaped((NZ * tok, count)) for count in columns]
            outs = each(outs + [shaped((height, half_width))] * NX, rows_of)
            aliases = {}
            if before is not None:
                aliases = {len(ins) + i: i for i in range(len(before))}
                ins += each(before, HBM)
            *kept, total = run(
                functools.partial(kernel, nc),
                [*outs, (tokens_wide, VMEM)],
                ins,
                input_output_aliases=aliases,
                scratch_shapes=[held(tokens_wide)],
            )
            return kept, total

        def summed(parts):
            total = parts[0].astype(F32)
            for part in parts[1:]:
                total = total + part.astype(F32)
            return total

        def mlp_pass(points, kernel, block, extra, columns, height):
            narrow = columns, height
            near = send(block, r=-1)
            middle = send(near, r=-1)
            kept, first = mlp_call(kernel, 1, at(points, near), extra, narrow, None)
            far = send(middle, r=-1)
            sent = [first.astype(BF16)]
            moving = send(sent[0], r=-1)
            kept, own = mlp_call(kernel, 0, block, extra, narrow, kept)
            early = []
            if height < NZ * tok:
                early, kept = kept[-NX:], kept[:-NX]
                early = square([early[dx] for dx, dy in SQUARE])
                mark(Due.near_grads, early[1:3])
                mark(Due.near_grads_xy, early[3])
            middle = at(points + 1, middle)
            kept, second = mlp_call(kernel, 2, middle, extra, narrow, kept)
            far = at(points + 2, far)
            kept, third = mlp_call(kernel, 3, far, extra, narrow, kept)
            sent.append(summed([second, moving]).astype(BF16))
            sent.append(summed([third, send(sent[1], r=-1)]).astype(BF16))
            parts = [own, send(at(points + 3, sent[2]), r=-1)]
            return kept, parts, sent, early

        columns = [nc * hidden] * NY + [NY * hidden] * 2 * nc
        kept, parts, sent, _ = mlp_pass(
            Point.F1, mlp_forward_kernel, mlp_in, (), columns, NZ * tok
        )
        products, by_gate, by_up, mlp_all = take(kept, NY, nc, nc)

        late = after(products, sent[1])
        got_products = square([late[dy] for dx, dy in SQUARE])
        mark(Due.products, got_products[1:3])
        mark(Due.products_xy, got_products[3])
        output, grad_mlp, grad_gain_mlp = run(
            functools.partial(mlp_kernel, len(parts)),
            [(tokens_shape, auto), (tokens_shape, VMEM), (wide_small, VMEM)],
            [
                (pos, SMEM),
                *each(at(Point.MLP_OUT, parts), auto),
                (hidden_state, auto),
                (gains, VMEM),
                (grad_out, auto),
            ],
            scratch_shapes=[held(tokens_wide)] * 2,
        )
        extra = *by_gate, *by_up
        columns = [NY * hidden] * 2 * nc
        kept, parts, sent, near_grads = mlp_pass(
            Point.B1, mlp_back_kernel, grad_mlp, extra, columns, 2 * tok
        )
        grad_gates, grad_ups, grad_all = take(kept, nc, nc)
        grad_hidden, grad_branch, grad_gain_attn = run(
            functools.partial(branch_back_kernel, len(parts)),
            [(tokens_wide, auto), (tokens_shape, VMEM), (wide_small, VMEM)],
            [
                (pos, SMEM),
                *each(at(Point.MIDDLE, parts), auto),
                (branch, auto),
                (gains, VMEM),
                (grad_out, auto),
            ],
            scratch_shapes=[held(tokens_wide)] * 2,
        )

        def products_of(left, right):
            return [[tn(block, grad).astype(BF16) for grad in right] for block in left]

        late = after(grad_all, sent[2])
        far_grads = square([late[dx] for dx, dy in SQUARE])
        mark(Due.far_grads, far_grads[1:3])
        mark(Due.far_grads_xy, far_grads[3])
        blocks = square([at(Point.BRANCH_BACK, grad_branch)] * GROUP)
        mlp_all = after(mlp_all, blocks[1])
        wg_blocks = products_of(mlp_all, grad_gates)
        wu_blocks = products_of(mlp_all, grad_ups)
        mark(Due.dots, (wg_blocks, wu_blocks))
        blocks = at(Point.ATTEND_BACK, blocks)
        wg_blocks, wu_blocks = after((wg_blocks, wu_blocks), blocks)
        w_pair = core_sums(wg_blocks, hidden), core_sums(wu_blocks, hidden)
        mark(Due.sums, w_pair)
        grad_query, grad_key, grad_value, stats, head_gains, branch_all = run(
            attend_back_kernel,
            [
                (by_head_wide, VMEM),
                (by_head_wide, VMEM),
                (by_head, VMEM),
                (by_token, VMEM),
                (shaped((8, HEADS), F32), VMEM),
                (shaped((group_tok, width)), VMEM),
            ],
            [
                (pos, SMEM),
                *each((lengths_row, scales, gains, cosine, sine, out_kept, *blocks), VMEM),
                *each((query_r, key_r, value_h, query_h, key_h), HBM),
            ],
            limit=16,
            scratch_shapes=[
                held(by_head),
                held(by_head),
                held(by_head),
                held(by_head_wide),
                held(by_head_wide),
                held(by_head_wide),
                held(by_head_wide),
                held(by_head),
                dma(5),
            ],
        )
        (grads,) = run(
            project_back_kernel,
            [(shaped((group_tok, 3 * HEADS)), VMEM)],
            [
                (at(Point.PROJECT_BACK, group_sum(at(Point.STATS_BACK, stats))), VMEM),
                (scales, VMEM),
                *each((grad_query, grad_key, grad_value, query_h, key_h), VMEM),
            ],
        )
        w_far = scatter_far(*after(w_pair, grads))
        w_near = scatter_near(*after(w_pair, w_far))
        w_last = scatter_last(*w_pair, w_far, w_near)
        mark(Due.w_far, w_far)
        mark(Due.w_near, w_near)
        mark(Due.w_last, w_last)

        def weight_parts(places):
            height = message.shape[0]
            results = run(
                functools.partial(weight_back_kernel, nc, places),
                [(shaped((len(places) * height, HEADS)), VMEM)] * nc,
                [
                    (pos, SMEM),
                    *each((x_kept, grads, attended, branch_all), VMEM),
                    *each((grad_gain_attn, grad_gain_mlp, head_gains), VMEM),
                ],
                scratch_shapes=[
                    pltpu.VMEM((group_tok, GROUP * HEAD_DIM), BF16),
                    pltpu.VMEM((GROUP * HEAD_DIM, 3 * HEADS), BF16),
                    pltpu.VMEM((HEAD_DIM, width), BF16),
                ],
            )
            results = core_parts(results)
            return [
                [part[i * height : (i + 1) * height] for part in results]
                for i in range(len(places))
            ]

        (first,) = weight_parts((1,))
        factors = []
        for *grads_of, product in zip(near_grads, far_grads, got_products):
            for k in range(nc):
                pieces = *grads_of, product[:, k * hidden : (k + 1) * hidden]
                factors.append([send(piece, c=k) if k else piece for piece in pieces])
        mark(Due.factors, factors)
        (grad_wd,) = run(
            down_back_kernel,
            [(shaped(w_down.shape, F32), VMEM)],
            each([entry[i] for i in range(3) for entry in factors], VMEM),
        )

        mark(Due.grad_wd, grad_wd)
        w_moving = send(at(Point.SUM_1, summed(first).astype(BF16)), r=-1)
        (second,) = weight_parts((2,))
        (third,) = weight_parts((3,))
        (own,) = weight_parts((0,))
        x_parts = run(
            input_back_kernel,
            [(tokens_shape, VMEM)] * GROUP,
            [(pos, SMEM), (after(grads, second), VMEM), *each(w_parts, VMEM)],
            scratch_shapes=[pltpu.VMEM((group_tok, GROUP * HEAD_DIM), BF16)],
        )
        mark(Due.x_parts, x_parts)
        late = after(x_parts[1:3], w_last)
        from_x = [x_parts[0], send(late[0], y=1), send(late[1], x=1)]
        mark(Due.x_sums, from_x)
        sent = summed(second + [w_moving]).astype(BF16)
        w_moving = send(at(Point.SUM_2, sent), r=-1)
        sent = summed(third + [w_moving]).astype(BF16)
        w_moving = send(at(Point.SUM_3, sent), r=-1)
        grad_wg, grad_wu = scatter_sum(*w_pair, w_near, w_last)
        parts = at(Point.COLLECT, own + [w_moving])
        grad_wo, *messages = run(
            functools.partial(collect_kernel, len(parts)),
            [(shaped((rows, width), F32), auto)] + [(piece, VMEM)] * GROUP,
            each(parts, auto),
        )
        grad_wq, grad_wk, grad_wv, total_gains = run(
            spread_kernel,
            [(shaped((rows, width), F32), auto)] * 3 + [(shaped((8, HEAD_DIM), F32), VMEM)],
            [(pos, SMEM), *each(at(Point.SPREAD, square(messages)), auto)],
        )
        last_x = send(after(x_parts[3], messages), x=1, y=1)
        grad_x = summed([grad_hidden, *from_x, last_x])

        return (
            output[None],
            grad_x.astype(BF16)[None],
            grad_wq,
            grad_wk,
            grad_wv,
            grad_wo,
            total_gains[0, :rows],
            total_gains[1, :rows],
            total_gains[2, :rows],
            total_gains[3, :rows],
            grad_wg,
            grad_wu,
            grad_wd,
        )

    return body


def solution(mesh):
    return jax.shard_map(
        make_body(mesh.shape["wide"]),
        mesh=mesh,
        in_specs=(
            P("wide", "blk", None),
            P("wide"),
            P(("blk", "wide"), None),
            P(("blk", "wide"), None),
            P(("blk", "wide"), None),
            P(("blk", "wide"), None),
            P(("blk", "wide")),
            P(("blk", "wide")),
            P(("blk", "wide")),
            P(("blk", "wide")),
            P("blk", "wide"),
            P("blk", "wide"),
            P("blk", "wide"),
            P("wide", "blk", None),
        ),
        out_specs=(
            P("wide", "blk", None),
            P("wide", "blk", None),
            P(("blk", "wide"), None),
            P(("blk", "wide"), None),
            P(("blk", "wide"), None),
            P(("blk", "wide"), None),
            P(("blk", "wide")),
            P(("blk", "wide")),
            P(("blk", "wide")),
            P(("blk", "wide")),
            P("blk", "wide"),
            P("blk", "wide"),
            P("blk", "wide"),
        ),
        check_vma=False,
    )
```

```python
import enum
import functools
import math

import jax
import jax.numpy as jnp
from jax import lax
from jax.experimental import pallas as pl
from jax.experimental.pallas import tpu as pltpu
from jax.sharding import PartitionSpec as P

HEAD_DIM = 128
EPSILON = 1e-06
NEGATIVE = -1e30
BF16 = jnp.bfloat16
F32 = jnp.float32
AXES = ("blk", "wide")
NX, NY, NZ = 2, 2, 4
GROUP = NX * NY
HEADS = NZ * HEAD_DIM
MIB = 1 << 20
SMEM = pl.BlockSpec(memory_space=pltpu.SMEM)
VMEM = pl.BlockSpec(memory_space=pltpu.VMEM)
HBM = pl.BlockSpec(memory_space=pltpu.HBM)
EXTRA = 16
class Point(enum.IntEnum):
    JOIN = 0
    RING_2 = 1
    RING_3 = 2
    LAST_ROWS = 3
    STATS = 4
    SCALES = 5
    BRANCH_SEND = 6
    BRANCH = 7
    F1 = 8
    F2 = 9
    F3 = 10
    F4 = 11
    MLP_OUT = 12
    B1 = 13
    B2 = 14
    B3 = 15
    B4 = 16
    MIDDLE = 17
    BRANCH_BACK = 18
    ATTEND_BACK = 19
    STATS_BACK = 20
    PROJECT_BACK = 21
    SUM_1 = 22
    SUM_2 = 23
    SUM_3 = 24
    COLLECT = 25
    SPREAD = 26
    NEVER = 27


class Due:
    far_down = Point.JOIN
    turns = Point.RING_2
    far = Point.RING_3
    tokens = Point.RING_2
    tokens_xy = Point.RING_2
    near = Point.LAST_ROWS
    own_gate_c = Point.RING_3
    own_down_c = Point.LAST_ROWS
    far_c = Point.LAST_ROWS
    far_down_c = Point.STATS
    total = Point.LAST_ROWS
    near_down = Point.BRANCH
    near_c = Point.BRANCH_SEND
    last = Point.BRANCH_SEND
    last_c = Point.F1
    near_down_c = Point.BRANCH_SEND
    near_grads = Point.B3
    near_grads_xy = Point.B4
    products = Point.B1
    products_xy = Point.B2
    far_grads = Point.BRANCH_BACK
    far_grads_xy = Point.STATS_BACK
    dots = Point.ATTEND_BACK
    sums = Point.STATS_BACK
    w_far = Point.SUM_2
    w_near = Point.COLLECT
    w_last = Point.COLLECT
    factors = Point.COLLECT
    grad_wd = Point.COLLECT
    x_parts = Point.SUM_3
    x_sums = Point.SPREAD

SQUARE = [(dx, dy) for dx in range(NX) for dy in range(NY)]
TOKEN_BLOCKS = [(dx, dy) for dy in range(NY) for dx in range(NX)]


def shaped(shape, dtype=BF16):
    return jax.ShapeDtypeStruct(tuple(shape), dtype)


def nn(left, right):
    return lax.dot_general(left, right, (((1,), (0,)), ((), ())), preferred_element_type=F32)


def nt(left, right):
    return lax.dot_general(left, right, (((1,), (1,)), ((), ())), preferred_element_type=F32)


def tn(left, right):
    return lax.dot_general(left, right, (((0,), (0,)), ((), ())), preferred_element_type=F32)


def auto(array):
    return pl.BlockSpec(array.shape, lambda i: (0,) * len(array.shape))


def run(body, outs, ins, limit=12, **options):
    return pl.pallas_call(
        body,
        grid=(1,),
        out_shape=[
            pltpu.HBM(out.shape, out.dtype) if spec is HBM else out for out, spec in outs
        ],
        out_specs=[spec if isinstance(spec, pl.BlockSpec) else spec(out) for out, spec in outs],
        in_specs=[spec if isinstance(spec, pl.BlockSpec) else spec(array) for array, spec in ins],
        compiler_params=pltpu.CompilerParams(vmem_limit_bytes=limit * MIB),
        cost_estimate=pl.CostEstimate(flops=0, bytes_accessed=0, transcendentals=0),
        **options,
    )(*[array for array, _ in ins])


def each(arrays, spec):
    return [(array, spec) for array in arrays]


def after(value, *others):
    return lax.optimization_barrier((value, others))[0]


class Copies:
    def __init__(self, sems):
        self.sems, self.count = sems, 0

    def start(self, source, target):
        copy = pltpu.make_async_copy(source, target, self.sems.at[self.count])
        self.count += 1
        copy.start()
        return copy


def finish(copies):
    for copy in copies:
        copy.wait()


def place(pos):
    return pos[0], pos[1], pos[2], pos[3]


def gray(index):
    return index ^ (index >> 1)


def ring(r, s):
    return gray((r + s) % NZ)


def column_of(x, z, y):
    return pl.multiple_of(((x * NZ + z) * NY + y) * HEAD_DIM, HEAD_DIM)


def extra_rows(blocks):
    used = sum(block.shape[0] for block in blocks)
    if used < EXTRA:
        blocks = [*blocks, jnp.zeros((EXTRA - used, HEAD_DIM), F32)]
    return jnp.concatenate(blocks, axis=0)


def put_extra(out, start, values):
    out[start : start + EXTRA, :HEAD_DIM] = values.astype(BF16)
    out[start : start + EXTRA, HEAD_DIM:] = jnp.zeros((EXTRA, out.shape[1] - HEAD_DIM), BF16)


def split_kernel(pos, gains, w_query, w_key, w_value, *outs):
    x, _, y, _ = place(pos)
    rows = w_query.shape[0]
    own = gains[...].astype(F32)
    own = jnp.concatenate([own, jnp.zeros((4, HEAD_DIM - rows), F32)], axis=1)
    length = jnp.full((1, HEAD_DIM), pos[4]).astype(F32)
    for (dx, dy), out in zip(SQUARE, outs):
        for i, weight in enumerate((w_query, w_key, w_value)):
            for head in range(NZ):
                start = column_of(x ^ dx, head, y ^ dy)
                at = i * HEADS + head * HEAD_DIM
                out[:rows, at : at + HEAD_DIM] = weight[:, pl.ds(start, HEAD_DIM)]
        put_extra(out, rows, extra_rows([own, length]))


def join_kernel(*refs):
    *parts, w_output, out, lengths = refs
    rows = parts[0].shape[0] - EXTRA
    extras = []
    for i, part in enumerate(parts):
        for j in range(3):
            at = (j * GROUP + i) * rows
            out[at : at + rows] = part[:rows, j * HEADS : (j + 1) * HEADS]
        at = (3 * GROUP + i) * rows
        out[at : at + rows] = w_output[:, i * HEADS : (i + 1) * HEADS]
        extras.append(part[rows:, :HEAD_DIM].astype(F32))
    put_extra(out, 4 * GROUP * rows, extra_rows([extra[:4] for extra in extras]))
    lengths[...] = jnp.concatenate(
        [extras[0][4:5], extras[1][4:5], jnp.zeros((6, HEAD_DIM), F32)], axis=0
    )


def row_stats(first, second):
    shape = (first.shape[0], HEAD_DIM)
    upper = lax.broadcasted_iota(jnp.int32, shape, 1) < 4
    sums = jnp.where(
        upper,
        jnp.sum(first, axis=1, keepdims=True),
        jnp.sum(second, axis=1, keepdims=True),
    )
    return jnp.transpose(sums)[:8]


def gather_kernel(*refs):
    blocks, (whole, kept, sem) = refs[:-3], refs[-3:]
    start = 0
    for block in blocks:
        whole[start : start + block.shape[0]] = block[...]
        start += block.shape[0]
    copy = pltpu.make_async_copy(whole, kept, sem)
    copy.start()
    copy.wait()


def project_kernel(nc, places, pos, x_all, *refs):
    weights, refs = refs[: nc * len(places)], refs[nc * len(places) :]
    last = places[-1] == NZ - 1
    if last:
        before, _, _, *refs = refs
    gains, out_w, *refs = refs
    w_rows, refs = refs[: len(places)], refs[len(places) :]
    if last:
        query, key, value, query_h, key_h, value_h, out_kept, stats, *refs = refs
    else:
        total, *refs = refs
    columns, w_part, sems = refs
    x, r, y, c = place(pos)
    rows = (weights[0].shape[0] - EXTRA) // (4 * GROUP)
    copies = Copies(sems)
    put = []
    for slot, s in enumerate(places):
        blocks = weights[slot * nc : (slot + 1) * nc]
        z = ring(r, s)
        extras = [block[4 * GROUP * rows :, :HEAD_DIM].astype(F32) for block in blocks]
        lanes = []
        for place_c in range(nc):
            chosen = 0.0
            for k, part in enumerate(extras):
                chosen = chosen + jnp.where((c ^ k) == place_c, part[:, :rows], 0.0)
            lanes.append(chosen)
        ordered = jnp.concatenate(lanes, axis=1)
        base = slot * GROUP * HEAD_DIM
        for i, (dx, dy) in enumerate(SQUARE):
            start = column_of(x ^ dx, z, y ^ dy)
            gains[:, pl.ds(start, HEAD_DIM)] = jnp.concatenate(
                [ordered[4 * i : 4 * i + 4], jnp.zeros((4, HEAD_DIM), F32)], axis=0
            )
            to = base + i * HEAD_DIM
            columns[:, to : to + HEAD_DIM] = x_all[:, pl.ds(start, HEAD_DIM)]
            for k, block in enumerate(blocks):
                at = pl.multiple_of(to + (c ^ k) * rows, rows)
                for j in range(3):
                    got = (j * GROUP + i) * rows
                    lanes = slice(j * HEADS, (j + 1) * HEADS)
                    w_part[pl.ds(at, rows), lanes] = block[got : got + rows]
                got = (3 * GROUP + i) * rows
                at = pl.multiple_of(z * HEAD_DIM + (c ^ k) * rows, rows)
                lanes = slice(i * HEADS, (i + 1) * HEADS)
                out_w[pl.ds(at, rows), lanes] = block[got : got + rows]
        put.append(
            copies.start(w_part.at[pl.ds(base, GROUP * HEAD_DIM)], w_rows[slot])
        )
    step = HEADS // 2
    for part in range(6):
        at = slice(part * step, (part + 1) * step)
        result = nn(columns[...], w_part[:, at])
        if last:
            result = before[:, at] + result
            out = (query, key, value)[part // 2]
            out[:, (part % 2) * step : (part % 2 + 1) * step] = result.astype(out.dtype)
        else:
            total[:, at] = result
    if last:
        stats[...] = row_stats(query[...] * query[...], key[...] * key[...])
        put += [
            copies.start(*pair)
            for pair in ((query, query_h), (key, key_h), (value, value_h), (out_w, out_kept))
        ]
    finish(put)


def turn(values, cosine, sine):
    return values * cosine + pltpu.roll(values, HEAD_DIM // 2, 1) * sine


def valid_keys(x, length, tok):
    shape = (NX * tok, NX * tok)
    queries = lax.broadcasted_iota(jnp.int32, shape, 0)
    keys = lax.broadcasted_iota(jnp.int32, shape, 1)

    def at(index):
        return jnp.where(index < tok, x * tok + index, (1 - x) * tok + index - tok)

    return (at(keys) <= at(queries)) & (at(keys).astype(F32) < length)


def softmax(query, key, valid):
    logits = jnp.where(valid, nt(query, key) * HEAD_DIM ** (-0.5), NEGATIVE)
    powers = jnp.exp(logits - jnp.max(logits, axis=1, keepdims=True))
    return powers / jnp.sum(powers, axis=1, keepdims=True)


def attend_kernel(pos, *refs):
    x, _, y, _ = place(pos)
    stats, *refs = refs
    lengths, gains, cosine, sine, query, key, value, out_w, *refs = refs
    query_out, key_out, attended_out, scales, *refs = refs
    pieces, refs = refs[:GROUP], refs[GROUP:]
    query_r, key_r, attended, sems = refs
    copies = Copies(sems)
    tok = query.shape[0] // GROUP
    span = NX * tok
    width = out_w.shape[1]
    scale = lax.rsqrt(stats[...] / width + EPSILON)
    scales[...] = scale
    for seq in range(NY):
        at = slice(seq * span, (seq + 1) * span)
        columns = jnp.transpose(scale[:, at])
        valid = valid_keys(x, lengths[seq : seq + 1, 0:1], tok)
        for head in range(NZ):
            lanes = slice(head * HEAD_DIM, (head + 1) * HEAD_DIM)
            gain = pl.ds(column_of(x, head, y), HEAD_DIM)
            for row, (raw, out) in enumerate(((query, query_r), (key, key_r))):
                normed = raw[at, lanes] * columns[:, 4 * row : 4 * row + 1]
                normed = normed * gains[row : row + 1, gain]
                out[at, lanes] = turn(normed, cosine[...], sine[...]).astype(BF16)
            chances = softmax(query_r[at, lanes], key_r[at, lanes], valid)
            attended[at, lanes] = nn(chances.astype(BF16), value[at, lanes]).astype(BF16)
    put = [
        copies.start(*pair)
        for pair in ((query_r, query_out), (key_r, key_out), (attended, attended_out))
    ]
    step = width // 4
    for part in range(4):
        columns = slice(part * step, (part + 1) * step)
        result = nn(attended[...], out_w[:, columns])
        for i, block in enumerate(TOKEN_BLOCKS):
            out = pieces[SQUARE.index(block)]
            out[:, columns] = result[i * tok : (i + 1) * tok].astype(out.dtype)
    finish(put)


def in_halves(values, x, out):
    half = out.shape[1] // NX
    for dx in range(NX):
        start = pl.multiple_of((x ^ dx) * half, half)
        out[:, dx * half : (dx + 1) * half] = values[:, pl.ds(start, half)].astype(out.dtype)


def sum_of(refs):
    total = refs[0][...].astype(F32)
    for ref in refs[1:]:
        total = total + ref[...].astype(F32)
    return total


def branch_kernel(pos, *refs):
    parts, refs = refs[:GROUP], refs[GROUP:]
    inputs, gains, branch_out, hidden_out, mlp_in = refs
    branch = sum_of(parts)
    branch_out[...] = branch
    scale = lax.rsqrt(jnp.mean(branch * branch, axis=1, keepdims=True) + EPSILON)
    hidden_out[...] = inputs[...].astype(F32) + branch * scale * gains[2:3, :]
    in_halves(hidden_out, pos[0], mlp_in)


def norm_back(values, gain, grad):
    scale = lax.rsqrt(jnp.mean(values * values, axis=1, keepdims=True) + EPSILON)
    normed = values * scale
    scaled = grad * gain
    mean = jnp.mean(scaled * normed, axis=1, keepdims=True)
    return scale * (scaled - normed * mean), jnp.sum(grad * normed, axis=0, keepdims=True)


def mlp_kernel(count, pos, *refs):
    parts, refs = refs[:count], refs[count:]
    hidden, gains, grad_output, output, grad_in, grad_gain, halves, mlp_out = refs
    halves[...] = sum_of(parts)
    in_halves(halves, pos[0], mlp_out)
    values = mlp_out[...]
    gain = gains[3:4, :]
    scale = lax.rsqrt(jnp.mean(values * values, axis=1, keepdims=True) + EPSILON)
    output[...] = (hidden[...] + values * scale * gain).astype(BF16)
    grad, by_gain = norm_back(values, gain, grad_output[...].astype(F32))
    halves[...] = grad
    in_halves(halves, pos[0], grad_in)
    grad_gain[...] = jnp.broadcast_to(by_gain, grad_gain.shape)


def branch_back_kernel(count, pos, *refs):
    parts, refs = refs[:count], refs[count:]
    branch, gains, grad_output, grad_hidden, grad_branch, grad_gain, halves, middle = refs
    halves[...] = sum_of(parts)
    in_halves(halves, pos[0], middle)
    total = grad_output[...].astype(F32) + middle[...]
    grad_hidden[...] = total
    grad, by_gain = norm_back(branch[...], gains[2:3, :], total)
    grad_branch[...] = grad.astype(BF16)
    grad_gain[...] = jnp.broadcast_to(by_gain, grad_gain.shape)


def attend_back_kernel(pos, *refs):
    lengths, scales, gains, cosine, sine, out_w, *refs = refs
    blocks, refs = refs[:GROUP], refs[GROUP:]
    held, refs = refs[:5], refs[5:]
    query_out, key_out, grad_value, stats, head_gains, branch_all, *refs = refs
    query_r, key_r, value, query, key, *refs = refs
    grad_query, grad_key, grad_att, sems = refs
    x, _, y, _ = place(pos)
    tok = blocks[0].shape[0]
    span = NX * tok
    copies = Copies(sems)
    later = [
        copies.start(*pair) for pair in zip(held, (query_r, key_r, value, query, key))
    ]
    for i, block in enumerate(TOKEN_BLOCKS):
        branch_all[i * tok : (i + 1) * tok] = blocks[SQUARE.index(block)][...]
    for half in range(2):
        lanes = slice(half * (HEADS // 2), (half + 1) * (HEADS // 2))
        grad_att[:, lanes] = nt(branch_all[...], out_w[lanes, :]).astype(BF16)
    head_gains[...] = jnp.zeros_like(head_gains)
    finish(later)
    for seq in range(NY):
        at = slice(seq * span, (seq + 1) * span)
        columns = jnp.transpose(scales[:, at])
        valid = valid_keys(x, lengths[seq : seq + 1, 0:1], tok)
        for head in range(NZ):
            lanes = slice(head * HEAD_DIM, (head + 1) * HEAD_DIM)
            gain = pl.ds(column_of(x, head, y), HEAD_DIM)
            queries, keys, values = query_r[at, lanes], key_r[at, lanes], value[at, lanes]
            chances = softmax(queries, keys, valid)
            incoming = grad_att[at, lanes]
            grad_chances = nt(incoming, values)
            grad_value[at, lanes] = tn(chances.astype(BF16), incoming).astype(BF16)
            balance = jnp.sum(chances * grad_chances, axis=1, keepdims=True)
            grad_logits = (chances * (grad_chances - balance)).astype(BF16)
            by_query = nn(grad_logits, keys) * HEAD_DIM ** (-0.5)
            by_key = tn(grad_logits, queries) * HEAD_DIM ** (-0.5)
            for row, (grad, raw, out) in enumerate(
                ((by_query, query, grad_query), (by_key, key, grad_key))
            ):
                back = turn(grad.astype(BF16).astype(F32), cosine[...], -sine[...])
                normed = raw[at, lanes] * columns[:, 4 * row : 4 * row + 1]
                head_gains[row : row + 1, lanes] += jnp.sum(back * normed, axis=0, keepdims=True)
                out[at, lanes] = back * gains[row : row + 1, gain]
    query_out[...] = grad_query[...]
    key_out[...] = grad_key[...]
    stats[...] = row_stats(grad_query[...] * query[...], grad_key[...] * key[...])


def project_back_kernel(*refs):
    stats, *refs = refs
    scales, grad_query, grad_key, grad_value, query, key, grads = refs
    width = NX * NY * HEADS
    means = jnp.transpose(stats[...] / width)
    columns = jnp.transpose(scales[...])
    for row, (grad, raw) in enumerate(((grad_query, query), (grad_key, key))):
        scale = columns[:, 4 * row : 4 * row + 1]
        mean = means[:, 4 * row : 4 * row + 1]
        result = scale * (grad[...] - raw[...] * (scale * scale * mean))
        grads[:, row * HEADS : (row + 1) * HEADS] = result.astype(BF16)
    grads[:, 2 * HEADS :] = grad_value[...]


def input_back_kernel(pos, grads, *refs):
    weights, refs = refs[:NZ], refs[NZ:]
    *pieces, results = refs
    x, r, y, _ = place(pos)
    tok = grads.shape[0] // GROUP
    for s, weight in enumerate(weights):
        for half in range(2):
            result = nt(grads[...], weight[half * HEADS // 2 : (half + 1) * HEADS // 2, :])
            results[:, half * HEADS // 2 : (half + 1) * HEADS // 2] = result.astype(BF16)
        for j, (dx, dy) in enumerate(SQUARE):
            start = column_of(x ^ dx, ring(r, s), y ^ dy)
            for i, block in enumerate(TOKEN_BLOCKS):
                out = pieces[SQUARE.index(block)]
                out[:, pl.ds(start, HEAD_DIM)] = results[
                    i * tok : (i + 1) * tok, j * HEAD_DIM : (j + 1) * HEAD_DIM
                ]


def weight_back_kernel(nc, places, pos, *refs):
    for i, s in enumerate(places):
        weight_back_part(nc, s, i, pos, *refs)


def weight_back_part(nc, s, slot, pos, x_all, grads, attended, branch_all, *refs):
    attn_gain, mlp_gain, head_gains, *outs, columns, sums, out_sums = refs
    x, r, y, c = place(pos)
    rows = HEAD_DIM // nc
    base = slot * (4 * GROUP * rows + EXTRA)
    z = ring(r, s)
    gains = []
    for i, (dx, dy) in enumerate(SQUARE):
        start = column_of(x ^ dx, z, y ^ dy)
        columns[:, i * HEAD_DIM : (i + 1) * HEAD_DIM] = x_all[:, pl.ds(start, HEAD_DIM)]
        if i == 0:
            heads = pl.ds(pl.multiple_of(z * HEAD_DIM, HEAD_DIM), HEAD_DIM)
            gains.append(head_gains[0:2, heads])
        else:
            gains.append(jnp.zeros((2, HEAD_DIM), F32))
        gains.append(attn_gain[0:1, pl.ds(start, HEAD_DIM)])
        gains.append(mlp_gain[0:1, pl.ds(start, HEAD_DIM)])
    gains = jnp.concatenate(gains, axis=0)
    step = grads.shape[1] // 3
    for part in range(3):
        lanes = slice(part * step, (part + 1) * step)
        sums[:, lanes] = tn(columns[...], grads[:, lanes]).astype(BF16)
    heads = pl.ds(pl.multiple_of(z * HEAD_DIM, HEAD_DIM), HEAD_DIM)
    out_sums[...] = tn(attended[:, heads], branch_all[...]).astype(BF16)
    for k, out in enumerate(outs):
        for i in range(GROUP):
            start = pl.multiple_of(i * HEAD_DIM + (c ^ k) * rows, rows)
            for j in range(3):
                at = base + (j * GROUP + i) * rows
                lanes = slice(j * HEADS, (j + 1) * HEADS)
                out[at : at + rows] = sums[pl.ds(start, rows), lanes]
            start = pl.multiple_of((c ^ k) * rows, rows)
            at = base + (3 * GROUP + i) * rows
            lanes = slice(i * HEADS, (i + 1) * HEADS)
            out[at : at + rows] = out_sums[pl.ds(start, rows), lanes]
        chosen = 0.0
        for place_c in range(nc):
            part = gains[:, place_c * rows : (place_c + 1) * rows]
            chosen = chosen + jnp.where((c ^ k) == place_c, part, 0.0)
        chosen = jnp.concatenate([chosen, jnp.zeros((EXTRA, HEAD_DIM - rows), F32)], axis=1)
        put_extra(out, base + 4 * GROUP * rows, chosen)


def collect_kernel(count, *refs):
    parts, (grad_wo, *outs) = refs[:count], refs[count:]
    rows = (parts[0].shape[0] - EXTRA) // (4 * GROUP)

    def total(at, height, lanes=slice(None)):
        result = parts[0][at : at + height, lanes].astype(F32)
        for part in parts[1:]:
            result = result + part[at : at + height, lanes].astype(F32)
        return result

    extra = total(4 * GROUP * rows, EXTRA, slice(0, HEAD_DIM))
    for i, out in enumerate(outs):
        for j in range(3):
            part = total((j * GROUP + i) * rows, rows)
            out[:rows, j * HEADS : (j + 1) * HEADS] = part.astype(BF16)
        grad_wo[:, i * HEADS : (i + 1) * HEADS] = total((3 * GROUP + i) * rows, rows)
        put_extra(out, rows, extra_rows([extra[4 * i : 4 * i + 4]]))


def spread_kernel(pos, *refs):
    parts, (*outs, gains) = refs[:GROUP], refs[GROUP:]
    x, _, y, _ = place(pos)
    rows = parts[0].shape[0] - EXTRA
    total = 0.0
    for (dx, dy), part in zip(SQUARE, parts):
        total = total + part[rows:, :HEAD_DIM].astype(F32)
        for i, out in enumerate(outs):
            for head in range(NZ):
                start = column_of(x ^ dx, head, y ^ dy)
                at = i * HEADS + head * HEAD_DIM
                out[:, pl.ds(start, HEAD_DIM)] = part[:rows, at : at + HEAD_DIM].astype(F32)
    gains[...] = total[:8]


def take(refs, *counts):
    groups = []
    for count in counts:
        groups.append(refs[:count])
        refs = refs[count:]
    return *groups, refs


def put_columns(block, kept):
    width = kept[0].shape[1]
    for i, out in enumerate(kept):
        out[...] = block[:, i * width : (i + 1) * width]


def mlp_forward_kernel(nc, block, *refs):
    count = NY * nc
    gates, ups, downs, refs = take(refs, NX * count, NX * count, 4 * count)
    refs = refs[-(2 * nc + NY + NX + 2) :]
    products, by_gate, by_up, kept, (out, total) = take(refs, NY, nc, nc, NX)
    put_columns(block, kept)
    hidden = gates[0].shape[1]
    quarter = kept[0].shape[1] // 2
    for k in range(nc):
        for dy in range(NY):
            at = dy * nc + k
            lanes = slice(dy * hidden, (dy + 1) * hidden)

            def through(weights):
                return nn(kept[0][...], weights[at][...]) + nn(
                    kept[1][...], weights[count + at][...]
                )

            gate, up = through(gates), through(ups)
            chance = 1.0 / (1.0 + jnp.exp(-gate))
            silu = gate * chance
            product = (silu * up).astype(BF16)
            products[dy][:, k * hidden : (k + 1) * hidden] = product
            by_up[k][:, lanes] = silu.astype(BF16)
            by_gate[k][:, lanes] = (up * (chance + silu * (1.0 - chance))).astype(BF16)
            for i in range(4):
                columns = slice(i * quarter, (i + 1) * quarter)
                part = nt(product, downs[i * count + at][...])
                total[:, columns] = part if k + dy == 0 else total[:, columns] + part
    out[...] = total[...]


def mlp_back_kernel(nc, block, *refs):
    count = NY * nc
    gates, ups, downs, by_gate, by_up, refs = take(
        refs, NX * count, NX * count, 4 * count, nc, nc
    )
    refs = refs[-(2 * nc + NX + 2) :]
    grad_gates, grad_ups, kept, (out, total) = take(refs, nc, nc, NX)
    put_columns(block, kept)
    hidden = gates[0].shape[1]
    quarter = kept[0].shape[1] // 2
    for k in range(nc):
        for dy in range(NY):
            at = dy * nc + k
            lanes = slice(dy * hidden, (dy + 1) * hidden)
            grad = 0.0
            for i in range(4):
                columns = slice((i % 2) * quarter, (i % 2 + 1) * quarter)
                grad = grad + nn(kept[i // 2][:, columns], downs[i * count + at][...])
            grad_gate = (grad * by_gate[k][:, lanes].astype(F32)).astype(BF16)
            grad_up = (grad * by_up[k][:, lanes].astype(F32)).astype(BF16)
            grad_gates[k][:, lanes] = grad_gate
            grad_ups[k][:, lanes] = grad_up
    for i in range(4):
        columns = slice(i * quarter, (i + 1) * quarter)
        rows = slice((i % 2) * quarter, (i % 2 + 1) * quarter)
        result = 0.0
        for k in range(nc):
            for dy in range(NY):
                lanes = slice(dy * hidden, (dy + 1) * hidden)
                weight = (i // 2) * count + dy * nc + k
                result = result + nt(grad_gates[k][:, lanes], gates[weight][rows, :])
                result = result + nt(grad_ups[k][:, lanes], ups[weight][rows, :])
        out[:, columns] = result


def down_back_kernel(*refs):
    *parts, out = refs
    count = len(parts) // 3
    near, far, products, _ = take(parts, count, count, count)
    tok = near[0].shape[0]
    step = out.shape[0] // 2
    for i in range(2):
        rows = slice(i * step, (i + 1) * step)
        for j, product in enumerate(products):
            part = tn(near[j][:, rows], product[:tok]) + tn(far[j][:, rows], product[tok:])
            out[rows, :] = part if j == 0 else out[rows, :] + part


def make_body(wide):
    nc = wide // (NY * NZ)

    def send(value, x=0, y=0, r=0, c=0):
        pairs = []
        for sx in range(NX):
            for sz in range(NZ):
                for sy in range(NY):
                    for sc in range(nc):
                        source = sx * wide + (sz * NY + sy) * nc + sc
                        target = (sx ^ x) * wide
                        target += (ring(gray(sz), r) * NY + (sy ^ y)) * nc + (sc ^ c)
                        pairs.append((source, target))
        return lax.ppermute(value, AXES, pairs)

    def square(parts):
        return [
            part if (dx, dy) == (0, 0) else send(part, x=dx, y=dy)
            for (dx, dy), part in zip(SQUARE, parts)
        ]

    def square_gather(first, second):
        first_x = send(first, x=1)
        second_y = send(second, y=1)
        first_y = send(first, y=1)
        second_x = send(second, x=1)
        first_xy = send(first_x, y=1)
        second_xy = send(second_y, x=1)
        return [first, first_y, first_x, first_xy], [second, second_y, second_x, second_xy]

    def scatter_far(first, second):
        return send(first[3], x=1), send(second[3], y=1)

    def scatter_near(first, second):
        return send(first[2], x=1), send(second[1], y=1)

    def scatter_last(first, second, far, near):
        return (
            send((first[1].astype(F32) + far[0].astype(F32)).astype(BF16), y=1),
            send((second[2].astype(F32) + far[1].astype(F32)).astype(BF16), x=1),
        )

    def scatter_sum(first, second, near, last):
        return (
            first[0].astype(F32) + near[0].astype(F32) + last[0].astype(F32),
            second[0].astype(F32) + near[1].astype(F32) + last[1].astype(F32),
        )

    def core_gather(block):
        return [block] + [send(block, c=k) for k in range(1, nc)]

    def core_sums(blocks, hidden):
        sums = []
        for row in blocks:
            total = row[0].astype(F32)
            for k in range(1, nc):
                total = total + send(row[k], c=k).astype(F32)
            total = total.astype(BF16)
            sums += [total[:, dy * hidden : (dy + 1) * hidden] for dy in range(NY)]
        return sums

    def core_parts(parts):
        return [parts[0]] + [send(parts[k], c=k) for k in range(1, nc)]

    def body(
        layer_input,
        lengths,
        w_query,
        w_key,
        w_value,
        w_output,
        query_gain,
        key_gain,
        attn_gain,
        mlp_gain,
        w_gate,
        w_up,
        w_down,
        grad_output,
    ):
        due = {}

        def mark(point, value):
            due.setdefault(point, []).append(value)

        def at(point, value):
            ready = due.pop(point, [])
            return after(value, ready) if ready else value

        x = lax.axis_index("blk")
        spot = lax.axis_index("wide")
        z, y, c = spot // (NY * nc), (spot // nc) % NY, spot % nc
        inputs, grad_out = layer_input[0], grad_output[0]
        tok, width = inputs.shape
        rows = w_query.shape[0]
        group_tok = GROUP * tok
        hidden = w_gate.shape[1]
        pos = jnp.stack([x, gray(z), y, c, lengths[0]]).astype(jnp.int32)
        wide_small = shaped((8, width), F32)
        by_head = shaped((group_tok, HEADS))
        by_head_wide = shaped((group_tok, HEADS), F32)
        by_token = shaped((8, group_tok), F32)
        tokens_shape = shaped((tok, width))
        tokens_wide = shaped((tok, width), F32)
        message = shaped((4 * GROUP * rows + EXTRA, HEADS))
        piece = shaped((rows + EXTRA, 3 * HEADS))

        def group_sum(stats, *ready):
            blocks = [stats[:, i * tok : (i + 1) * tok] for i in range(GROUP)]
            for flip, way in ((1, {"x": 1}), (2, {"y": 1})):
                total = jnp.concatenate(blocks, axis=1)
                if flip == 2 and ready:
                    total = after(total, ready)
                got = send(total, **way)
                got = [got[:, i * tok : (i + 1) * tok] for i in range(GROUP)]
                blocks = [block + got[i ^ flip] for i, block in enumerate(blocks)]
            return jnp.concatenate(blocks, axis=1)

        def dma(count):
            return pltpu.SemaphoreType.DMA((count,))

        def held(shape):
            return pltpu.VMEM(shape.shape, shape.dtype)

        gains = jnp.stack([query_gain, key_gain, attn_gain, mlp_gain])
        pieces = run(
            split_kernel,
            each([piece] * GROUP, VMEM),
            [(pos, SMEM), (gains, VMEM), (w_query, auto), (w_key, auto), (w_value, auto)],
        )
        down_rows = w_down.shape[0] // 2
        down_halves = w_down[:down_rows], w_down[down_rows:]
        far_down = send(down_halves[0], x=1), send(down_halves[1], y=1)
        mark(Due.far_down, far_down)
        received = at(Point.JOIN, square(pieces))
        own_rows, lengths_row = run(
            join_kernel,
            [(message, VMEM), (shaped((8, HEAD_DIM), F32), VMEM)],
            each((*received, w_output), VMEM),
        )
        lane = jnp.arange(HEAD_DIM)[None, :]
        row = jnp.arange(NX * tok)[:, None]
        row = jnp.where(row < tok, x * tok + row, (1 - x) * tok + row - tok).astype(F32)
        half = HEAD_DIM // 2
        frequency = jnp.exp((lane % half).astype(F32) * (-2.0 * math.log(500000.0) / HEAD_DIM))
        cosine = jnp.cos(row * frequency)
        sine = jnp.sin(row * jnp.where(lane < half, -frequency, frequency))
        mark(Due.turns, (cosine, sine))
        w_ring = [own_rows, send(own_rows, r=-1)]
        half_tok = tok // 2
        from_x = send(after(inputs, own_rows), x=1)
        from_y = send(after(inputs, own_rows), y=1)
        from_xy = send(from_x[:half_tok], y=1), send(from_y[half_tok:], x=1)
        far_gate = send(after(w_gate, from_xy), x=1)
        far_up = send(after(w_up, from_xy), y=1)
        near_gate = send(after(w_gate, far_up), y=1)
        near_up = send(after(w_up, far_gate), x=1)
        mark(Due.far, (far_gate, far_up))
        mark(Due.tokens, (from_x, from_y))
        mark(Due.tokens_xy, from_xy)
        mark(Due.near, (near_gate, near_up))
        own_gate, own_up = core_gather(w_gate), core_gather(w_up)
        own_down = core_gather(w_down)
        far_gate, far_up = core_gather(far_gate), core_gather(far_up)
        far_down = core_gather(far_down[0]), core_gather(far_down[1])
        mark(Due.own_gate_c, (own_gate, own_up))
        mark(Due.own_down_c, own_down)
        mark(Due.far_c, (far_gate, far_up))
        mark(Due.far_down_c, far_down)
        first_blocks = core_gather(own_rows)
        w_ring.append(send(at(Point.RING_2, w_ring[1]), r=-1))
        second_blocks = core_gather(w_ring[1])
        w_ring.append(send(at(Point.RING_3, w_ring[2]), r=-1))
        x_all, x_kept = run(
            gather_kernel,
            [(shaped((group_tok, width)), VMEM), (shaped((group_tok, width)), HBM)],
            each([inputs, from_x, from_y, *from_xy], VMEM),
            scratch_shapes=[pltpu.SemaphoreType.DMA],
        )
        w_shape = shaped((GROUP * HEAD_DIM, 3 * HEADS))
        by_three = shaped((group_tok, 3 * HEADS), F32)
        out_shape = shaped((HEADS, width))

        def project(places, blocks, before, outs):
            ins = [(pos, SMEM), (x_all, VMEM), *each(blocks, VMEM), *each(before, VMEM)]
            depth = len(places) * GROUP * HEAD_DIM
            return run(
                functools.partial(project_kernel, nc, places),
                [(wide_small, VMEM), (out_shape, VMEM)] + [(w_shape, HBM)] * len(places) + outs,
                ins,
                limit=16,
                input_output_aliases={len(ins) - 2: 0, len(ins) - 1: 1} if before else {},
                scratch_shapes=[
                    pltpu.VMEM((group_tok, depth), BF16),
                    pltpu.VMEM((depth, 3 * HEADS), BF16),
                    dma(len(places) + 4),
                ],
            )

        blocks = first_blocks + second_blocks + core_gather(w_ring[2])
        gains, out_w, *w_parts, total = project((0, 1, 2), blocks, (), [(by_three, VMEM)])
        mark(Due.total, total)
        last_block = core_gather(at(Point.LAST_ROWS, w_ring[3]))
        near_down = (
            send(after(down_halves[0], near_gate), y=1),
            send(after(down_halves[1], near_up), x=1),
        )
        mark(Due.near_down, near_down)
        near_gate, near_up = core_gather(near_gate), core_gather(near_up)
        mark(Due.near_c, (near_gate, near_up))
        gains, out_w, w_part, query, key, value, query_h, key_h, value_h, out_kept, stats = project(
            (3,),
            last_block,
            (total, gains, out_w),
            [(by_head_wide, VMEM), (by_head_wide, VMEM), (by_head, VMEM)]
            + [(by_head_wide, HBM), (by_head_wide, HBM), (by_head, HBM)]
            + [(out_shape, HBM), (by_token, VMEM)],
        )
        w_parts.append(w_part)
        group_stats = at(Point.SCALES, group_sum(at(Point.STATS, stats)))
        last_gate = send(after(far_gate[0], group_stats, near_gate[0]), y=1)
        last_up = send(after(far_up[0], group_stats, near_up[0]), x=1)
        mark(Due.last, (last_gate, last_up))
        last_gate, last_up = core_gather(last_gate), core_gather(last_up)
        mark(Due.last_c, (last_gate, last_up))
        gate_w = [*own_gate, *near_gate, *far_gate, *last_gate]
        up_w = [*own_up, *far_up, *near_up, *last_up]
        near_down = core_gather(near_down[0]), core_gather(near_down[1])
        mark(Due.near_down_c, near_down)

        query_r, key_r, attended, scales, *parts = run(
            attend_kernel,
            [(by_head, HBM)] * 3 + [(by_token, VMEM)] + [(tokens_shape, VMEM)] * GROUP,
            [
                (pos, SMEM),
                (group_stats, VMEM),
                *each((lengths_row, gains, cosine, sine), VMEM),
                *each((query, key, value, out_w), VMEM),
            ],
            scratch_shapes=[held(by_head), held(by_head), held(by_head), dma(3)],
        )
        parts = square(at(Point.BRANCH_SEND, parts))
        first_x, second_y = far_down
        last_down = (
            core_gather(send(after(first_x[0], parts), y=1)),
            core_gather(send(after(second_y[0], parts), x=1)),
        )
        own_first = [part[:down_rows] for part in own_down]
        own_second = [part[down_rows:] for part in own_down]
        down_first = own_first, near_down[0], first_x, last_down[0]
        down_second = own_second, second_y, near_down[1], last_down[1]
        down_w = [
            piece
            for dx in range(NX)
            for half in (down_first, down_second)
            for dy in range(NY)
            for piece in half[dx * NY + dy]
        ]
        branch, hidden_state, mlp_in = run(
            branch_kernel,
            [(tokens_wide, auto), (tokens_wide, auto), (tokens_shape, VMEM)],
            [(pos, SMEM), *each(at(Point.BRANCH, parts), auto), (inputs, auto), (gains, VMEM)],
        )

        half_width = width // NX
        quarter = half_width // 2

        def mlp_call(kernel, s, block, extra, narrow, before):
            def rows_of(array):
                count = array.shape[0] // tok
                return pl.BlockSpec((tok, array.shape[1]), lambda i: (s % count, 0))

            ins = each((block, *gate_w, *up_w, *down_w), VMEM) + each(extra, rows_of)
            columns, height = narrow
            outs = [shaped((NZ * tok, count)) for count in columns]
            outs = each(outs + [shaped((height, half_width))] * NX, rows_of)
            aliases = {}
            if before is not None:
                aliases = {len(ins) + i: i for i in range(len(before))}
                ins += each(before, HBM)
            *kept, total = run(
                functools.partial(kernel, nc),
                [*outs, (tokens_wide, VMEM)],
                ins,
                input_output_aliases=aliases,
                scratch_shapes=[held(tokens_wide)],
            )
            return kept, total

        def summed(parts):
            total = parts[0].astype(F32)
            for part in parts[1:]:
                total = total + part.astype(F32)
            return total

        def mlp_pass(points, kernel, block, extra, columns, height):
            narrow = columns, height
            near = send(block, r=-1)
            middle = send(near, r=-1)
            kept, first = mlp_call(kernel, 1, at(points, near), extra, narrow, None)
            far = send(middle, r=-1)
            sent = [first.astype(BF16)]
            moving = send(sent[0], r=-1)
            kept, own = mlp_call(kernel, 0, block, extra, narrow, kept)
            early = []
            if height < NZ * tok:
                early, kept = kept[-NX:], kept[:-NX]
                early = square([early[dx] for dx, dy in SQUARE])
                mark(Due.near_grads, early[1:3])
                mark(Due.near_grads_xy, early[3])
            middle = at(points + 1, middle)
            kept, second = mlp_call(kernel, 2, middle, extra, narrow, kept)
            far = at(points + 2, far)
            kept, third = mlp_call(kernel, 3, far, extra, narrow, kept)
            sent.append(summed([second, moving]).astype(BF16))
            sent.append(summed([third, send(sent[1], r=-1)]).astype(BF16))
            parts = [own, send(at(points + 3, sent[2]), r=-1)]
            return kept, parts, sent, early

        columns = [nc * hidden] * NY + [NY * hidden] * 2 * nc
        kept, parts, sent, _ = mlp_pass(
            Point.F1, mlp_forward_kernel, mlp_in, (), columns, NZ * tok
        )
        products, by_gate, by_up, mlp_all = take(kept, NY, nc, nc)

        late = after(products, sent[1])
        got_products = square([late[dy] for dx, dy in SQUARE])
        mark(Due.products, got_products[1:3])
        mark(Due.products_xy, got_products[3])
        output, grad_mlp, grad_gain_mlp = run(
            functools.partial(mlp_kernel, len(parts)),
            [(tokens_shape, auto), (tokens_shape, VMEM), (wide_small, VMEM)],
            [
                (pos, SMEM),
                *each(at(Point.MLP_OUT, parts), auto),
                (hidden_state, auto),
                (gains, VMEM),
                (grad_out, auto),
            ],
            scratch_shapes=[held(tokens_wide)] * 2,
        )
        extra = *by_gate, *by_up
        columns = [NY * hidden] * 2 * nc
        kept, parts, sent, near_grads = mlp_pass(
            Point.B1, mlp_back_kernel, grad_mlp, extra, columns, 2 * tok
        )
        grad_gates, grad_ups, grad_all = take(kept, nc, nc)
        grad_hidden, grad_branch, grad_gain_attn = run(
            functools.partial(branch_back_kernel, len(parts)),
            [(tokens_wide, auto), (tokens_shape, VMEM), (wide_small, VMEM)],
            [
                (pos, SMEM),
                *each(at(Point.MIDDLE, parts), auto),
                (branch, auto),
                (gains, VMEM),
                (grad_out, auto),
            ],
            scratch_shapes=[held(tokens_wide)] * 2,
        )

        def products_of(left, right):
            return [[tn(block, grad).astype(BF16) for grad in right] for block in left]

        late = after(grad_all, sent[2])
        far_grads = square([late[dx] for dx, dy in SQUARE])
        mark(Due.far_grads, far_grads[1:3])
        mark(Due.far_grads_xy, far_grads[3])
        blocks = square([at(Point.BRANCH_BACK, grad_branch)] * GROUP)
        mlp_all = after(mlp_all, blocks[1])
        wg_blocks = products_of(mlp_all, grad_gates)
        wu_blocks = products_of(mlp_all, grad_ups)
        mark(Due.dots, (wg_blocks, wu_blocks))
        blocks = at(Point.ATTEND_BACK, blocks)
        wg_blocks, wu_blocks = after((wg_blocks, wu_blocks), blocks)
        w_pair = core_sums(wg_blocks, hidden), core_sums(wu_blocks, hidden)
        mark(Due.sums, w_pair)
        grad_query, grad_key, grad_value, stats, head_gains, branch_all = run(
            attend_back_kernel,
            [
                (by_head_wide, VMEM),
                (by_head_wide, VMEM),
                (by_head, VMEM),
                (by_token, VMEM),
                (shaped((8, HEADS), F32), VMEM),
                (shaped((group_tok, width)), VMEM),
            ],
            [
                (pos, SMEM),
                *each((lengths_row, scales, gains, cosine, sine, out_kept, *blocks), VMEM),
                *each((query_r, key_r, value_h, query_h, key_h), HBM),
            ],
            limit=16,
            scratch_shapes=[
                held(by_head),
                held(by_head),
                held(by_head),
                held(by_head_wide),
                held(by_head_wide),
                held(by_head_wide),
                held(by_head_wide),
                held(by_head),
                dma(5),
            ],
        )
        (grads,) = run(
            project_back_kernel,
            [(shaped((group_tok, 3 * HEADS)), VMEM)],
            [
                (at(Point.PROJECT_BACK, group_sum(at(Point.STATS_BACK, stats))), VMEM),
                (scales, VMEM),
                *each((grad_query, grad_key, grad_value, query_h, key_h), VMEM),
            ],
        )
        w_far = scatter_far(*after(w_pair, grads))
        w_near = scatter_near(*after(w_pair, w_far))
        w_last = scatter_last(*w_pair, w_far, w_near)
        mark(Due.w_far, w_far)
        mark(Due.w_near, w_near)
        mark(Due.w_last, w_last)

        def weight_parts(places):
            height = message.shape[0]
            results = run(
                functools.partial(weight_back_kernel, nc, places),
                [(shaped((len(places) * height, HEADS)), VMEM)] * nc,
                [
                    (pos, SMEM),
                    *each((x_kept, grads, attended, branch_all), VMEM),
                    *each((grad_gain_attn, grad_gain_mlp, head_gains), VMEM),
                ],
                scratch_shapes=[
                    pltpu.VMEM((group_tok, GROUP * HEAD_DIM), BF16),
                    pltpu.VMEM((GROUP * HEAD_DIM, 3 * HEADS), BF16),
                    pltpu.VMEM((HEAD_DIM, width), BF16),
                ],
            )
            results = core_parts(results)
            return [
                [part[i * height : (i + 1) * height] for part in results]
                for i in range(len(places))
            ]

        (first,) = weight_parts((1,))
        factors = []
        for *grads_of, product in zip(near_grads, far_grads, got_products):
            for k in range(nc):
                pieces = *grads_of, product[:, k * hidden : (k + 1) * hidden]
                factors.append([send(piece, c=k) if k else piece for piece in pieces])
        mark(Due.factors, factors)
        (grad_wd,) = run(
            down_back_kernel,
            [(shaped(w_down.shape, F32), VMEM)],
            each([entry[i] for i in range(3) for entry in factors], VMEM),
        )

        mark(Due.grad_wd, grad_wd)
        w_moving = send(at(Point.SUM_1, summed(first).astype(BF16)), r=-1)
        (second,) = weight_parts((2,))
        (third,) = weight_parts((3,))
        (own,) = weight_parts((0,))
        x_parts = run(
            input_back_kernel,
            [(tokens_shape, VMEM)] * GROUP,
            [(pos, SMEM), (after(grads, second), VMEM), *each(w_parts, VMEM)],
            scratch_shapes=[pltpu.VMEM((group_tok, GROUP * HEAD_DIM), BF16)],
        )
        mark(Due.x_parts, x_parts)
        late = after(x_parts[1:3], w_last)
        from_x = [x_parts[0], send(late[0], y=1), send(late[1], x=1)]
        mark(Due.x_sums, from_x)
        sent = summed(second + [w_moving]).astype(BF16)
        w_moving = send(at(Point.SUM_2, sent), r=-1)
        sent = summed(third + [w_moving]).astype(BF16)
        w_moving = send(at(Point.SUM_3, sent), r=-1)
        grad_wg, grad_wu = scatter_sum(*w_pair, w_near, w_last)
        parts = at(Point.COLLECT, own + [w_moving])
        grad_wo, *messages = run(
            functools.partial(collect_kernel, len(parts)),
            [(shaped((rows, width), F32), auto)] + [(piece, VMEM)] * GROUP,
            each(parts, auto),
        )
        grad_wq, grad_wk, grad_wv, total_gains = run(
            spread_kernel,
            [(shaped((rows, width), F32), auto)] * 3 + [(shaped((8, HEAD_DIM), F32), VMEM)],
            [(pos, SMEM), *each(at(Point.SPREAD, square(messages)), auto)],
        )
        last_x = send(after(x_parts[3], messages), x=1, y=1)
        grad_x = summed([grad_hidden, *from_x, last_x])

        return (
            output[None],
            grad_x.astype(BF16)[None],
            grad_wq,
            grad_wk,
            grad_wv,
            grad_wo,
            total_gains[0, :rows],
            total_gains[1, :rows],
            total_gains[2, :rows],
            total_gains[3, :rows],
            grad_wg,
            grad_wu,
            grad_wd,
        )

    return body


def solution(mesh):
    return jax.shard_map(
        make_body(mesh.shape["wide"]),
        mesh=mesh,
        in_specs=(
            P("wide", "blk", None),
            P("wide"),
            P(("blk", "wide"), None),
            P(("blk", "wide"), None),
            P(("blk", "wide"), None),
            P(("blk", "wide"), None),
            P(("blk", "wide")),
            P(("blk", "wide")),
            P(("blk", "wide")),
            P(("blk", "wide")),
            P("blk", "wide"),
            P("blk", "wide"),
            P("blk", "wide"),
            P("wide", "blk", None),
        ),
        out_specs=(
            P("wide", "blk", None),
            P("wide", "blk", None),
            P(("blk", "wide"), None),
            P(("blk", "wide"), None),
            P(("blk", "wide"), None),
            P(("blk", "wide"), None),
            P(("blk", "wide")),
            P(("blk", "wide")),
            P(("blk", "wide")),
            P(("blk", "wide")),
            P("blk", "wide"),
            P("blk", "wide"),
            P("blk", "wide"),
        ),
        check_vma=False,
    )
```
